256 devices in a mesh: dp: 16 (over z, x_lo), cont: 16 (over y, x_hi, core).
Axes of the slice: x: 4 (x_hi: 2, x_lo: 2; x = x_hi * 2 + x_lo), y: 4, z: 8, core: 2. Of those that a mesh axis runs over, the one named last changes fastest.
Arguments:
- tokens: bfloat16 [32768, 8192], P(('dp', 'cont')), may hold values from -6 to 6
- frozen_step_queries: bfloat16 [32768, 8192], P(('dp', 'cont')), may hold values from -96 to 96
- step_token_keys: bfloat16 [32768, 1024], P(('dp', 'cont')), may hold values from -6 to 6
- step_token_values: bfloat16 [32768, 1024], P(('dp', 'cont')), may hold values from -6 to 6
- prefix_key_table: bfloat16 [8192, 1024], P(('dp', 'cont')), may hold values from -4 to 4
- prefix_value_table: bfloat16 [8192, 1024], P(('dp', 'cont')), may hold values from -6 to 6
- adapter_down_map: bfloat16 [16, 8192], replicated, may hold values from -0.0625 to 0.0625
- adapter_up_map: bfloat16 [16, 8192], replicated, may hold values from -1.5 to 1.5
- readout: bfloat16 [8192], replicated, may hold values from -0.0625 to 0.0625
- step_pair_lengths: int32 [256, 2], P(('dp', 'cont')), may hold values from 32 to 64, as said below
- prefix_length_table: int32 [16], P('dp'), may hold values from 32 to 512, as said below
- prefix_block_mask: int32 [512, 16], P(('dp', 'cont')), may hold values from 0 to 1, as said below
Outputs:
- loss_total: float32 [], replicated
- grad_down: float32 [16, 8192], replicated
- up_map_gradient: float32 [16, 8192], replicated
The draws below stay inside these ranges and needn't reach their ends.
Inputs may be any that keep to these rules, and one draw needn't show every extreme that they name: `step_pair_lengths`: each length is at least 32, and some step has exactly 64. `prefix_length_table`: a multiple of 32; some group's prefix fills all 512 slots. `prefix_block_mask`: the first block is always 1.
All inputs are finite; a program needn't handle non-finite values.
Results may differ from the reference program's by a relative error of at most 0.025.
Values may be sent and summed in bfloat16 or wider, within the bound.
A program may use at most 128 MiB of HBM per device.

```python
import jax
import jax.numpy as jnp
from jax import lax

MODEL_WIDTH = 8192
HQ = 64
KVH = 8
HD = 128
ADAPTER_RANK = 16
BLOCK = 32
STEP = 64
QUERY_FEATURES = 8192
KVD = 1024
PREFIX = 512
PBLK = 16
SEQS = 256
TOKENS = 32768
N_DP = 16
N_CONT = 16


def shared_prefix(key):
    drawn = jnp.clip(jax.random.normal(jax.random.fold_in(key, 101), (N_DP * PREFIX, KVD), jnp.float32), -4.0, 4.0)
    anchor_at = jax.random.randint(jax.random.fold_in(key, 102), (N_DP,), 0, BLOCK - 1, dtype=jnp.int32)
    levels = jax.random.randint(jax.random.fold_in(key, 103), (N_DP,), 0, 3, dtype=jnp.int32).at[0].set(2)
    return (drawn, anchor_at, levels)


def strength_of(levels, lowest, middle, highest):
    return jnp.where(levels == 0, lowest, jnp.where(levels == 1, middle, highest)).astype(jnp.float32)


def anchor_rows(drawn, anchor_at):
    grouped = drawn.reshape(N_DP, PREFIX, KVD)
    return (grouped, grouped[jnp.arange(N_DP), anchor_at])


def draw_prefix_key_table(key, part):
    drawn, anchor_at, levels = shared_prefix(key)
    strength = strength_of(levels, 6.0, 12.0, 18.0)
    factor = 1.0 - 2.0 / (strength * HD ** 0.5)
    grouped, anchor = anchor_rows(drawn, anchor_at)
    position = jnp.arange(PREFIX, dtype=jnp.int32)
    partner = position[None, :] == (anchor_at + 1)[:, None]
    result = jnp.where(partner[:, :, None], factor[:, None, None] * anchor[:, None, :], grouped)
    return result.reshape(N_DP * PREFIX, KVD).astype(jnp.bfloat16)


def draw_frozen_step_queries(key, part):
    drawn, anchor_at, levels = shared_prefix(key)
    key = jax.random.fold_in(key, 7)
    per_group = TOKENS // N_DP
    strength = strength_of(levels, 6.0, 12.0, 18.0)
    background = jnp.clip(jax.random.normal(jax.random.fold_in(key, 2), (TOKENS, QUERY_FEATURES), jnp.float32), -6.0, 6.0)
    grouped, anchor = anchor_rows(drawn, anchor_at)
    spread = jnp.broadcast_to(anchor.reshape(N_DP, KVH, 1, HD), (N_DP, KVH, HQ // KVH, HD)).reshape(N_DP, 1, QUERY_FEATURES)
    aligned = jax.random.randint(jax.random.fold_in(key, 3), (N_DP, per_group, 1), 0, 8, dtype=jnp.int32) == 0
    result = jnp.where(aligned, strength[:, None, None] * spread, background.reshape(N_DP, per_group, QUERY_FEATURES))
    return result.reshape(TOKENS, QUERY_FEATURES).astype(jnp.bfloat16)


def draw_step_pair_lengths(key, part):
    key = jax.random.fold_in(key, 11)
    values = jax.random.randint(key, (SEQS, 2), STEP // 2, STEP + 1, dtype=jnp.int32)
    return values.at[0, 0].set(STEP)


def draw_prefix_length_table(key, part):
    key = jax.random.fold_in(key, 23)
    blocks = jax.random.randint(key, (N_DP,), 1, PBLK + 1, dtype=jnp.int32)
    return (blocks * BLOCK).at[0].set(PREFIX)


def draw_prefix_block_mask(key, part):
    key = jax.random.fold_in(key, 37)
    values = jax.random.randint(key, (2 * SEQS, PBLK), 0, 2, dtype=jnp.int32)
    return values.at[:, 0].set(1)


def shard_levels(key, shape, cuts, smallest, largest):
    level = 1.0
    for dim, shards_of in cuts:
        heights = jax.random.uniform(jax.random.fold_in(jax.random.fold_in(key, 6), dim), (shards_of,), jnp.float32, smallest / len(cuts), largest / len(cuts))
        level = level * jnp.repeat(jnp.exp(heights), shape[dim] // shards_of).reshape((-1,) + (1,) * (len(shape) - 1 - dim))
    return level


def noise(key, dims, scale, limit, cuts=(), held_as=jnp.bfloat16):
    array = jax.random.normal(key, dims, jnp.float32) * scale
    if len(cuts) > 0:
        array = shard_levels(key, dims, cuts, -0.22, 0.18) * array
    return jnp.clip(array, min=-limit, max=limit).astype(held_as)


def setup_inputs(seed: int = 0) -> dict:
    splits = jax.random.split(jax.random.key(seed), 13)
    tokens = noise(splits[0], (TOKENS, MODEL_WIDTH), 1.0, 6.0, ((0, 256),))
    frozen_step_queries = draw_frozen_step_queries(jax.random.fold_in(splits[12], 71), 0)
    step_token_keys = noise(splits[2], (TOKENS, KVD), 1.0, 6.0, ((0, 256),))
    step_token_values = noise(splits[3], (TOKENS, KVD), 1.0, 6.0, ((0, 256),))
    prefix_key_table = draw_prefix_key_table(jax.random.fold_in(splits[12], 71), 0)
    prefix_value_table = noise(splits[5], (N_DP * PREFIX, KVD), 1.0, 6.0, ((0, 256),))
    adapter_down_map = noise(splits[6], (ADAPTER_RANK, MODEL_WIDTH), MODEL_WIDTH ** -0.5, 0.0625)
    adapter_up_map = noise(splits[7], (ADAPTER_RANK, QUERY_FEATURES), ADAPTER_RANK ** -0.5, 1.5)
    readout = noise(splits[8], (QUERY_FEATURES,), QUERY_FEATURES ** -0.5, 0.0625)
    step_pair_lengths = draw_step_pair_lengths(jax.random.fold_in(splits[12], 71), 0)
    prefix_length_table = draw_prefix_length_table(jax.random.fold_in(splits[12], 71), 0)
    prefix_block_mask = draw_prefix_block_mask(jax.random.fold_in(splits[12], 71), 0)
    return dict(tokens=tokens, frozen_step_queries=frozen_step_queries, step_token_keys=step_token_keys, step_token_values=step_token_values, prefix_key_table=prefix_key_table, prefix_value_table=prefix_value_table, adapter_down_map=adapter_down_map, adapter_up_map=adapter_up_map, readout=readout, step_pair_lengths=step_pair_lengths, prefix_length_table=prefix_length_table, prefix_block_mask=prefix_block_mask)


NEG = -1e30
BETA = 0.1
ADAPTER_SCALE = 2.0
LOSS_SCALE = 1024.0


def attend(query, keys, values, visible):
    score = jnp.einsum('tghd,kgd->tghk', query.astype(jnp.float32), keys.astype(jnp.float32)) * (HD ** -0.5)
    seen = visible[:, None, None, :]
    score = jnp.where(seen, score, NEG)
    peak = jnp.max(score, axis=-1)
    weights = jnp.where(seen, jnp.exp(score - peak[..., None]), 0.0)
    total = jnp.sum(weights, axis=-1)
    rounded = lax.optimization_barrier(weights.astype(jnp.bfloat16)).astype(jnp.float32)
    out = jnp.einsum('tghk,kgd->tghd', rounded, values.astype(jnp.float32)) / total[..., None]
    return weights / total[..., None], out


def per_device_terms(tokens, frozen_step_queries, step_token_keys, step_token_values, group_prefix_keys, group_prefix_values, length_table, row_mask_table, prefix_length_value, adapter_down_map, adapter_up_map, readout):
    rows_all = tokens.shape[0]
    half = rows_all // 2
    groups = HQ // KVH
    down_projection = jnp.dot(tokens, adapter_down_map.T, preferred_element_type=jnp.float32).astype(jnp.bfloat16)
    adapted_queries = (frozen_step_queries.astype(jnp.float32) + ADAPTER_SCALE * jnp.dot(down_projection, adapter_up_map, preferred_element_type=jnp.float32)).astype(jnp.bfloat16)
    keys = jnp.concatenate([group_prefix_keys, step_token_keys], 0).reshape(-1, KVH, HD)
    values = jnp.concatenate([group_prefix_values, step_token_values], 0).reshape(-1, KVH, HD)
    position = jnp.arange(PREFIX, dtype=jnp.int32)
    key_seen = (jnp.repeat(row_mask_table, BLOCK, axis=1) > 0) & (position < prefix_length_value)[None, :]
    rows = jnp.arange(rows_all, dtype=jnp.int32)
    seq = rows // half
    seen_prefix = key_seen[seq]
    seen_step = (seq[:, None] == seq[None, :]) & (rows[None, :] <= rows[:, None])
    visible = jnp.concatenate([seen_prefix, seen_step], 1)
    q_pol = adapted_queries.reshape(rows_all, KVH, groups, HD)
    q_ref = frozen_step_queries.reshape(rows_all, KVH, groups, HD)
    prob, out_policy = attend(q_pol, keys, values, visible)
    unused, out_reference = attend(q_ref, keys, values, visible)
    diff = (out_policy - out_reference).reshape(rows_all, QUERY_FEATURES)
    read = readout.astype(jnp.float32)
    token_score = jnp.sum(diff * read[None, :], axis=1)
    valid = (rows - seq * half) < length_table[seq]
    margin = jnp.sum(jnp.where(valid, token_score, 0.0).reshape(2, half), axis=1)
    zvalue = BETA * (margin[0] - margin[1])
    loss = jax.nn.softplus(-zvalue)
    weight = BETA * jax.nn.sigmoid(-zvalue) * LOSS_SCALE
    d_margin = jnp.stack([-weight, weight])
    d_out = (jnp.where(valid, d_margin[seq], 0.0)[:, None] * read[None, :]).astype(jnp.bfloat16)
    d_heads = d_out.reshape(rows_all, KVH, groups, HD).astype(jnp.float32)
    row_dot = jnp.sum(d_heads * out_policy, axis=-1)
    d_weight = jnp.einsum('tghd,kgd->tghk', d_heads, values.astype(jnp.float32))
    d_score = (prob * (d_weight - row_dot[..., None])).astype(jnp.bfloat16)
    d_score = lax.optimization_barrier(d_score).astype(jnp.float32)
    query_gradient = (jnp.einsum('tghk,kgd->tghd', d_score, keys.astype(jnp.float32)) * (HD ** -0.5)).astype(jnp.bfloat16).reshape(rows_all, QUERY_FEATURES)
    up_map_gradient = ADAPTER_SCALE * jnp.dot(down_projection.T, query_gradient, preferred_element_type=jnp.float32)
    down_gradient = (ADAPTER_SCALE * jnp.dot(query_gradient, adapter_up_map.T, preferred_element_type=jnp.float32)).astype(jnp.bfloat16)
    grad_down = jnp.dot(down_gradient.T, tokens, preferred_element_type=jnp.float32)
    return loss, grad_down, up_map_gradient


def reference(tokens, frozen_step_queries, step_token_keys, step_token_values, prefix_key_table, prefix_value_table, adapter_down_map, adapter_up_map, readout, step_pair_lengths, prefix_length_table, prefix_block_mask):
    span = 2 * STEP

    def one_pair(index, carry):
        group = (index // N_CONT).astype(jnp.int32)
        first = (index * span).astype(jnp.int32)
        pre_first = (group * PREFIX).astype(jnp.int32)
        terms = per_device_terms(
            lax.dynamic_slice_in_dim(tokens, first, span, 0),
            lax.dynamic_slice_in_dim(frozen_step_queries, first, span, 0),
            lax.dynamic_slice_in_dim(step_token_keys, first, span, 0),
            lax.dynamic_slice_in_dim(step_token_values, first, span, 0),
            lax.dynamic_slice_in_dim(prefix_key_table, pre_first, PREFIX, 0),
            lax.dynamic_slice_in_dim(prefix_value_table, pre_first, PREFIX, 0),
            lax.dynamic_slice_in_dim(step_pair_lengths, index.astype(jnp.int32), 1, 0)[0],
            lax.dynamic_slice_in_dim(prefix_block_mask, (2 * index).astype(jnp.int32), 2, 0),
            lax.dynamic_slice_in_dim(prefix_length_table, group, 1, 0)[0],
            adapter_down_map, adapter_up_map, readout)
        return (carry[0] + terms[0], carry[1] + terms[1], carry[2] + terms[2])

    start = (jnp.zeros((), jnp.float32), jnp.zeros((ADAPTER_RANK, MODEL_WIDTH), jnp.float32), jnp.zeros((ADAPTER_RANK, QUERY_FEATURES), jnp.float32))
    loss_total, grad_down, up_map_gradient = lax.fori_loop(0, SEQS, one_pair, start)
    return (loss_total, grad_down, up_map_gradient)
```

```python
import functools

import jax
import jax.numpy as jnp
from jax import lax
from jax.experimental import pallas as pl
from jax.experimental.pallas import tpu as pltpu
from jax.sharding import PartitionSpec as P

HQ = 64
KVH = 8
HD = 128
HPG = HQ // KVH
BLOCK = 32
STEP = 64
RANK = 16
FEATURES = 8192
GCOL = HPG * HD
LANES = HPG * STEP

NEG = -1e30
BETA = 0.1
ADAPTER_SCALE = 2.0
LOSS_SCALE = 1024.0
FACTOR = HD**-0.5
LOG2E = 1.4426950408889634

MESH = pl.DeviceIdType.MESH
f32 = jnp.float32
bf16 = jnp.bfloat16


def nn(a, b):
    return lax.dot_general(a, b, (((1,), (0,)), ((), ())), preferred_element_type=f32)


def nt(a, b):
    return lax.dot_general(a, b, (((1,), (1,)), ((), ())), preferred_element_type=f32)


def iota(shape, dim):
    return lax.broadcasted_iota(jnp.int32, shape, dim)


def kernel(
    dims,
    tokens_hbm, fq_hbm, sk_hbm, sv_hbm, kshard, vshard, dmap_hbm, up_hbm, rd, lens, plen, mask,
    grads, loss_out,
    tokens, fq, sk, sv, dmap, up, kv, shard, ubuf, zbuf, rs, zs, bias, dblk, lossbuf,
    local_sem, gsend, grecv, fsend, frecv, psend, precv, zsend, zrecv, asend, arecv,
    lsend, lrecv,
):
    n_cont, n_z, nch = dims
    n_plane = 2 * n_cont
    n_chip = n_cont // 2
    prefix = BLOCK * n_cont
    width = FEATURES // n_plane
    per = KVH // nch
    dp = lax.axis_index("dp")
    cont = lax.axis_index("cont")
    core = lax.rem(cont, 2)
    chip = cont // 2
    zi = dp // 2
    xlo = lax.rem(dp, 2)
    me = xlo * n_cont + cont

    def plane_dev(p):
        return {"dp": zi * 2 + p // n_cont, "cont": lax.rem(p, n_cont)}

    def z_dev(z):
        return {"dp": z * 2 + xlo, "cont": cont}

    loads = []
    for i, (src, dst) in enumerate(
        ((dmap_hbm, dmap), (tokens_hbm, tokens), (sk_hbm, sk), (sv_hbm, sv), (fq_hbm, fq), (up_hbm, up))
    ):
        cp = pltpu.make_async_copy(src, dst, local_sem.at[i])
        cp.start()
        loads.append(cp)
    ld_dmap, ld_tokens, ld_sk, ld_sv, ld_fq, ld_up = loads

    barrier = pltpu.get_barrier_semaphore()

    def greet_plane(k, carry):
        pl.semaphore_signal(
            barrier, inc=1, device_id=plane_dev(lax.rem(me + k, n_plane)), device_id_type=MESH
        )
        return carry

    def greet_z(k, carry):
        pl.semaphore_signal(barrier, inc=1, device_id=z_dev(lax.rem(zi + k, n_z)), device_id_type=MESH)
        return carry

    lax.fori_loop(1, n_plane, greet_plane, 0)
    lax.fori_loop(1, n_z, greet_z, 0)

    rdf = rd[...].astype(f32)
    r2 = jnp.concatenate(
        [rdf[(i // 2) * HPG : (i // 2 + 1) * HPG] for i in range(2 * KVH)], axis=0
    )
    r2 = r2.astype(bf16)
    row_g = iota((HD, HD), 0) // 16

    def rv_of(values):
        total = None
        for g in range(KVH):
            w = jnp.where(row_g == g, r2, jnp.zeros_like(r2))
            part = nt(values[:, g * HD : (g + 1) * HD], w)
            total = part if total is None else total + part
        high = total.astype(bf16).astype(f32)
        low = total - high
        part_of = lax.rem(iota(total.shape, 1) // HPG, 2)
        return jnp.where(part_of == 0, high, low).astype(bf16)

    shard[:, 0:HD] = rv_of(vshard[...])
    shard[:, HD:] = kshard[...]
    kv[core, chip] = shard[...]

    pl.semaphore_wait(barrier, n_plane - 1 + n_z - 1)

    bounds = [0] + [HD * (1 + per * (n + 1)) for n in range(nch)]

    def gather_copy(n, k, slot):
        cols = pl.ds(bounds[n], bounds[n + 1] - bounds[n])
        other = lax.rem(chip + k, n_chip)
        return pltpu.make_async_remote_copy(
            src_ref=shard.at[:, cols],
            dst_ref=kv.at[core, slot, :, cols],
            send_sem=gsend.at[n, k],
            recv_sem=grecv.at[n, slot],
            device_id={"cont": other * 2 + core},
            device_id_type=MESH,
        )

    for n in range(nch):

        def start_gather(k, carry, n=n):
            gather_copy(n, k, chip).start()
            return carry

        lax.fori_loop(1, n_chip, start_gather, 0)

    def forward_copy(n):
        cols = pl.ds(bounds[n], bounds[n + 1] - bounds[n])
        return pltpu.make_async_remote_copy(
            src_ref=kv.at[core, :, :, cols],
            dst_ref=kv.at[core, :, :, cols],
            send_sem=fsend.at[n],
            recv_sem=frecv.at[n],
            device_id={"cont": chip * 2 + (1 - core)},
            device_id_type=MESH,
        )

    def forward_wait(n):
        cols = pl.ds(bounds[n], bounds[n + 1] - bounds[n])
        return pltpu.make_async_remote_copy(
            src_ref=kv.at[core, :, :, cols],
            dst_ref=kv.at[1 - core, :, :, cols],
            send_sem=fsend.at[n],
            recv_sem=frecv.at[n],
            device_id={"cont": chip * 2 + (1 - core)},
            device_id_type=MESH,
        )

    def arrive(n):
        def one(k, carry):
            gather_copy(n, k, lax.rem(chip + n_chip - k, n_chip)).wait_recv()
            return carry

        lax.fori_loop(1, n_chip, one, 0)
        forward_copy(n).start()

    ld_dmap.wait()
    ld_tokens.wait()
    down_f = nt(tokens[...], dmap[...])
    down = down_f.astype(bf16)
    len0 = lens[0, 0]
    len1 = lens[0, 1]
    lane128 = iota((RANK, HD), 1)
    t128 = lax.rem(lane128, STEP)
    down_t = nt(dmap[...], tokens[...]).astype(bf16).astype(f32)
    swapped = pltpu.roll(down_t, STEP, 1)
    first_half = lane128 < STEP
    blk_mask = (iota((HD, LANES), 0) // RANK) == (iota((HD, LANES), 1) // STEP)
    for c in range(2):
        both = jnp.where(first_half, down_t, swapped) if c == 0 else jnp.where(first_half, swapped, down_t)
        signed = jnp.where(t128 < (len0 if c == 0 else len1), -both if c == 0 else both, 0.0)
        tiled = jnp.concatenate([jnp.concatenate([signed] * 4, axis=1)] * KVH, axis=0)
        dblk[c] = jnp.where(blk_mask, tiled, 0.0).astype(bf16)

    limit = plen[0]
    for c in range(2):
        for b in range(n_cont):
            block = 2 * (b % n_chip) + b // n_chip
            ok = (mask[c, block] > 0) & (block * BLOCK < limit)
            bias[c, pl.ds(b * BLOCK, BLOCK), :] = jnp.full((BLOCK, HD), jnp.where(ok, 0.0, NEG), f32)
    causal = jnp.where(
        iota((STEP, LANES), 0) > lax.rem(iota((STEP, LANES), 1), STEP), NEG, 0.0
    ).astype(f32)

    ld_sk.wait()
    ld_sv.wait()
    rvs = rv_of(sv[...])
    rvs_t = [rvs[c * STEP : (c + 1) * STEP].astype(f32).T.astype(bf16) for c in range(2)]

    ld_fq.wait()
    ld_up.wait()

    ones_p = jnp.ones((RANK, prefix), bf16)
    ones_s = jnp.ones((RANK, STEP), bf16)
    pick = lax.rem(iota((RANK, LANES), 0), HPG) == (iota((RANK, LANES), 1) // STEP)

    def group_step(g, carry):
        acc0, acc1, dd0, dd1 = carry
        col = pl.multiple_of(g * GCOL, GCOL)
        kcol = pl.multiple_of(g * HD, HD)
        fq_g = fq[:, pl.ds(col, GCOL)]
        up_g = up[:, pl.ds(col, GCOL)]
        qp_g = (fq_g.astype(f32) + ADAPTER_SCALE * nn(down, up_g)).astype(bf16)
        up_blk = jnp.concatenate([up_g[:, h * HD : (h + 1) * HD] for h in range(HPG)], axis=0)
        kp_g = kv[:, :, :, pl.ds(kcol + HD, HD)]
        kp_g = kp_g.reshape(prefix, HD)
        kp_t = kp_g.T
        rvp = kv[:, :, :, 0:HD].reshape(prefix, HD)
        rowi = iota((HD, LANES), 0)
        expand = ((rowi // 16 == g) & (lax.rem(rowi, HPG) == iota((HD, LANES), 1) // STEP)).astype(
            f32
        ).astype(bf16)
        rvx_p = nn(rvp, expand)
        pick16 = (iota((16, HD), 0) + g * 16 == iota((16, HD), 1)).astype(f32).astype(bf16)
        rvp_t = nt(pick16, rvp).astype(bf16)
        left_p = jnp.concatenate([rvp_t, ones_p], axis=0)
        accs = [acc0, acc1]
        dds = [dd0, dd1]
        u_total = None
        for c in range(2):
            rows = slice(c * STEP, (c + 1) * STEP)
            ks_c = sk[rows, pl.ds(kcol, HD)]
            left_s = jnp.concatenate([nt(pick16, rvs[rows]).astype(bf16), ones_s], axis=0)
            rvx_s = nn(rvs[rows], expand)
            bias_c = jnp.concatenate([bias[c]] * (LANES // HD), axis=1)
            outs = []
            for q_g in (qp_g, fq_g):
                q = jnp.concatenate([q_g[rows, h * HD : (h + 1) * HD] for h in range(HPG)], axis=0)
                s_p = nt(kp_g, q) + bias_c
                s_s = nt(ks_c, q) + causal
                peak = jnp.maximum(
                    jnp.max(s_p, axis=0, keepdims=True), jnp.max(s_s, axis=0, keepdims=True)
                )
                e_p = jnp.exp2((s_p - peak) * (FACTOR * LOG2E)).astype(bf16)
                e_s = jnp.exp2((s_s - peak) * (FACTOR * LOG2E)).astype(bf16)
                st = nn(left_p, e_p) + nn(left_s, e_s)
                total = st[16:17]
                o = jnp.sum(jnp.where(pick, st[0:16], 0.0), axis=0, keepdims=True) / total
                outs.append((e_p, e_s, total, o))
            (e_p, e_s, total, o), o_ref = outs[0], outs[1][3]
            accs[c] = accs[c] + (o - o_ref)
            ds_p = (e_p.astype(f32) * (rvx_p - o)).astype(bf16)
            ds_s = (e_s.astype(f32) * (rvx_s - o)).astype(bf16)
            dq = nn(kp_t, ds_p) + nn(ks_c.T, ds_s)
            dq = (dq * (FACTOR / total)).astype(bf16)
            u = nt(dblk[c], dq)
            u_total = u if u_total is None else u_total + u
            t = jnp.where(blk_mask, nn(up_blk, dq), 0.0)
            folded = t[0:RANK]
            for h in range(1, HPG):
                folded = folded + t[h * RANK : (h + 1) * RANK]
            dds[c] = dds[c] + folded
        for h in range(HPG):
            ubuf[:, pl.ds(col + h * HD, HD)] = u_total[h * RANK : (h + 1) * RANK]
        return accs[0], accs[1], dds[0], dds[1]

    zero_acc = jnp.zeros((1, LANES), f32)
    zero_dd = jnp.zeros((RANK, LANES), f32)
    carry = (zero_acc, zero_acc, zero_dd, zero_dd)
    arrive(0)
    for n in range(nch):
        if n + 1 < nch:
            arrive(n + 1)
        forward_wait(n).wait_recv()
        carry = lax.fori_loop(n * per, (n + 1) * per, group_step, carry)
    acc0, acc1, dd0, dd1 = carry

    tl = lax.rem(iota((1, LANES), 1), STEP)
    m0 = jnp.sum(jnp.where(tl < len0, acc0, 0.0), axis=1, keepdims=True)
    m1 = jnp.sum(jnp.where(tl < len1, acc1, 0.0), axis=1, keepdims=True)
    zv = BETA * (m0 - m1)
    small = jnp.exp(-jnp.abs(zv))
    loss = jnp.maximum(-zv, 0.0) + jnp.log1p(small)
    weight = (BETA * LOSS_SCALE) * jnp.where(zv >= 0.0, small, 1.0) / (1.0 + small)

    def fold(dd):
        x = dd[:, 0:HD]
        for i in range(1, LANES // HD):
            x = x + dd[:, i * HD : (i + 1) * HD]
        return x + pltpu.roll(x, STEP, 1)

    f0 = fold(dd0)
    f1 = fold(dd1)
    dd = jnp.where(
        first_half,
        jnp.where(t128 < len0, -f0, 0.0),
        jnp.where(t128 < len1, f1, 0.0),
    )
    dd = (ADAPTER_SCALE * dd).astype(bf16)

    def finish(i, carry):
        cols = pl.ds(pl.multiple_of(i * GCOL, GCOL), GCOL)
        zbuf[0:RANK, cols] = (nn(dd, tokens[:, cols]) * weight).astype(bf16)
        zbuf[RANK:, cols] = (ubuf[:, cols] * (ADAPTER_SCALE * weight)).astype(bf16)
        return carry

    lax.fori_loop(0, KVH, finish, 0)

    def plane_copy(k, slot):
        p = lax.rem(me + k, n_plane)
        return pltpu.make_async_remote_copy(
            src_ref=zbuf.at[:, pl.ds(pl.multiple_of(p * width, 128), width)],
            dst_ref=rs.at[slot],
            send_sem=psend.at[k],
            recv_sem=precv.at[slot],
            device_id=plane_dev(p),
            device_id_type=MESH,
        )

    def start_plane(k, carry):
        plane_copy(k, me).start()
        return carry

    lax.fori_loop(1, n_plane, start_plane, 0)

    n_sub = n_cont // 4
    n_rest = 2 * n_sub
    sub = lax.rem(cont, 4)
    rest = xlo * n_sub + cont // 4

    def loss_copy(stage, k, size):
        if stage == 0:
            mine = sub
            to = {"cont": (cont // 4) * 4 + lax.rem(sub + k, 4)}
        elif stage == 1:
            mine = zi
            to = z_dev(lax.rem(zi + k, n_z))
        else:
            mine = rest
            r = lax.rem(rest + k, n_rest)
            to = {"dp": zi * 2 + r // n_sub, "cont": lax.rem(r, n_sub) * 4 + sub}
        return mine, lambda slot: pltpu.make_async_remote_copy(
            src_ref=lossbuf.at[stage, mine],
            dst_ref=lossbuf.at[stage, slot],
            send_sem=lsend.at[stage, k],
            recv_sem=lrecv.at[stage, slot],
            device_id=to,
            device_id_type=MESH,
        )

    def loss_start(stage, size, value):
        mine = (sub, zi, rest)[stage]
        lossbuf[stage, mine] = value
        for k in range(1, size):
            loss_copy(stage, k, size)[1](mine).start()

    def loss_end(stage, size):
        for k in range(1, size):
            mine, make = loss_copy(stage, k, size)
            cp = make(lax.rem(mine + size - k, size))
            cp.wait_recv()
        out = lossbuf[stage, 0]
        for k in range(1, size):
            out = out + lossbuf[stage, k]
        return out

    loss_start(0, 4, jnp.broadcast_to(loss, (1, 128)))

    my_cols = pl.ds(pl.multiple_of(me * width, 128), width)
    rs[me] = zbuf[:, my_cols]

    def plane_sum(k, acc):
        slot = lax.rem(me + n_plane - k, n_plane)
        plane_copy(k, slot).wait_recv()
        return acc + rs[slot].astype(f32)

    acc = lax.fori_loop(1, n_plane, plane_sum, rs[me].astype(f32))

    zs[zi] = acc.astype(bf16)

    def z_copy(k, slot):
        return pltpu.make_async_remote_copy(
            src_ref=zs.at[zi],
            dst_ref=zs.at[slot],
            send_sem=zsend.at[k],
            recv_sem=zrecv.at[slot],
            device_id=z_dev(lax.rem(zi + k, n_z)),
            device_id_type=MESH,
        )

    for k in range(1, n_z):
        z_copy(k, zi).start()
    loss_start(1, n_z, loss_end(0, 4))
    for k in range(1, n_z):
        z_copy(k, lax.rem(zi + n_z - k, n_z)).wait_recv()
    acc = zs[0].astype(f32)
    for z in range(1, n_z):
        acc = acc + zs[z].astype(f32)
    grads[:, my_cols] = acc.astype(bf16)

    def all_copy(k, p):
        cols = pl.ds(pl.multiple_of(p * width, 128), width)
        return pltpu.make_async_remote_copy(
            src_ref=grads.at[:, cols],
            dst_ref=grads.at[:, cols],
            send_sem=asend.at[k],
            recv_sem=arecv.at[p],
            device_id=plane_dev(lax.rem(me + k, n_plane)),
            device_id_type=MESH,
        )

    def start_all(k, carry):
        all_copy(k, me).start()
        return carry

    lax.fori_loop(1, n_plane, start_all, 0)
    loss_start(2, n_rest, loss_end(1, n_z))

    def drain_gather(k, carry):
        for n in range(nch):
            gather_copy(n, k, chip).wait_send()
        return carry

    lax.fori_loop(1, n_chip, drain_gather, 0)
    for n in range(nch):
        forward_copy(n).wait_send()

    def drain_plane(k, carry):
        plane_copy(k, me).wait_send()
        return carry

    lax.fori_loop(1, n_plane, drain_plane, 0)
    for k in range(1, n_z):
        z_copy(k, zi).wait_send()

    loss_out[...] = loss_end(2, n_rest)

    def end_all(k, carry):
        all_copy(k, lax.rem(me + n_plane - k, n_plane)).wait_recv()
        return carry

    lax.fori_loop(1, n_plane, end_all, 0)

    def drain_all(k, carry):
        all_copy(k, me).wait_send()
        return carry

    lax.fori_loop(1, n_plane, drain_all, 0)
    for stage, size in ((0, 4), (1, n_z), (2, n_rest)):
        for k in range(1, size):
            mine, make = loss_copy(stage, k, size)
            make(mine).wait_send()


def local(n_cont, n_z, tokens, fq, sk, sv, kshard, vshard, dmap, up, readout, lens, plen, mask):
    nch = 4
    n_plane = 2 * n_cont
    n_chip = n_cont // 2
    width = FEATURES // n_plane
    rows = tokens.shape[0]
    prefix = BLOCK * n_cont
    n_rest = n_cont // 2
    cols = HD + KVH * HD
    anyspec = pl.BlockSpec(memory_space=pl.ANY)
    vspec = pl.BlockSpec(memory_space=pltpu.VMEM)
    sspec = pl.BlockSpec(memory_space=pltpu.SMEM)
    dma = pltpu.SemaphoreType.DMA
    grads, loss = pl.pallas_call(
        functools.partial(kernel, (n_cont, n_z, nch)),
        out_shape=(
            jax.ShapeDtypeStruct((2 * RANK, FEATURES), bf16),
            jax.ShapeDtypeStruct((1, 128), f32),
        ),
        in_specs=[anyspec] * 4 + [vspec] * 2 + [anyspec] * 2 + [vspec] + [sspec] * 3,
        out_specs=(vspec, vspec),
        scratch_shapes=[
            pltpu.VMEM((rows, FEATURES), bf16),
            pltpu.VMEM((rows, FEATURES), bf16),
            pltpu.VMEM((rows, KVH * HD), bf16),
            pltpu.VMEM((rows, KVH * HD), bf16),
            pltpu.VMEM((RANK, FEATURES), bf16),
            pltpu.VMEM((RANK, FEATURES), bf16),
            pltpu.VMEM((2, n_chip, BLOCK, cols), bf16),
            pltpu.VMEM((BLOCK, cols), bf16),
            pltpu.VMEM((RANK, FEATURES), f32),
            pltpu.VMEM((2 * RANK, FEATURES), bf16),
            pltpu.VMEM((n_plane, 2 * RANK, width), bf16),
            pltpu.VMEM((n_z, 2 * RANK, width), bf16),
            pltpu.VMEM((2, prefix, HD), f32),
            pltpu.VMEM((2, HD, LANES), bf16),
            pltpu.VMEM((3, max(4, n_z, n_rest), 1, 128), f32),
            dma((6,)),
            dma((nch, n_chip)),
            dma((nch, n_chip)),
            dma((nch,)),
            dma((nch,)),
            dma((n_plane,)),
            dma((n_plane,)),
            dma((n_z,)),
            dma((n_z,)),
            dma((n_plane,)),
            dma((n_plane,)),
            dma((3, max(4, n_z, n_rest))),
            dma((3, max(4, n_z, n_rest))),
        ],
        compiler_params=pltpu.CompilerParams(
            collective_id=0, has_side_effects=True, vmem_limit_bytes=60 * 1024 * 1024
        ),
    )(tokens, fq, sk, sv, kshard, vshard, dmap, up, readout.reshape(HQ, HD), lens, plen, mask)
    return loss[0, 0], grads[0:RANK].astype(f32), grads[RANK:].astype(f32)


def solution(mesh):
    return jax.shard_map(
        functools.partial(local, mesh.shape["cont"], mesh.shape["dp"] // 2),
        mesh=mesh,
        in_specs=(
            P(("dp", "cont"), None),
            P(("dp", "cont"), None),
            P(("dp", "cont"), None),
            P(("dp", "cont"), None),
            P(("dp", "cont"), None),
            P(("dp", "cont"), None),
            P(),
            P(),
            P(),
            P(("dp", "cont"), None),
            P("dp"),
            P(("dp", "cont"), None),
        ),
        out_specs=(P(), P(), P()),
        check_vma=False,
    )
```

```python
import functools

import jax
import jax.numpy as jnp
from jax import lax
from jax.experimental import pallas as pl
from jax.experimental.pallas import tpu as pltpu
from jax.sharding import PartitionSpec as P

HQ = 64
KVH = 8
HD = 128
HPG = HQ // KVH
BLOCK = 32
STEP = 64
RANK = 16
FEATURES = 8192
GCOL = HPG * HD
LANES = HPG * STEP
HALF = LANES // 2

NEG = -1e30
BETA = 0.1
ADAPTER_SCALE = 2.0
LOSS_SCALE = 1024.0
FACTOR = HD**-0.5
LOG2E = 1.4426950408889634

MESH = pl.DeviceIdType.MESH
f32 = jnp.float32
bf16 = jnp.bfloat16


def nn(a, b):
    return lax.dot_general(a, b, (((1,), (0,)), ((), ())), preferred_element_type=f32)


def nt(a, b):
    return lax.dot_general(a, b, (((1,), (1,)), ((), ())), preferred_element_type=f32)


def iota(shape, dim):
    return lax.broadcasted_iota(jnp.int32, shape, dim)


def kernel(
    dims,
    tokens_hbm, fq_hbm, sk_hbm, sv_hbm, ks_hbm, vs_hbm, dmap_hbm, up_hbm, rd_hbm,
    lens_hbm, plen_hbm, mask_hbm,
    grads, loss_out,
    tokens, fq, sk, sv, dmap, up, vshard, rd, lens, plen, mask,
    kv, shard, ubuf, dbuf, ru, rdn, zu, zd, bias, rvf, rvs, gbuf, notes, znotes,
    local_sem, gsend, grecv, fsend, frecv, usend, urecv, dsend, drecv,
    zusend, zurecv, zdsend, zdrecv, ausend, aurecv, adsend, adrecv,
    nsend, nrecv, znsend, znrecv,
):
    n_cont, n_z = dims
    n_plane = 2 * n_cont
    n_chip = n_cont // 2
    prefix = BLOCK * n_cont
    width = FEATURES // n_plane
    dests = n_plane // KVH
    dp = lax.axis_index("dp")
    cont = lax.axis_index("cont")
    core = lax.rem(cont, 2)
    chip = cont // 2
    zi = dp // 2
    xlo = lax.rem(dp, 2)
    me = xlo * n_cont + cont

    def plane_dev(p):
        return {"dp": zi * 2 + p // n_cont, "cont": lax.rem(p, n_cont)}

    def z_dev(z):
        return {"dp": z * 2 + xlo, "cont": cont}

    barrier = pltpu.get_barrier_semaphore()

    def greet_plane(k, carry):
        pl.semaphore_signal(
            barrier, inc=1, device_id=plane_dev(lax.rem(me + k, n_plane)), device_id_type=MESH
        )
        return carry

    def greet_z(k, carry):
        pl.semaphore_signal(barrier, inc=1, device_id=z_dev(lax.rem(zi + k, n_z)), device_id_type=MESH)
        return carry

    lax.fori_loop(1, n_plane, greet_plane, 0)
    lax.fori_loop(1, n_z, greet_z, 0)

    loads = []
    for i, (src, dst) in enumerate(
        (
            (vs_hbm, vshard),
            (rd_hbm, rd),
            (ks_hbm, shard.at[:, HD:]),
            (dmap_hbm, dmap),
            (tokens_hbm, tokens),
            (sv_hbm, sv),
            (lens_hbm, lens),
            (plen_hbm, plen),
            (mask_hbm, mask),
            (fq_hbm, fq),
            (up_hbm, up),
            (sk_hbm, sk),
        )
    ):
        cp = pltpu.make_async_copy(src, dst, local_sem.at[i])
        cp.start()
        loads.append(cp)
    ld_vs, ld_rd, ld_ks, ld_dmap, ld_tokens, ld_sv, ld_lens, ld_plen, ld_mask, ld_fq, ld_up, ld_sk = loads

    ld_vs.wait()
    ld_rd.wait()
    rd2 = jnp.concatenate([rd[...], rd[...]], axis=0)
    row_g = lax.rem(iota((HD, HD), 0), HQ) // HPG

    def rv_of(values):
        total = None
        for g in range(KVH):
            w = jnp.where(row_g == g, rd2, jnp.zeros_like(rd2))
            part = nt(values[:, g * HD : (g + 1) * HD], w)
            total = part if total is None else total + part
        return total

    rv = rv_of(vshard[...])
    high = rv.astype(bf16).astype(f32)
    shard[:, 0:HD] = jnp.where(iota(rv.shape, 1) < HQ, high, rv - high).astype(bf16)
    ld_ks.wait()
    kv[core, chip] = shard[...]

    pl.semaphore_wait(barrier, n_plane - 1 + n_z - 1)

    def block_cols(n):
        return pl.ds(pl.multiple_of(n * HD, HD), HD)

    def gather_copy(n, k, slot):
        return pltpu.make_async_remote_copy(
            src_ref=shard.at[:, block_cols(n)],
            dst_ref=kv.at[core, slot, :, block_cols(n)],
            send_sem=gsend.at[n, k],
            recv_sem=grecv.at[n, slot],
            device_id={"cont": lax.rem(chip + k, n_chip) * 2 + core},
            device_id_type=MESH,
        )

    def issue(n):
        def one(k, carry):
            gather_copy(n, k, chip).start()
            return carry

        lax.fori_loop(1, n_chip, one, 0)

    def forward_copy(n, which):
        return pltpu.make_async_remote_copy(
            src_ref=kv.at[core, :, :, block_cols(n)],
            dst_ref=kv.at[which, :, :, block_cols(n)],
            send_sem=fsend.at[n],
            recv_sem=frecv.at[n],
            device_id={"cont": chip * 2 + (1 - core)},
            device_id_type=MESH,
        )

    def arrive(n):
        def one(k, carry):
            gather_copy(n, k, lax.rem(chip + n_chip - k, n_chip)).wait_recv()
            return carry

        lax.fori_loop(1, n_chip, one, 0)
        forward_copy(n, core).start()

    issue(0)
    issue(1)
    issue(2)

    ld_dmap.wait()
    ld_tokens.wait()
    down_t = nt(dmap[...], tokens[...]).astype(bf16)
    down = down_t.astype(f32).T.astype(bf16)
    ld_lens.wait()
    len0 = lens[0, 0]
    len1 = lens[0, 1]
    lane = iota((RANK, HD), 1)
    t_of = lax.rem(lane, STEP)
    sign = jnp.where(
        lane < STEP,
        jnp.where(t_of < len0, -1.0, 0.0),
        jnp.where(t_of < len1, 1.0, 0.0),
    ).astype(f32)
    down_signed = (down_t.astype(f32) * sign).astype(bf16)

    ld_plen.wait()
    ld_mask.wait()
    limit = plen[0]
    for c in range(2):
        for b in range(n_cont):
            block = 2 * (b % n_chip) + b // n_chip
            ok = (mask[c, block] > 0) & (block * BLOCK < limit)
            bias[c, pl.ds(b * BLOCK, BLOCK), :] = jnp.full((BLOCK, HD), jnp.where(ok, 0.0, NEG), f32)
    causal = jnp.where(iota((STEP, HD), 0) > lax.rem(iota((STEP, HD), 1), STEP), NEG, 0.0).astype(f32)
    causal = jnp.concatenate([causal] * (HALF // HD), axis=1)

    ld_sv.wait()
    rvs[...] = rv_of(sv[...])
    ld_fq.wait()
    ld_up.wait()
    ld_sk.wait()

    def up_copy(p, slot):
        return pltpu.make_async_remote_copy(
            src_ref=ubuf.at[:, pl.ds(pl.multiple_of(p * width, 128), width)],
            dst_ref=ru.at[slot],
            send_sem=usend.at[p],
            recv_sem=urecv.at[slot],
            device_id=plane_dev(p),
            device_id_type=MESH,
        )

    def group_step(g, carry):
        accs = list(carry[:4])
        dd = carry[4]

        @pl.when(g + 2 <= KVH)
        def _():
            arrive(g + 2)

        @pl.when(g + 3 <= KVH)
        def _():
            issue(g + 3)

        forward_copy(g + 1, 1 - core).wait_recv()

        col = pl.multiple_of(g * GCOL, GCOL)
        fq_g = fq[:, pl.ds(col, GCOL)]
        up_g = up[:, pl.ds(col, GCOL)]
        qp_g = (fq_g.astype(f32) + ADAPTER_SCALE * nn(down, up_g)).astype(bf16)
        kp = kv[:, :, :, block_cols(g + 1)].reshape(prefix, HD)
        kp_t = kp.T
        ks = sk[:, block_cols(g)]
        units = [(c, j) for c in range(2) for j in range(2)]

        def query_t(q_g, c, j):
            rows = slice(c * STEP, (c + 1) * STEP)
            parts = []
            for i in range(2):
                h = 4 * j + 2 * i
                parts.append(
                    jnp.concatenate(
                        [q_g[rows, h * HD : (h + 1) * HD], q_g[rows, (h + 1) * HD : (h + 2) * HD]], axis=0
                    ).T
                )
            return jnp.concatenate(parts, axis=1)

        def stage_a(c, j):
            ks_c = ks[c * STEP : (c + 1) * STEP]
            out = []
            for q_g in (qp_g, fq_g):
                q = query_t(q_g, c, j)
                out.append((nn(kp, q), nn(ks_c, q)))
            return out

        def expand(rows, j):
            parts = []
            for i in range(2):
                index = g * HPG + 4 * j + 2 * i + iota(rows.shape, 1) // STEP
                parts.append(jnp.take_along_axis(rows, index, axis=1))
            return jnp.concatenate(parts, axis=1)

        def softmax(s_p, s_s, bias_c, rv_p, rv_s):
            s_p = s_p + bias_c
            s_s = s_s + causal
            peak = jnp.maximum(jnp.max(s_p, axis=0, keepdims=True), jnp.max(s_s, axis=0, keepdims=True))
            e_p = jnp.exp2((s_p - peak) * (FACTOR * LOG2E))
            e_s = jnp.exp2((s_s - peak) * (FACTOR * LOG2E))
            total = jnp.sum(e_p, axis=0, keepdims=True) + jnp.sum(e_s, axis=0, keepdims=True)
            o = jnp.sum(e_p * rv_p, axis=0, keepdims=True) + jnp.sum(e_s * rv_s, axis=0, keepdims=True)
            inverse = 1.0 / total
            return e_p, e_s, inverse, o * inverse

        def stage_b(scores, c, j):
            bias_c = jnp.concatenate([bias[c]] * (HALF // HD), axis=1)
            rv_p = expand(rvf[...], j)
            rv_s = expand(rvs[c * STEP : (c + 1) * STEP], j)
            e_p, e_s, inverse, o = softmax(*scores[0], bias_c, rv_p, rv_s)
            o_ref = softmax(*scores[1], bias_c, rv_p, rv_s)[3]
            ds_p = (e_p * (rv_p - o)).astype(bf16)
            ds_s = (e_s * (rv_s - o)).astype(bf16)
            return ds_p, ds_s, inverse * FACTOR, o - o_ref

        def stage_c(ds_p, ds_s, scale, c, j):
            ks_t = ks[c * STEP : (c + 1) * STEP].T
            dq = ((nn(kp_t, ds_p) + nn(ks_t, ds_s)) * scale).astype(bf16)
            for i in range(2):
                h = 4 * j + 2 * i
                nat = dq[:, i * HD : (i + 1) * HD].T
                for k in range(2):
                    gbuf[pl.ds(c * STEP, STEP), (h + k) * HD : (h + k + 1) * HD] = nat[
                        k * STEP : (k + 1) * STEP
                    ]

        scores = {0: stage_a(*units[0])}
        for u in range(4):
            if u + 1 < 4:
                scores[u + 1] = stage_a(*units[u + 1])
            ds_p, ds_s, scale, diff = stage_b(scores.pop(u), *units[u])
            accs[u] = accs[u] + diff
            stage_c(ds_p, ds_s, scale, *units[u])

        gq = gbuf[...]
        ubuf[:, pl.ds(col, GCOL)] = nn(down_signed, gq).astype(bf16)
        dd = dd + nt(up_g, gq)
        for i in range(dests):
            p = g * dests + i

            @pl.when(p != me)
            def _(p=p):
                up_copy(p, me).start()

        return (*accs, dd)

    arrive(0)
    arrive(1)
    forward_copy(0, 1 - core).wait_recv()
    rvx = kv[:, :, :, 0:HD].reshape(prefix, HD).astype(f32)
    rvf[...] = rvx + pltpu.roll(rvx, HQ, 1)

    zero_acc = jnp.zeros((1, HALF), f32)
    carry = lax.fori_loop(0, KVH, group_step, (zero_acc,) * 4 + (jnp.zeros((RANK, HD), f32),))
    dd = carry[4]

    tl = lax.rem(iota((1, HALF), 1), STEP)
    m0 = jnp.sum(jnp.where(tl < len0, carry[0] + carry[1], 0.0), axis=1, keepdims=True)
    m1 = jnp.sum(jnp.where(tl < len1, carry[2] + carry[3], 0.0), axis=1, keepdims=True)
    zv = BETA * (m0 - m1)
    small = jnp.exp(-jnp.abs(zv))
    loss = jnp.maximum(-zv, 0.0) + jnp.log1p(small)
    weight = (BETA * LOSS_SCALE) * jnp.where(zv >= 0.0, small, 1.0) / (1.0 + small)

    def note_copy(k, slot):
        return pltpu.make_async_remote_copy(
            src_ref=notes.at[me],
            dst_ref=notes.at[slot],
            send_sem=nsend.at[k],
            recv_sem=nrecv.at[slot],
            device_id=plane_dev(lax.rem(me + k, n_plane)),
            device_id_type=MESH,
        )

    notes[me] = jnp.where(iota((1, HD), 1) < 64, loss, weight)

    def start_note(k, carry):
        note_copy(k, me).start()
        return carry

    lax.fori_loop(1, n_plane, start_note, 0)

    dd = (ADAPTER_SCALE * dd * sign).astype(bf16)

    def down_copy(p, slot):
        return pltpu.make_async_remote_copy(
            src_ref=dbuf.at[:, pl.ds(pl.multiple_of(p * width, 128), width)],
            dst_ref=rdn.at[slot],
            send_sem=dsend.at[p],
            recv_sem=drecv.at[slot],
            device_id=plane_dev(p),
            device_id_type=MESH,
        )

    def finish(i, carry):
        cols = pl.ds(pl.multiple_of(i * GCOL, GCOL), GCOL)
        dbuf[:, cols] = (nn(dd, tokens[:, cols]) * weight).astype(bf16)
        for k in range(dests):
            p = i * dests + k

            @pl.when(p != me)
            def _(p=p):
                down_copy(p, me).start()

        return carry

    lax.fori_loop(0, KVH, finish, 0)

    my_cols = pl.ds(pl.multiple_of(me * width, 128), width)

    def z_copies(buf, send, recv):
        def make(k, slot):
            return pltpu.make_async_remote_copy(
                src_ref=buf.at[zi],
                dst_ref=buf.at[slot],
                send_sem=send.at[k],
                recv_sem=recv.at[slot],
                device_id=z_dev(lax.rem(zi + k, n_z)),
                device_id_type=MESH,
            )

        def start():
            for k in range(1, n_z):
                make(k, zi).start()

        def end():
            for k in range(1, n_z):
                make(k, lax.rem(zi + n_z - k, n_z)).wait_recv()
            out = buf[0].astype(f32)
            for z in range(1, n_z):
                out = out + buf[z].astype(f32)
            return out

        def drain():
            for k in range(1, n_z):
                make(k, zi).wait_send()

        return start, end, drain

    def all_copies(row, send, recv):
        def make(k, p):
            part = grads.at[pl.ds(row, RANK), pl.ds(pl.multiple_of(p * width, 128), width)]
            return pltpu.make_async_remote_copy(
                src_ref=part,
                dst_ref=part,
                send_sem=send.at[k],
                recv_sem=recv.at[p],
                device_id=plane_dev(lax.rem(me + k, n_plane)),
                device_id_type=MESH,
            )

        def loop(step):
            def one(k, carry):
                step(k)
                return carry

            lax.fori_loop(1, n_plane, one, 0)

        def start():
            loop(lambda k: make(k, me).start())

        def end():
            loop(lambda k: make(k, lax.rem(me + n_plane - k, n_plane)).wait_recv())

        def drain():
            loop(lambda k: make(k, me).wait_send())

        return start, end, drain

    zu_start, zu_end, zu_drain = z_copies(zu, zusend, zurecv)
    zd_start, zd_end, zd_drain = z_copies(zd, zdsend, zdrecv)
    zn_start, zn_end, zn_drain = z_copies(znotes, znsend, znrecv)
    au_start, au_end, au_drain = all_copies(0, ausend, aurecv)
    ad_start, ad_end, ad_drain = all_copies(RANK, adsend, adrecv)

    def up_sum(k, acc):
        slot = lax.rem(me + n_plane - k, n_plane)
        note_copy(k, slot).wait_recv()
        up_copy(slot, slot).wait_recv()
        return acc + notes[slot][:, HD - 1 : HD] * ru[slot].astype(f32)

    acc = lax.fori_loop(1, n_plane, up_sum, weight * ubuf[:, my_cols].astype(f32))
    zu[zi] = (ADAPTER_SCALE * acc).astype(bf16)
    zu_start()

    def note_sum(p, acc):
        return acc + notes[p]

    znotes[zi] = lax.fori_loop(1, n_plane, note_sum, notes[0])
    zn_start()

    def down_sum(k, acc):
        slot = lax.rem(me + n_plane - k, n_plane)
        down_copy(slot, slot).wait_recv()
        return acc + rdn[slot].astype(f32)

    acc = lax.fori_loop(1, n_plane, down_sum, dbuf[:, my_cols].astype(f32))
    zd[zi] = acc.astype(bf16)
    zd_start()

    grads[pl.ds(0, RANK), my_cols] = zu_end().astype(bf16)
    au_start()
    loss_out[...] = zn_end()
    grads[pl.ds(RANK, RANK), my_cols] = zd_end().astype(bf16)
    ad_start()

    def drain_gather(k, carry):
        for n in range(KVH + 1):
            gather_copy(n, k, chip).wait_send()
        return carry

    lax.fori_loop(1, n_chip, drain_gather, 0)
    for n in range(KVH + 1):
        forward_copy(n, core).wait_send()

    def drain_plane(k, carry):
        p = lax.rem(me + k, n_plane)
        up_copy(p, me).wait_send()
        down_copy(p, me).wait_send()
        note_copy(k, me).wait_send()
        return carry

    lax.fori_loop(1, n_plane, drain_plane, 0)
    zu_drain()
    zd_drain()
    zn_drain()
    au_drain()
    au_end()
    ad_drain()
    ad_end()


def local(n_cont, n_z, tokens, fq, sk, sv, kshard, vshard, dmap, up, readout, lens, plen, mask):
    n_plane = 2 * n_cont
    n_chip = n_cont // 2
    width = FEATURES // n_plane
    rows = tokens.shape[0]
    prefix = BLOCK * n_cont
    cols = HD + KVH * HD
    anyspec = pl.BlockSpec(memory_space=pl.ANY)
    vspec = pl.BlockSpec(memory_space=pltpu.VMEM)
    dma = pltpu.SemaphoreType.DMA
    grads, loss = pl.pallas_call(
        functools.partial(kernel, (n_cont, n_z)),
        out_shape=(
            jax.ShapeDtypeStruct((2 * RANK, FEATURES), bf16),
            jax.ShapeDtypeStruct((1, 128), f32),
        ),
        in_specs=[anyspec] * 12,
        out_specs=(vspec, vspec),
        scratch_shapes=[
            pltpu.VMEM((rows, FEATURES), bf16),
            pltpu.VMEM((rows, FEATURES), bf16),
            pltpu.VMEM((rows, KVH * HD), bf16),
            pltpu.VMEM((rows, KVH * HD), bf16),
            pltpu.VMEM((RANK, FEATURES), bf16),
            pltpu.VMEM((RANK, FEATURES), bf16),
            pltpu.VMEM((BLOCK, KVH * HD), bf16),
            pltpu.VMEM((HQ, HD), bf16),
            pltpu.SMEM((1, 2), jnp.int32),
            pltpu.SMEM((1,), jnp.int32),
            pltpu.SMEM((2, n_cont), jnp.int32),
            pltpu.VMEM((2, n_chip, BLOCK, cols), bf16),
            pltpu.VMEM((BLOCK, cols), bf16),
            pltpu.VMEM((RANK, FEATURES), bf16),
            pltpu.VMEM((RANK, FEATURES), bf16),
            pltpu.VMEM((n_plane, RANK, width), bf16),
            pltpu.VMEM((n_plane, RANK, width), bf16),
            pltpu.VMEM((n_z, RANK, width), bf16),
            pltpu.VMEM((n_z, RANK, width), bf16),
            pltpu.VMEM((2, prefix, HD), f32),
            pltpu.VMEM((prefix, HD), f32),
            pltpu.VMEM((rows, HD), f32),
            pltpu.VMEM((rows, GCOL), bf16),
            pltpu.VMEM((n_plane, 1, 128), f32),
            pltpu.VMEM((n_z, 1, 128), f32),
            dma((12,)),
            dma((KVH + 1, n_chip)),
            dma((KVH + 1, n_chip)),
            dma((KVH + 1,)),
            dma((KVH + 1,)),
            *[dma((n_plane,))] * 4,
            *[dma((n_z,))] * 4,
            *[dma((n_plane,))] * 6,
            *[dma((n_z,))] * 2,
        ],
        compiler_params=pltpu.CompilerParams(
            collective_id=0, has_side_effects=True, vmem_limit_bytes=60 * 1024 * 1024
        ),
    )(tokens, fq, sk, sv, kshard, vshard, dmap, up, readout.reshape(HQ, HD), lens, plen, mask)
    return loss[0, 0], grads[RANK:].astype(f32), grads[0:RANK].astype(f32)


def solution(mesh):
    return jax.shard_map(
        functools.partial(local, mesh.shape["cont"], mesh.shape["dp"] // 2),
        mesh=mesh,
        in_specs=(
            P(("dp", "cont"), None),
            P(("dp", "cont"), None),
            P(("dp", "cont"), None),
            P(("dp", "cont"), None),
            P(("dp", "cont"), None),
            P(("dp", "cont"), None),
            P(),
            P(),
            P(),
            P(("dp", "cont"), None),
            P("dp"),
            P(("dp", "cont"), None),
        ),
        out_specs=(P(), P(), P()),
        check_vma=False,
    )
```

```python
import functools

import jax
import jax.numpy as jnp
from jax import lax
from jax.experimental import pallas as pl
from jax.experimental.pallas import tpu as pltpu
from jax.sharding import PartitionSpec as P

HQ = 64
KVH = 8
HD = 128
HPG = HQ // KVH
BLOCK = 32
STEP = 64
RANK = 16
FEATURES = 8192
GCOL = HPG * HD
LANES = HPG * STEP
HALF = LANES // 2

NEG = -1e30
BETA = 0.1
ADAPTER_SCALE = 2.0
LOSS_SCALE = 1024.0
FACTOR = HD**-0.5
LOG2E = 1.4426950408889634

MESH = pl.DeviceIdType.MESH
f32 = jnp.float32
bf16 = jnp.bfloat16


def nn(a, b):
    return lax.dot_general(a, b, (((1,), (0,)), ((), ())), preferred_element_type=f32)


def nt(a, b):
    return lax.dot_general(a, b, (((1,), (1,)), ((), ())), preferred_element_type=f32)


def iota(shape, dim):
    return lax.broadcasted_iota(jnp.int32, shape, dim)


def kernel(
    dims,
    tokens_hbm, fq_hbm, sk_hbm, sv_hbm, ks_hbm, vs_hbm, dmap_hbm, up_hbm, rd_hbm,
    lens_hbm, plen_hbm, mask_hbm,
    grads, loss_out,
    tokens, fq, sk, sv, dmap, up, vshard, rd, lens, plen, mask,
    kv, shard, ubuf, dbuf, ru, rdn, zu, zd, qt, seen, rvf, rvs, gbuf, notes, znotes,
    local_sem, gsend, grecv, fsend, frecv, usend, urecv, dsend, drecv, nsend, nrecv,
    zusend, zurecv, zdsend, zdrecv, znsend, znrecv, ausend, aurecv, adsend, adrecv,
    susend, surecv, sdsend, sdrecv,
):
    n_cont, n_z = dims
    n_plane = 2 * n_cont
    n_chip = n_cont // 2
    prefix = BLOCK * n_cont
    width = FEATURES // n_plane
    dests = n_plane // KVH
    n_half = n_plane // 2
    dp = lax.axis_index("dp")
    cont = lax.axis_index("cont")
    core = lax.rem(cont, 2)
    chip = cont // 2
    zi = dp // 2
    xlo = lax.rem(dp, 2)
    place = xlo * n_chip + chip
    me = core * n_half + place

    def plane_dev(p):
        r = lax.rem(p, n_half)
        return {"dp": zi * 2 + r // n_chip, "cont": lax.rem(r, n_chip) * 2 + p // n_half}

    sibling = {"cont": chip * 2 + (1 - core)}

    def remote(src, dst, send, recv, to):
        return pltpu.make_async_remote_copy(
            src_ref=src, dst_ref=dst, send_sem=send, recv_sem=recv, device_id=to, device_id_type=MESH
        )

    def z_dev(z):
        return {"dp": z * 2 + xlo, "cont": cont}

    barrier = pltpu.get_barrier_semaphore()

    def greet_plane(k, carry):
        pl.semaphore_signal(
            barrier, inc=1, device_id=plane_dev(lax.rem(me + k, n_plane)), device_id_type=MESH
        )
        return carry

    def greet_z(k, carry):
        pl.semaphore_signal(barrier, inc=1, device_id=z_dev(lax.rem(zi + k, n_z)), device_id_type=MESH)
        return carry

    lax.fori_loop(1, n_plane, greet_plane, 0)
    lax.fori_loop(1, n_z, greet_z, 0)

    loads = []
    for i, (src, dst) in enumerate(
        (
            (vs_hbm, vshard),
            (rd_hbm, rd),
            (ks_hbm, shard.at[:, HD:]),
            (dmap_hbm, dmap),
            (tokens_hbm, tokens),
            (sv_hbm, sv),
            (lens_hbm, lens),
            (plen_hbm, plen),
            (mask_hbm, mask),
            (fq_hbm, fq),
            (up_hbm, up),
            (sk_hbm, sk),
        )
    ):
        cp = pltpu.make_async_copy(src, dst, local_sem.at[i])
        cp.start()
        loads.append(cp)
    ld_vs, ld_rd, ld_ks, ld_dmap, ld_tokens, ld_sv, ld_lens, ld_plen, ld_mask, ld_fq, ld_up, ld_sk = loads

    ld_vs.wait()
    ld_rd.wait()
    rd2 = jnp.concatenate([rd[...], rd[...]], axis=0)
    row_g = lax.rem(iota((HD, HD), 0), HQ) // HPG

    def rv_of(values):
        total = None
        for g in range(KVH):
            w = jnp.where(row_g == g, rd2, jnp.zeros_like(rd2))
            part = nt(values[:, g * HD : (g + 1) * HD], w)
            total = part if total is None else total + part
        return total

    rv = rv_of(vshard[...])
    high = rv.astype(bf16).astype(f32)
    shard[:, 0:HD] = jnp.where(iota(rv.shape, 1) < HQ, high, rv - high).astype(bf16)
    ld_ks.wait()
    kv[core, chip] = shard[...]

    pl.semaphore_wait(barrier, n_plane - 1 + n_z - 1)

    part_width = 3 * HD

    def part_cols(n):
        return pl.ds(pl.multiple_of(n * part_width, HD), part_width)

    def block_cols(n):
        return pl.ds(pl.multiple_of(n * HD, HD), HD)

    def issue(n):
        def one(k, carry):
            remote(
                shard.at[:, part_cols(n)],
                kv.at[core, chip, :, part_cols(n)],
                gsend.at[n],
                grecv.at[n],
                {"cont": lax.rem(chip + k, n_chip) * 2 + core},
            ).start()
            return carry

        lax.fori_loop(1, n_chip, one, 0)

    def forward_copy(n, which):
        part = kv.at[core, :, :, part_cols(n)]
        return remote(part, kv.at[which, :, :, part_cols(n)], fsend.at[n], frecv.at[n], sibling)

    def arrive(n):
        part = kv.at[core, pl.ds(0, n_chip - 1), :, part_cols(n)]
        remote(part, part, gsend.at[n], grecv.at[n], sibling).wait_recv()
        forward_copy(n, core).start()

    for n in range(3):
        issue(n)

    ld_dmap.wait()
    ld_tokens.wait()
    down_t = nt(dmap[...], tokens[...]).astype(bf16)
    down = down_t.astype(f32).T.astype(bf16)
    ld_lens.wait()
    len0 = lens[0, 0]
    len1 = lens[0, 1]
    lane = iota((RANK, HD), 1)
    t_of = lax.rem(lane, STEP)
    sign = jnp.where(
        lane < STEP,
        jnp.where(t_of < len0, -1.0, 0.0),
        jnp.where(t_of < len1, 1.0, 0.0),
    ).astype(f32)
    down_signed = (down_t.astype(f32) * sign).astype(bf16)

    ld_plen.wait()
    ld_mask.wait()
    limit = plen[0]
    for b in range(n_cont):
        block = 2 * (b % n_chip) + b // n_chip
        inside = block * BLOCK < limit
        fill = [jnp.where((mask[c, block] > 0) & inside, 0.0, NEG) for c in range(2)]
        col = iota((BLOCK, HD), 1)
        seen[pl.ds(b * BLOCK, BLOCK), :] = jnp.where(
            col == 0, fill[0], jnp.where(col == 1, fill[1], 0.0)
        ).astype(bf16)
    causal = jnp.where(iota((STEP, HD), 0) > lax.rem(iota((STEP, HD), 1), STEP), NEG, 0.0).astype(f32)
    causal = jnp.concatenate([causal] * (HALF // HD), axis=1)

    ld_sv.wait()
    rvs[...] = rv_of(sv[...])
    ld_fq.wait()
    ld_up.wait()
    ld_sk.wait()

    def prepare(g, carry):
        col = pl.multiple_of(g * GCOL, GCOL)
        frozen = fq[:, pl.ds(col, GCOL)].astype(f32) * (FACTOR * LOG2E)
        change = nn(down, up[:, pl.ds(col, GCOL)]) * (ADAPTER_SCALE * FACTOR * LOG2E)
        for s, q in enumerate(((frozen + change).astype(bf16), frozen.astype(bf16))):
            for c in range(2):
                rows = slice(c * STEP, (c + 1) * STEP)
                for h in range(0, HPG, 2):
                    pair = [q[rows, (h + i) * HD : (h + i + 1) * HD] for i in range(2)]
                    at = c * LANES + h * STEP
                    qt[s, g, :, at : at + HD] = jnp.concatenate(pair, axis=0).T
        return carry

    lax.fori_loop(0, KVH, prepare, 0)
    picks = [(iota((HD, HALF), 0) == c).astype(f32).astype(bf16) for c in range(2)]

    def up_copy(p):
        cols = pl.ds(pl.multiple_of(p * width, 128), width)
        return remote(ubuf.at[:, cols], ru.at[me], usend.at[0], urecv.at[0], plane_dev(p))

    def group_step(g, carry):
        accs = list(carry[:4])
        dd = carry[4]

        for n in (1, 2):

            @pl.when(g == 3 * n - 2)
            def _(n=n):
                arrive(n)

            @pl.when(g == 3 * n - 1)
            def _(n=n):
                forward_copy(n, 1 - core).wait_recv()

        col = pl.multiple_of(g * GCOL, GCOL)
        up_g = up[:, pl.ds(col, GCOL)]
        kp = kv[:, :, :, block_cols(g + 1)].reshape(prefix, HD)
        kp_seen = jnp.concatenate([kp, seen[...]], axis=1)
        kp_t = kp.T
        ks = sk[:, block_cols(g)]
        units = [(c, j) for c in range(2) for j in range(2)]

        def stage_a(c, j):
            ks_c = ks[c * STEP : (c + 1) * STEP]
            out = []
            for s in range(2):
                at = c * LANES + j * HALF
                q = qt[s, g, :, at : at + HALF]
                out.append((nn(kp_seen, jnp.concatenate([q, picks[c]], axis=0)), nn(ks_c, q)))
            return out

        def expand(rows, j):
            parts = []
            for i in range(2):
                index = g * HPG + 4 * j + 2 * i + iota(rows.shape, 1) // STEP
                parts.append(jnp.take_along_axis(rows, index, axis=1))
            return jnp.concatenate(parts, axis=1)

        def softmax(s_p, s_s, rv_p, rv_s):
            s_s = s_s + causal
            peak = jnp.maximum(jnp.max(s_p, axis=0, keepdims=True), jnp.max(s_s, axis=0, keepdims=True))
            e_p = jnp.exp2(s_p - peak)
            e_s = jnp.exp2(s_s - peak)
            total = jnp.sum(e_p, axis=0, keepdims=True) + jnp.sum(e_s, axis=0, keepdims=True)
            o = jnp.sum(e_p * rv_p, axis=0, keepdims=True) + jnp.sum(e_s * rv_s, axis=0, keepdims=True)
            inverse = 1.0 / total
            return e_p, e_s, inverse, o * inverse

        def stage_b(scores, c, j):
            rv_p = expand(rvf[...], j)
            rv_s = expand(rvs[c * STEP : (c + 1) * STEP], j)
            e_p, e_s, inverse, o = softmax(*scores[0], rv_p, rv_s)
            o_ref = softmax(*scores[1], rv_p, rv_s)[3]
            ds_p = (e_p * (rv_p - o)).astype(bf16)
            ds_s = (e_s * (rv_s - o)).astype(bf16)
            return ds_p, ds_s, inverse * FACTOR, o - o_ref

        def stage_c(ds_p, ds_s, scale, c, j):
            ks_t = ks[c * STEP : (c + 1) * STEP].T
            dq = ((nn(kp_t, ds_p) + nn(ks_t, ds_s)) * scale).astype(bf16)
            for i in range(2):
                h = 4 * j + 2 * i
                nat = dq[:, i * HD : (i + 1) * HD].T
                for k in range(2):
                    gbuf[pl.ds(c * STEP, STEP), (h + k) * HD : (h + k + 1) * HD] = nat[
                        k * STEP : (k + 1) * STEP
                    ]

        scores = {0: stage_a(*units[0])}
        for u in range(4):
            if u + 1 < 4:
                scores[u + 1] = stage_a(*units[u + 1])
            ds_p, ds_s, scale, diff = stage_b(scores.pop(u), *units[u])
            accs[u] = accs[u] + diff
            stage_c(ds_p, ds_s, scale, *units[u])

        gq = gbuf[...]
        ubuf[:, pl.ds(col, GCOL)] = nn(down_signed, gq).astype(bf16)
        dd = dd + nt(up_g, gq)
        for i in range(dests):
            p = g * dests + i

            @pl.when(p != me)
            def _(p=p):
                up_copy(p).start()

        return (*accs, dd)

    arrive(0)
    forward_copy(0, 1 - core).wait_recv()
    rvx = kv[:, :, :, 0:HD].reshape(prefix, HD).astype(f32)
    rvf[...] = rvx + pltpu.roll(rvx, HQ, 1)

    zero_acc = jnp.zeros((1, HALF), f32)
    carry = lax.fori_loop(0, KVH, group_step, (zero_acc,) * 4 + (jnp.zeros((RANK, HD), f32),))
    dd = carry[4]

    tl = lax.rem(iota((1, HALF), 1), STEP)
    m0 = jnp.sum(jnp.where(tl < len0, carry[0] + carry[1], 0.0), axis=1, keepdims=True)
    m1 = jnp.sum(jnp.where(tl < len1, carry[2] + carry[3], 0.0), axis=1, keepdims=True)
    zv = BETA * (m0 - m1)
    small = jnp.exp(-jnp.abs(zv))
    loss = jnp.maximum(-zv, 0.0) + jnp.log1p(small)
    weight = (BETA * LOSS_SCALE) * jnp.where(zv >= 0.0, small, 1.0) / (1.0 + small)

    notes[me] = jnp.where(iota((1, HD), 1) < 64, loss, weight)

    def start_note(k, carry):
        to = plane_dev(lax.rem(me + k, n_plane))
        remote(notes.at[me], notes.at[me], nsend.at[0], nrecv.at[0], to).start()
        return carry

    lax.fori_loop(1, n_plane, start_note, 0)

    dd = (ADAPTER_SCALE * dd * sign).astype(bf16)

    def down_copy(p):
        cols = pl.ds(pl.multiple_of(p * width, 128), width)
        return remote(dbuf.at[:, cols], rdn.at[me], dsend.at[0], drecv.at[0], plane_dev(p))

    def finish(i, carry):
        cols = pl.ds(pl.multiple_of(i * GCOL, GCOL), GCOL)
        dbuf[:, cols] = (nn(dd, tokens[:, cols]) * weight).astype(bf16)
        for k in range(dests):
            p = i * dests + k

            @pl.when(p != me)
            def _(p=p):
                down_copy(p).start()

        return carry

    lax.fori_loop(0, KVH, finish, 0)

    my_cols = pl.ds(pl.multiple_of(me * width, 128), width)

    def z_start(buf, send, recv):
        for k in range(1, n_z):
            remote(buf.at[zi], buf.at[zi], send, recv, z_dev(lax.rem(zi + k, n_z))).start()

    def z_end(buf, send, recv):
        others = buf.at[pl.ds(0, n_z - 1)]
        remote(others, others, send, recv, sibling).wait_recv()
        out = buf[0].astype(f32)
        for z in range(1, n_z):
            out = out + buf[z].astype(f32)
        return out

    def all_start(row, send, recv):
        part = grads.at[pl.ds(row, RANK), my_cols]

        def one(k, carry):
            to = plane_dev(core * n_half + lax.rem(place + k, n_half))
            remote(part, part, send, recv, to).start()
            return carry

        lax.fori_loop(1, n_half, one, 0)

    def half_of(row, which):
        return grads.at[
            pl.ds(row, RANK), pl.ds(pl.multiple_of(which * n_half * width, 128), n_half * width)
        ]

    def all_forward(row, recv, send, to_sibling):
        others = grads.at[pl.ds(row, RANK), pl.ds(0, (n_half - 1) * width)]
        remote(others, others, send, recv, sibling).wait_recv()
        remote(half_of(row, core), half_of(row, core), send, to_sibling, sibling).start()

    def all_end(row, send, to_sibling):
        remote(half_of(row, core), half_of(row, 1 - core), send, to_sibling, sibling).wait_recv()

    others = notes.at[pl.ds(0, n_plane - 1)]
    remote(others, others, nsend.at[0], nrecv.at[0], sibling).wait_recv()
    others = ru.at[pl.ds(0, n_plane - 1)]
    remote(others, others, usend.at[0], urecv.at[0], sibling).wait_recv()
    ru[me] = ubuf[:, my_cols]

    def up_sum(p, acc):
        return acc + notes[p][:, HD - 1 : HD] * ru[p].astype(f32)

    acc = lax.fori_loop(0, n_plane, up_sum, jnp.zeros((RANK, width), f32))
    zu[zi] = (ADAPTER_SCALE * acc).astype(bf16)
    z_start(zu, zusend.at[0], zurecv.at[0])

    def note_sum(p, acc):
        return acc + notes[p]

    znotes[zi] = lax.fori_loop(1, n_plane, note_sum, notes[0])
    z_start(znotes, znsend.at[0], znrecv.at[0])

    others = rdn.at[pl.ds(0, n_plane - 1)]
    remote(others, others, dsend.at[0], drecv.at[0], sibling).wait_recv()
    rdn[me] = dbuf[:, my_cols]

    def down_sum(p, acc):
        return acc + rdn[p].astype(f32)

    acc = lax.fori_loop(0, n_plane, down_sum, jnp.zeros((RANK, width), f32))
    zd[zi] = acc.astype(bf16)
    z_start(zd, zdsend.at[0], zdrecv.at[0])

    grads[pl.ds(0, RANK), my_cols] = z_end(zu, zusend.at[0], zurecv.at[0]).astype(bf16)
    all_start(0, ausend.at[0], aurecv.at[0])
    loss_out[...] = z_end(znotes, znsend.at[0], znrecv.at[0])
    grads[pl.ds(RANK, RANK), my_cols] = z_end(zd, zdsend.at[0], zdrecv.at[0]).astype(bf16)
    all_start(RANK, adsend.at[0], adrecv.at[0])

    all_forward(0, aurecv.at[0], susend.at[0], surecv.at[0])

    def sent(ref, sem):
        remote(ref, ref, sem, sem, sibling).wait_send()

    for n in range(3):
        sent(kv.at[core, pl.ds(0, n_chip - 1), :, part_cols(n)], gsend.at[n])
        sent(kv.at[core, :, :, part_cols(n)], fsend.at[n])
    sent(ru.at[pl.ds(0, n_plane - 1)], usend.at[0])
    sent(rdn.at[pl.ds(0, n_plane - 1)], dsend.at[0])
    sent(notes.at[pl.ds(0, n_plane - 1)], nsend.at[0])
    sent(zu.at[pl.ds(0, n_z - 1)], zusend.at[0])
    sent(zd.at[pl.ds(0, n_z - 1)], zdsend.at[0])
    sent(znotes.at[pl.ds(0, n_z - 1)], znsend.at[0])

    all_forward(RANK, adrecv.at[0], sdsend.at[0], sdrecv.at[0])
    for row, sem in ((0, ausend), (RANK, adsend)):
        sent(grads.at[pl.ds(row, RANK), pl.ds(0, (n_half - 1) * width)], sem.at[0])
    all_end(0, susend.at[0], surecv.at[0])
    all_end(RANK, sdsend.at[0], sdrecv.at[0])
    sent(half_of(0, core), susend.at[0])
    sent(half_of(RANK, core), sdsend.at[0])


def local(n_cont, n_z, tokens, fq, sk, sv, kshard, vshard, dmap, up, readout, lens, plen, mask):
    n_plane = 2 * n_cont
    n_chip = n_cont // 2
    width = FEATURES // n_plane
    rows = tokens.shape[0]
    prefix = BLOCK * n_cont
    cols = HD + KVH * HD
    anyspec = pl.BlockSpec(memory_space=pl.ANY)
    vspec = pl.BlockSpec(memory_space=pltpu.VMEM)
    dma = pltpu.SemaphoreType.DMA
    grads, loss = pl.pallas_call(
        functools.partial(kernel, (n_cont, n_z)),
        out_shape=(
            jax.ShapeDtypeStruct((2 * RANK, FEATURES), bf16),
            jax.ShapeDtypeStruct((1, 128), f32),
        ),
        in_specs=[anyspec] * 12,
        out_specs=(vspec, vspec),
        scratch_shapes=[
            pltpu.VMEM((rows, FEATURES), bf16),
            pltpu.VMEM((rows, FEATURES), bf16),
            pltpu.VMEM((rows, KVH * HD), bf16),
            pltpu.VMEM((rows, KVH * HD), bf16),
            pltpu.VMEM((RANK, FEATURES), bf16),
            pltpu.VMEM((RANK, FEATURES), bf16),
            pltpu.VMEM((BLOCK, KVH * HD), bf16),
            pltpu.VMEM((HQ, HD), bf16),
            pltpu.SMEM((1, 2), jnp.int32),
            pltpu.SMEM((1,), jnp.int32),
            pltpu.SMEM((2, n_cont), jnp.int32),
            pltpu.VMEM((2, n_chip, BLOCK, cols), bf16),
            pltpu.VMEM((BLOCK, cols), bf16),
            pltpu.VMEM((RANK, FEATURES), bf16),
            pltpu.VMEM((RANK, FEATURES), bf16),
            pltpu.VMEM((n_plane, RANK, width), bf16),
            pltpu.VMEM((n_plane, RANK, width), bf16),
            pltpu.VMEM((n_z, RANK, width), bf16),
            pltpu.VMEM((n_z, RANK, width), bf16),
            pltpu.VMEM((2, KVH, HD, 2 * LANES), bf16),
            pltpu.VMEM((prefix, HD), bf16),
            pltpu.VMEM((prefix, HD), f32),
            pltpu.VMEM((rows, HD), f32),
            pltpu.VMEM((rows, GCOL), bf16),
            pltpu.VMEM((n_plane, 1, 128), f32),
            pltpu.VMEM((n_z, 1, 128), f32),
            dma((12,)),
            *[dma((3,))] * 4,
            *[dma((1,))] * 20,
        ],
        compiler_params=pltpu.CompilerParams(
            collective_id=0, has_side_effects=True, vmem_limit_bytes=60 * 1024 * 1024
        ),
    )(tokens, fq, sk, sv, kshard, vshard, dmap, up, readout.reshape(HQ, HD), lens, plen, mask)
    return loss[0, 0], grads[RANK:].astype(f32), grads[0:RANK].astype(f32)


def solution(mesh):
    return jax.shard_map(
        functools.partial(local, mesh.shape["cont"], mesh.shape["dp"] // 2),
        mesh=mesh,
        in_specs=(
            P(("dp", "cont"), None),
            P(("dp", "cont"), None),
            P(("dp", "cont"), None),
            P(("dp", "cont"), None),
            P(("dp", "cont"), None),
            P(("dp", "cont"), None),
            P(),
            P(),
            P(),
            P(("dp", "cont"), None),
            P("dp"),
            P(("dp", "cont"), None),
        ),
        out_specs=(P(), P(), P()),
        check_vma=False,
    )
```

```python
import functools

import jax
import jax.numpy as jnp
from jax import lax
from jax.experimental import pallas as pl
from jax.experimental.pallas import tpu as pltpu
from jax.sharding import PartitionSpec as P

HQ = 64
KVH = 8
HD = 128
HPG = HQ // KVH
BLOCK = 32
STEP = 64
RANK = 16
FEATURES = 8192
GCOL = HPG * HD
LANES = HPG * STEP
HALF = LANES // 2

NEG = -1e30
BETA = 0.1
ADAPTER_SCALE = 2.0
LOSS_SCALE = 1024.0
FACTOR = HD**-0.5
LOG2E = 1.4426950408889634

MESH = pl.DeviceIdType.MESH
f32 = jnp.float32
bf16 = jnp.bfloat16


def nn(a, b):
    return lax.dot_general(a, b, (((1,), (0,)), ((), ())), preferred_element_type=f32)


def nt(a, b):
    return lax.dot_general(a, b, (((1,), (1,)), ((), ())), preferred_element_type=f32)


def iota(shape, dim):
    return lax.broadcasted_iota(jnp.int32, shape, dim)


def kernel(
    dims,
    tokens_hbm, fq_hbm, sk_hbm, sv_hbm, ks_hbm, vs_hbm, dmap_hbm, up_hbm, rd_hbm,
    lens_hbm, plen_hbm, mask_hbm,
    grads, loss_out,
    tokens, fq, sk, sv, dmap, up, vshard, rd, lens, plen, mask,
    kv, shard, ubuf, dbuf, ru, rdn, zu, zd, qt, seen, picks, rvf, rvs, sbuf, mbuf, gbuf, notes, znotes,
    local_sem, gsend, grecv, fsend, frecv, usend, urecv, dsend, drecv, nsend, nrecv,
    zusend, zurecv, zdsend, zdrecv, znsend, znrecv, ausend, aurecv, adsend, adrecv,
    susend, surecv, sdsend, sdrecv,
):
    n_cont, n_z = dims
    n_plane = 2 * n_cont
    n_chip = n_cont // 2
    prefix = BLOCK * n_cont
    width = FEATURES // n_plane
    dests = n_plane // KVH
    n_half = n_plane // 2
    dp = lax.axis_index("dp")
    cont = lax.axis_index("cont")
    core = lax.rem(cont, 2)
    chip = cont // 2
    zi = dp // 2
    xlo = lax.rem(dp, 2)
    place = xlo * n_chip + chip
    me = core * n_half + place

    def plane_dev(p):
        r = lax.rem(p, n_half)
        return {"dp": zi * 2 + r // n_chip, "cont": lax.rem(r, n_chip) * 2 + p // n_half}

    sibling = {"cont": chip * 2 + (1 - core)}

    def remote(src, dst, send, recv, to):
        return pltpu.make_async_remote_copy(
            src_ref=src, dst_ref=dst, send_sem=send, recv_sem=recv, device_id=to, device_id_type=MESH
        )

    def z_dev(z):
        return {"dp": z * 2 + xlo, "cont": cont}

    barrier = pltpu.get_barrier_semaphore()

    def greet_plane(k, carry):
        pl.semaphore_signal(
            barrier, inc=1, device_id=plane_dev(lax.rem(me + k, n_plane)), device_id_type=MESH
        )
        return carry

    def greet_z(k, carry):
        pl.semaphore_signal(barrier, inc=1, device_id=z_dev(lax.rem(zi + k, n_z)), device_id_type=MESH)
        return carry

    lax.fori_loop(1, n_plane, greet_plane, 0)
    lax.fori_loop(1, n_z, greet_z, 0)

    loads = []
    for i, (src, dst) in enumerate(
        (
            (vs_hbm, vshard),
            (rd_hbm, rd),
            (ks_hbm, shard.at[:, HD:]),
            (dmap_hbm, dmap),
            (tokens_hbm, tokens),
            (sv_hbm, sv),
            (lens_hbm, lens),
            (plen_hbm, plen),
            (mask_hbm, mask),
            (fq_hbm, fq),
            (up_hbm, up),
            (sk_hbm, sk),
        )
    ):
        cp = pltpu.make_async_copy(src, dst, local_sem.at[i])
        cp.start()
        loads.append(cp)
    ld_vs, ld_rd, ld_ks, ld_dmap, ld_tokens, ld_sv, ld_lens, ld_plen, ld_mask, ld_fq, ld_up, ld_sk = loads

    ld_vs.wait()
    ld_rd.wait()
    rd2 = jnp.concatenate([rd[...], rd[...]], axis=0)
    row_g = lax.rem(iota((HD, HD), 0), HQ) // HPG

    def rv_of(values):
        total = None
        for g in range(KVH):
            w = jnp.where(row_g == g, rd2, jnp.zeros_like(rd2))
            part = nt(values[:, g * HD : (g + 1) * HD], w)
            total = part if total is None else total + part
        return total

    rv = rv_of(vshard[...])
    high = rv.astype(bf16).astype(f32)
    shard[:, 0:HD] = jnp.where(iota(rv.shape, 1) < HQ, high, rv - high).astype(bf16)
    ld_ks.wait()
    kv[core, chip] = shard[...]

    pl.semaphore_wait(barrier, n_plane - 1 + n_z - 1)

    part_width = 3 * HD

    def part_cols(n):
        return pl.ds(pl.multiple_of(n * part_width, HD), part_width)

    def block_cols(n):
        return pl.ds(pl.multiple_of(n * HD, HD), HD)

    def issue(n):
        def one(k, carry):
            remote(
                shard.at[:, part_cols(n)],
                kv.at[core, chip, :, part_cols(n)],
                gsend.at[n],
                grecv.at[n],
                {"cont": lax.rem(chip + k, n_chip) * 2 + core},
            ).start()
            return carry

        lax.fori_loop(1, n_chip, one, 0)

    def forward_copy(n, which):
        part = kv.at[core, :, :, part_cols(n)]
        return remote(part, kv.at[which, :, :, part_cols(n)], fsend.at[n], frecv.at[n], sibling)

    def arrive(n):
        part = kv.at[core, pl.ds(0, n_chip - 1), :, part_cols(n)]
        remote(part, part, gsend.at[n], grecv.at[n], sibling).wait_recv()
        forward_copy(n, core).start()

    issue(0)

    ld_dmap.wait()
    ld_tokens.wait()
    down_t = nt(dmap[...], tokens[...]).astype(bf16)
    down = down_t.astype(f32).T.astype(bf16)
    ld_lens.wait()
    len0 = lens[0, 0]
    len1 = lens[0, 1]
    lane = iota((RANK, HD), 1)
    t_of = lax.rem(lane, STEP)
    sign = jnp.where(
        lane < STEP,
        jnp.where(t_of < len0, -1.0, 0.0),
        jnp.where(t_of < len1, 1.0, 0.0),
    ).astype(f32)
    down_signed = (down_t.astype(f32) * sign).astype(bf16)

    ld_plen.wait()
    ld_mask.wait()
    limit = plen[0]
    for b in range(n_cont):
        block = 2 * (b % n_chip) + b // n_chip
        inside = block * BLOCK < limit
        fill = [jnp.where((mask[c, block] > 0) & inside, 0.0, NEG) for c in range(2)]
        col = iota((BLOCK, HD), 1)
        seen[pl.ds(b * BLOCK, BLOCK), :] = jnp.where(
            col == 0, fill[0], jnp.where(col == 1, fill[1], 0.0)
        ).astype(bf16)
    causal = jnp.where(iota((STEP, HD), 0) > lax.rem(iota((STEP, HD), 1), STEP), NEG, 0.0).astype(f32)
    causal = jnp.concatenate([causal] * (HALF // HD), axis=1)

    ld_sv.wait()
    rvs[...] = rv_of(sv[...])
    issue(1)
    ld_fq.wait()
    ld_up.wait()
    ld_sk.wait()

    def prepare(g, carry):
        col = pl.multiple_of(g * GCOL, GCOL)
        frozen = fq[:, pl.ds(col, GCOL)].astype(f32) * (FACTOR * LOG2E)
        change = nn(down, up[:, pl.ds(col, GCOL)]) * (ADAPTER_SCALE * FACTOR * LOG2E)
        for s, q in enumerate(((frozen + change).astype(bf16), frozen.astype(bf16))):
            for c in range(2):
                rows = slice(c * STEP, (c + 1) * STEP)
                for h in range(0, HPG, 2):
                    pair = [q[rows, (h + i) * HD : (h + i + 1) * HD] for i in range(2)]
                    at = c * LANES + h * STEP
                    qt[s, g, :, at : at + HD] = jnp.concatenate(pair, axis=0).T
        return carry

    lax.fori_loop(0, KVH, prepare, 0)
    issue(2)
    for c in range(2):
        picks[c] = (iota((HD, HALF), 0) == c).astype(f32).astype(bf16)

    def up_copy(p):
        cols = pl.ds(pl.multiple_of(p * width, 128), width)
        return remote(ubuf.at[:, cols], ru.at[me], usend.at[0], urecv.at[0], plane_dev(p))

    units = [(c, j) for c in range(2) for j in range(2)]

    def stage_a(g, u, slot):
        c, j = units[u]
        kp = kv[:, :, :, block_cols(g + 1)].reshape(prefix, HD)
        ks = sk[pl.ds(c * STEP, STEP), block_cols(g)]
        at = c * LANES + j * HALF
        for s in range(2):
            q = qt[s, g, :, at : at + HALF]
            s_p = nn(jnp.concatenate([kp, seen[...]], axis=1), jnp.concatenate([q, picks[c]], axis=0))
            s_s = nn(ks, q) + causal
            sbuf[slot, s, pl.ds(0, prefix), :] = s_p
            sbuf[slot, s, pl.ds(prefix, STEP), :] = s_s
            mbuf[slot, s] = jnp.maximum(
                jnp.max(s_p, axis=0, keepdims=True), jnp.max(s_s, axis=0, keepdims=True)
            )

    def expand(rows, g, j):
        parts = []
        for i in range(2):
            index = g * HPG + 4 * j + 2 * i + iota(rows.shape, 1) // STEP
            parts.append(jnp.take_along_axis(rows, index, axis=1))
        return jnp.concatenate(parts, axis=1)

    def softmax(slot, s, rv_p, rv_s):
        peak = mbuf[slot, s]
        e_p = jnp.exp2(sbuf[slot, s, pl.ds(0, prefix), :] - peak)
        e_s = jnp.exp2(sbuf[slot, s, pl.ds(prefix, STEP), :] - peak)
        total = jnp.sum(e_p, axis=0, keepdims=True) + jnp.sum(e_s, axis=0, keepdims=True)
        o = jnp.sum(e_p * rv_p, axis=0, keepdims=True) + jnp.sum(e_s * rv_s, axis=0, keepdims=True)
        inverse = 1.0 / total
        return e_p, e_s, inverse, o * inverse

    def stage_b(g, u, slot):
        c, j = units[u]
        rv_p = expand(rvf[...], g, j)
        rv_s = expand(rvs[pl.ds(c * STEP, STEP), :], g, j)
        e_p, e_s, inverse, o = softmax(slot, 0, rv_p, rv_s)
        ds_p = (e_p * (rv_p - o)).astype(bf16)
        ds_s = (e_s * (rv_s - o)).astype(bf16)
        o_ref = softmax(slot, 1, rv_p, rv_s)[3]
        return ds_p, ds_s, inverse * FACTOR, o - o_ref

    def stage_c(g, u, kp_t, ds_p, ds_s, scale):
        c, j = units[u]
        ks_t = sk[pl.ds(c * STEP, STEP), block_cols(g)].T
        dq = ((nn(kp_t, ds_p) + nn(ks_t, ds_s)) * scale).astype(bf16)
        for i in range(2):
            h = 4 * j + 2 * i
            nat = dq[:, i * HD : (i + 1) * HD].T
            for k in range(2):
                gbuf[pl.ds(c * STEP, STEP), (h + k) * HD : (h + k + 1) * HD] = nat[
                    k * STEP : (k + 1) * STEP
                ]

    def tail(g, dd):
        col = pl.multiple_of(g * GCOL, GCOL)
        gq = gbuf[...]
        ubuf[:, pl.ds(col, GCOL)] = nn(down_signed, gq).astype(bf16)
        return dd + nt(up[:, pl.ds(col, GCOL)], gq)

    def send_up(g):
        for i in range(dests):
            p = g * dests + i

            @pl.when(p != me)
            def _(p=p):
                up_copy(p).start()

    def group_step(g, carry):
        accs = list(carry[:4])

        for n in (1, 2):

            @pl.when(g == 3 * n - 3)
            def _(n=n):
                arrive(n)

            @pl.when(g == 3 * n - 2)
            def _(n=n):
                forward_copy(n, 1 - core).wait_recv()

        @pl.when(g >= 2)
        def _():
            send_up(g - 2)

        dd = tail(jnp.maximum(g - 1, 0), carry[4])
        kp_t = kv[:, :, :, block_cols(g + 1)].reshape(prefix, HD).T
        for u in range(4):
            if u < 3:
                stage_a(g, u + 1, (u + 1) % 2)
            else:
                stage_a(jnp.minimum(g + 1, KVH - 1), 0, 0)
            ds_p, ds_s, scale, diff = stage_b(g, u, u % 2)
            accs[u] = accs[u] + diff
            stage_c(g, u, kp_t, ds_p, ds_s, scale)
        return (*accs, dd)

    arrive(0)
    forward_copy(0, 1 - core).wait_recv()
    rvx = kv[:, :, :, 0:HD].reshape(prefix, HD).astype(f32)
    rvf[...] = rvx + pltpu.roll(rvx, HQ, 1)

    gbuf[...] = jnp.zeros_like(gbuf)
    stage_a(0, 0, 0)
    zero_acc = jnp.zeros((1, HALF), f32)
    carry = lax.fori_loop(0, KVH, group_step, (zero_acc,) * 4 + (jnp.zeros((RANK, HD), f32),))
    send_up(KVH - 2)
    dd = tail(KVH - 1, carry[4])
    send_up(KVH - 1)

    tl = lax.rem(iota((1, HALF), 1), STEP)
    m0 = jnp.sum(jnp.where(tl < len0, carry[0] + carry[1], 0.0), axis=1, keepdims=True)
    m1 = jnp.sum(jnp.where(tl < len1, carry[2] + carry[3], 0.0), axis=1, keepdims=True)
    zv = BETA * (m0 - m1)
    small = jnp.exp(-jnp.abs(zv))
    loss = jnp.maximum(-zv, 0.0) + jnp.log1p(small)
    weight = (BETA * LOSS_SCALE) * jnp.where(zv >= 0.0, small, 1.0) / (1.0 + small)

    notes[me] = jnp.where(iota((2, HD), 0) == 0, loss, weight)

    def start_note(k, carry):
        to = plane_dev(lax.rem(me + k, n_plane))
        remote(notes.at[me], notes.at[me], nsend.at[0], nrecv.at[0], to).start()
        return carry

    dd = (ADAPTER_SCALE * dd * sign).astype(bf16)
    for i in range(KVH):
        cols = pl.ds(i * GCOL, GCOL)
        dbuf[:, cols] = nn(dd, tokens[:, cols]).astype(bf16)

    lax.fori_loop(1, n_plane, start_note, 0)

    def start_down(k, carry):
        p = lax.rem(me + k, n_plane)
        cols = pl.ds(pl.multiple_of(p * width, 128), width)
        remote(dbuf.at[:, cols], rdn.at[me], dsend.at[0], drecv.at[0], plane_dev(p)).start()
        return carry

    lax.fori_loop(1, n_plane, start_down, 0)

    my_cols = pl.ds(pl.multiple_of(me * width, 128), width)

    def z_start(buf, send, recv):
        for k in range(1, n_z):
            remote(buf.at[zi], buf.at[zi], send, recv, z_dev(lax.rem(zi + k, n_z))).start()

    def z_end(buf, send, recv):
        others = buf.at[pl.ds(0, n_z - 1)]
        remote(others, others, send, recv, sibling).wait_recv()
        out = buf[0].astype(f32)
        for z in range(1, n_z):
            out = out + buf[z].astype(f32)
        return out

    def all_start(row, send, recv):
        part = grads.at[pl.ds(row, RANK), my_cols]

        def one(k, carry):
            to = plane_dev(core * n_half + lax.rem(place + k, n_half))
            remote(part, part, send, recv, to).start()
            return carry

        lax.fori_loop(1, n_half, one, 0)

    def half_of(row, which):
        return grads.at[
            pl.ds(row, RANK), pl.ds(pl.multiple_of(which * n_half * width, 128), n_half * width)
        ]

    def all_forward(row, recv, send, to_sibling):
        others = grads.at[pl.ds(row, RANK), pl.ds(0, (n_half - 1) * width)]
        remote(others, others, send, recv, sibling).wait_recv()
        remote(half_of(row, core), half_of(row, core), send, to_sibling, sibling).start()

    def all_end(row, send, to_sibling):
        remote(half_of(row, core), half_of(row, 1 - core), send, to_sibling, sibling).wait_recv()

    others = notes.at[pl.ds(0, n_plane - 1)]
    remote(others, others, nsend.at[0], nrecv.at[0], sibling).wait_recv()
    others = ru.at[pl.ds(0, n_plane - 1)]
    remote(others, others, usend.at[0], urecv.at[0], sibling).wait_recv()
    ru[me] = ubuf[:, my_cols]

    def weighted(buf):
        acc = jnp.zeros((RANK, width), f32)
        for p in range(n_plane):
            w = jnp.concatenate([notes[p][1:2]] * (width // HD), axis=1)
            acc = acc + w * buf[p].astype(f32)
        return acc

    zu[zi] = (ADAPTER_SCALE * weighted(ru)).astype(bf16)
    z_start(zu, zusend.at[0], zurecv.at[0])
    loss_sum = notes[0][0:1]
    for p in range(1, n_plane):
        loss_sum = loss_sum + notes[p][0:1]
    znotes[zi] = loss_sum
    z_start(znotes, znsend.at[0], znrecv.at[0])

    others = rdn.at[pl.ds(0, n_plane - 1)]
    remote(others, others, dsend.at[0], drecv.at[0], sibling).wait_recv()
    rdn[me] = dbuf[:, my_cols]
    zd[zi] = weighted(rdn).astype(bf16)
    z_start(zd, zdsend.at[0], zdrecv.at[0])

    grads[pl.ds(0, RANK), my_cols] = z_end(zu, zusend.at[0], zurecv.at[0]).astype(bf16)
    all_start(0, ausend.at[0], aurecv.at[0])
    loss_out[...] = z_end(znotes, znsend.at[0], znrecv.at[0])
    grads[pl.ds(RANK, RANK), my_cols] = z_end(zd, zdsend.at[0], zdrecv.at[0]).astype(bf16)
    all_start(RANK, adsend.at[0], adrecv.at[0])

    all_forward(0, aurecv.at[0], susend.at[0], surecv.at[0])

    def sent(ref, sem):
        remote(ref, ref, sem, sem, sibling).wait_send()

    for n in range(3):
        sent(kv.at[core, pl.ds(0, n_chip - 1), :, part_cols(n)], gsend.at[n])
        sent(kv.at[core, :, :, part_cols(n)], fsend.at[n])
    sent(ru.at[pl.ds(0, n_plane - 1)], usend.at[0])
    sent(rdn.at[pl.ds(0, n_plane - 1)], dsend.at[0])
    sent(notes.at[pl.ds(0, n_plane - 1)], nsend.at[0])
    sent(zu.at[pl.ds(0, n_z - 1)], zusend.at[0])
    sent(zd.at[pl.ds(0, n_z - 1)], zdsend.at[0])
    sent(znotes.at[pl.ds(0, n_z - 1)], znsend.at[0])

    all_forward(RANK, adrecv.at[0], sdsend.at[0], sdrecv.at[0])
    for row, sem in ((0, ausend), (RANK, adsend)):
        sent(grads.at[pl.ds(row, RANK), pl.ds(0, (n_half - 1) * width)], sem.at[0])
    all_end(0, susend.at[0], surecv.at[0])
    all_end(RANK, sdsend.at[0], sdrecv.at[0])
    sent(half_of(0, core), susend.at[0])
    sent(half_of(RANK, core), sdsend.at[0])


def local(n_cont, n_z, tokens, fq, sk, sv, kshard, vshard, dmap, up, readout, lens, plen, mask):
    n_plane = 2 * n_cont
    n_chip = n_cont // 2
    width = FEATURES // n_plane
    rows = tokens.shape[0]
    prefix = BLOCK * n_cont
    cols = HD + KVH * HD
    anyspec = pl.BlockSpec(memory_space=pl.ANY)
    vspec = pl.BlockSpec(memory_space=pltpu.VMEM)
    dma = pltpu.SemaphoreType.DMA
    grads, loss = pl.pallas_call(
        functools.partial(kernel, (n_cont, n_z)),
        out_shape=(
            jax.ShapeDtypeStruct((2 * RANK, FEATURES), bf16),
            jax.ShapeDtypeStruct((1, 128), f32),
        ),
        in_specs=[anyspec] * 12,
        out_specs=(vspec, vspec),
        scratch_shapes=[
            pltpu.VMEM((rows, FEATURES), bf16),
            pltpu.VMEM((rows, FEATURES), bf16),
            pltpu.VMEM((rows, KVH * HD), bf16),
            pltpu.VMEM((rows, KVH * HD), bf16),
            pltpu.VMEM((RANK, FEATURES), bf16),
            pltpu.VMEM((RANK, FEATURES), bf16),
            pltpu.VMEM((BLOCK, KVH * HD), bf16),
            pltpu.VMEM((HQ, HD), bf16),
            pltpu.SMEM((1, 2), jnp.int32),
            pltpu.SMEM((1,), jnp.int32),
            pltpu.SMEM((2, n_cont), jnp.int32),
            pltpu.VMEM((2, n_chip, BLOCK, cols), bf16),
            pltpu.VMEM((BLOCK, cols), bf16),
            pltpu.VMEM((RANK, FEATURES), bf16),
            pltpu.VMEM((RANK, FEATURES), bf16),
            pltpu.VMEM((n_plane, RANK, width), bf16),
            pltpu.VMEM((n_plane, RANK, width), bf16),
            pltpu.VMEM((n_z, RANK, width), bf16),
            pltpu.VMEM((n_z, RANK, width), bf16),
            pltpu.VMEM((2, KVH, HD, 2 * LANES), bf16),
            pltpu.VMEM((prefix, HD), bf16),
            pltpu.VMEM((2, HD, HALF), bf16),
            pltpu.VMEM((prefix, HD), f32),
            pltpu.VMEM((rows, HD), f32),
            pltpu.VMEM((2, 2, prefix + STEP, HALF), f32),
            pltpu.VMEM((2, 2, 1, HALF), f32),
            pltpu.VMEM((rows, GCOL), bf16),
            pltpu.VMEM((n_plane, 2, 128), f32),
            pltpu.VMEM((n_z, 1, 128), f32),
            dma((12,)),
            *[dma((3,))] * 4,
            *[dma((1,))] * 20,
        ],
        compiler_params=pltpu.CompilerParams(
            collective_id=0, has_side_effects=True, vmem_limit_bytes=60 * 1024 * 1024
        ),
    )(tokens, fq, sk, sv, kshard, vshard, dmap, up, readout.reshape(HQ, HD), lens, plen, mask)
    return loss[0, 0], grads[RANK:].astype(f32), grads[0:RANK].astype(f32)


def solution(mesh):
    return jax.shard_map(
        functools.partial(local, mesh.shape["cont"], mesh.shape["dp"] // 2),
        mesh=mesh,
        in_specs=(
            P(("dp", "cont"), None),
            P(("dp", "cont"), None),
            P(("dp", "cont"), None),
            P(("dp", "cont"), None),
            P(("dp", "cont"), None),
            P(("dp", "cont"), None),
            P(),
            P(),
            P(),
            P(("dp", "cont"), None),
            P("dp"),
            P(("dp", "cont"), None),
        ),
        out_specs=(P(), P(), P()),
        check_vma=False,
    )
```

```python
import functools

import jax
import jax.numpy as jnp
from jax import lax
from jax.experimental import pallas as pl
from jax.experimental.pallas import tpu as pltpu
from jax.sharding import PartitionSpec as P

HQ = 64
KVH = 8
HD = 128
HPG = HQ // KVH
BLOCK = 32
STEP = 64
RANK = 16
FEATURES = 8192
GCOL = HPG * HD
LANES = HPG * STEP
HALF = LANES // 2

NEG = -1e30
BETA = 0.1
ADAPTER_SCALE = 2.0
LOSS_SCALE = 1024.0
FACTOR = HD**-0.5
LOG2E = 1.4426950408889634

MESH = pl.DeviceIdType.MESH
f32 = jnp.float32
bf16 = jnp.bfloat16


def nn(a, b):
    return lax.dot_general(a, b, (((1,), (0,)), ((), ())), preferred_element_type=f32)


def nt(a, b):
    return lax.dot_general(a, b, (((1,), (1,)), ((), ())), preferred_element_type=f32)


def iota(shape, dim):
    return lax.broadcasted_iota(jnp.int32, shape, dim)


def kernel(
    dims,
    tokens_hbm, fq_hbm, sk_hbm, sv_hbm, ks_hbm, vs_hbm, dmap_hbm, up_hbm, rd_hbm,
    lens_hbm, plen_hbm, mask_hbm,
    grads, loss_out,
    tokens, fq, sk, sv, dmap, up, vshard, rd, lens, plen, mask,
    kv, shard, ubuf, dbuf, ru, rdn, zu, zd, qt, seen, picks, rvf, rvt, rvs, rvst, rvx, sbuf, mbuf, gbuf, notes, znotes,
    local_sem, gsend, grecv, fsend, frecv, usend, urecv, dsend, drecv, nsend, nrecv,
    zusend, zurecv, zdsend, zdrecv, znsend, znrecv, ausend, aurecv, adsend, adrecv,
    susend, surecv, sdsend, sdrecv,
):
    n_cont, n_z = dims
    n_plane = 2 * n_cont
    n_chip = n_cont // 2
    prefix = BLOCK * n_cont
    width = FEATURES // n_plane
    dests = n_plane // KVH
    n_half = n_plane // 2
    dp = lax.axis_index("dp")
    cont = lax.axis_index("cont")
    core = lax.rem(cont, 2)
    chip = cont // 2
    zi = dp // 2
    xlo = lax.rem(dp, 2)
    place = xlo * n_chip + chip
    me = core * n_half + place

    def plane_dev(p):
        r = lax.rem(p, n_half)
        return {"dp": zi * 2 + r // n_chip, "cont": lax.rem(r, n_chip) * 2 + p // n_half}

    sibling = {"cont": chip * 2 + (1 - core)}

    def remote(src, dst, send, recv, to):
        return pltpu.make_async_remote_copy(
            src_ref=src, dst_ref=dst, send_sem=send, recv_sem=recv, device_id=to, device_id_type=MESH
        )

    def z_dev(z):
        return {"dp": z * 2 + xlo, "cont": cont}

    barrier = pltpu.get_barrier_semaphore()

    def greet_plane(k, carry):
        pl.semaphore_signal(
            barrier, inc=1, device_id=plane_dev(lax.rem(me + k, n_plane)), device_id_type=MESH
        )
        return carry

    def greet_z(k, carry):
        pl.semaphore_signal(barrier, inc=1, device_id=z_dev(lax.rem(zi + k, n_z)), device_id_type=MESH)
        return carry

    lax.fori_loop(1, n_plane, greet_plane, 0)
    lax.fori_loop(1, n_z, greet_z, 0)

    loads = []
    for i, (src, dst) in enumerate(
        (
            (vs_hbm, vshard),
            (rd_hbm, rd),
            (ks_hbm, shard.at[:, HD:]),
            (dmap_hbm, dmap),
            (tokens_hbm, tokens),
            (sv_hbm, sv),
            (lens_hbm, lens),
            (plen_hbm, plen),
            (mask_hbm, mask),
            (fq_hbm, fq),
            (up_hbm, up),
            (sk_hbm, sk),
        )
    ):
        cp = pltpu.make_async_copy(src, dst, local_sem.at[i])
        cp.start()
        loads.append(cp)
    ld_vs, ld_rd, ld_ks, ld_dmap, ld_tokens, ld_sv, ld_lens, ld_plen, ld_mask, ld_fq, ld_up, ld_sk = loads

    ld_vs.wait()
    ld_rd.wait()
    rdf = rd[...].astype(f32)
    rd2 = jnp.concatenate(
        [rdf[(i // 2) * HPG : (i // 2 + 1) * HPG] for i in range(2 * KVH)], axis=0
    ).astype(bf16)
    row_g = iota((HD, HD), 0) // (2 * HPG)

    def rv_of(values):
        total = None
        for g in range(KVH):
            w = jnp.where(row_g == g, rd2, jnp.zeros_like(rd2))
            part = nt(values[:, g * HD : (g + 1) * HD], w)
            total = part if total is None else total + part
        return total

    def parts_of(x):
        high = x.astype(bf16).astype(f32)
        return jnp.where(lax.rem(iota(x.shape, 1) // HPG, 2) == 0, high, x - high).astype(bf16)

    shard[:, 0:HD] = parts_of(rv_of(vshard[...]))
    ld_ks.wait()
    kv[core, chip] = shard[...]

    pl.semaphore_wait(barrier, n_plane - 1 + n_z - 1)

    part_at = (0, 2, 3, 6, 9)
    n_parts = len(part_at) - 1

    def part_cols(n):
        return pl.ds(part_at[n] * HD, (part_at[n + 1] - part_at[n]) * HD)

    def block_cols(n):
        return pl.ds(pl.multiple_of(n * HD, HD), HD)

    def issue(n):
        def one(k, carry):
            remote(
                shard.at[:, part_cols(n)],
                kv.at[core, chip, :, part_cols(n)],
                gsend.at[n],
                grecv.at[n],
                {"cont": lax.rem(chip + k, n_chip) * 2 + core},
            ).start()
            return carry

        lax.fori_loop(1, n_chip, one, 0)

    def forward_copy(n, which):
        part = kv.at[core, :, :, part_cols(n)]
        return remote(part, kv.at[which, :, :, part_cols(n)], fsend.at[n], frecv.at[n], sibling)

    def arrive(n):
        part = kv.at[core, pl.ds(0, n_chip - 1), :, part_cols(n)]
        remote(part, part, gsend.at[n], grecv.at[n], sibling).wait_recv()
        forward_copy(n, core).start()

    issue(0)
    issue(1)

    ld_dmap.wait()
    ld_tokens.wait()
    down_t = nt(dmap[...], tokens[...]).astype(bf16)
    down = down_t.astype(f32).T.astype(bf16)
    ld_lens.wait()
    len0 = lens[0, 0]
    len1 = lens[0, 1]
    lane = iota((RANK, HD), 1)
    t_of = lax.rem(lane, STEP)
    sign = jnp.where(
        lane < STEP,
        jnp.where(t_of < len0, -1.0, 0.0),
        jnp.where(t_of < len1, 1.0, 0.0),
    ).astype(f32)
    down_signed = (down_t.astype(f32) * sign).astype(bf16)

    ld_plen.wait()
    ld_mask.wait()
    limit = plen[0]
    for b in range(n_cont):
        block = 2 * (b % n_chip) + b // n_chip
        inside = block * BLOCK < limit
        fill = [jnp.where((mask[c, block] > 0) & inside, 0.0, NEG) for c in range(2)]
        col = iota((BLOCK, HD), 1)
        seen[pl.ds(b * BLOCK, BLOCK), :] = jnp.where(
            col == 0, fill[0], jnp.where(col == 1, fill[1], 0.0)
        ).astype(bf16)
    causal = jnp.where(iota((STEP, HD), 0) > lax.rem(iota((STEP, HD), 1), STEP), NEG, 0.0).astype(f32)
    causal = jnp.concatenate([causal] * (HALF // HD), axis=1)

    ld_sv.wait()
    rvs[...] = rv_of(sv[...])
    step_parts = parts_of(rvs[...]).astype(f32)
    for c in range(2):
        rvst[c] = step_parts[c * STEP : (c + 1) * STEP].T.astype(bf16)
    issue(2)
    ld_fq.wait()
    ld_up.wait()
    ld_sk.wait()

    def prepare(g, carry):
        col = pl.multiple_of(g * GCOL, GCOL)
        frozen = fq[:, pl.ds(col, GCOL)].astype(f32) * (FACTOR * LOG2E)
        change = nn(down, up[:, pl.ds(col, GCOL)]) * (ADAPTER_SCALE * FACTOR * LOG2E)
        for s, q in enumerate(((frozen + change).astype(bf16), frozen.astype(bf16))):
            for c in range(2):
                rows = slice(c * STEP, (c + 1) * STEP)
                for h in range(0, HPG, 2):
                    pair = [q[rows, (h + i) * HD : (h + i + 1) * HD] for i in range(2)]
                    at = c * LANES + h * STEP
                    qt[s, g, :, at : at + HD] = jnp.concatenate(pair, axis=0).T
        return carry

    lax.fori_loop(0, KVH, prepare, 0)
    issue(3)
    for c in range(2):
        picks[c] = (iota((HD, HALF), 0) == c).astype(f32).astype(bf16)

    def up_copy(p):
        cols = pl.ds(pl.multiple_of(p * width, 128), width)
        return remote(ubuf.at[:, cols], ru.at[me], usend.at[0], urecv.at[0], plane_dev(p))

    units = [(c, j) for j in range(2) for c in range(2)]

    def stage_a(g, u, slot):
        c, j = units[u]
        kp = kv[:, :, :, block_cols(g + 1)].reshape(prefix, HD)
        ks = sk[pl.ds(c * STEP, STEP), block_cols(g)]
        at = c * LANES + j * HALF
        for s in range(2):
            q = qt[s, g, :, at : at + HALF]
            s_p = nn(jnp.concatenate([kp, seen[...]], axis=1), jnp.concatenate([q, picks[c]], axis=0))
            s_s = nn(ks, q) + causal
            sbuf[slot, s, pl.ds(0, prefix), :] = s_p
            sbuf[slot, s, pl.ds(prefix, STEP), :] = s_s
            mbuf[slot, s] = jnp.maximum(
                jnp.max(s_p, axis=0, keepdims=True), jnp.max(s_s, axis=0, keepdims=True)
            )

    def expand(rows, g, j):
        parts = []
        for i in range(2):
            index = g * (2 * HPG) + 4 * j + 2 * i + iota(rows.shape, 1) // STEP
            parts.append(jnp.take_along_axis(rows, index, axis=1))
        return jnp.concatenate(parts, axis=1)

    def weights(slot, s):
        peak = mbuf[slot, s]
        e_p = jnp.exp2(sbuf[slot, s, pl.ds(0, prefix), :] - peak)
        e_s = jnp.exp2(sbuf[slot, s, pl.ds(prefix, STEP), :] - peak)
        return e_p, e_s

    def stage_b(g, u, slot):
        c, j = units[u]
        rv_p = rvx[j]
        rv_s = expand(rvs[pl.ds(c * STEP, STEP), :], g, j)
        e_p, e_s = weights(slot, 0)
        total = jnp.sum(e_p, axis=0, keepdims=True) + jnp.sum(e_s, axis=0, keepdims=True)
        o = jnp.sum(e_p * rv_p, axis=0, keepdims=True) + jnp.sum(e_s * rv_s, axis=0, keepdims=True)
        inverse = 1.0 / total
        o = o * inverse
        ds_p = (e_p * (rv_p - o)).astype(bf16)
        ds_s = (e_s * (rv_s - o)).astype(bf16)
        e_p, e_s = weights(slot, 1)
        own = pl.ds(pl.multiple_of(g * 16, 16), 16)
        sums = nn(jnp.concatenate([rvt[own, :], jnp.ones((16, prefix), bf16)], axis=0), e_p.astype(bf16))
        sums = sums + nn(
            jnp.concatenate([rvst[c, own, :], jnp.ones((16, STEP), bf16)], axis=0), e_s.astype(bf16)
        )
        shape = (16, HALF)
        mine = lax.rem(iota(shape, 0), HPG) == 4 * j + iota(shape, 1) // STEP
        o_ref = jnp.sum(jnp.where(mine, sums[0:16], 0.0), axis=0, keepdims=True) / sums[16:17]
        return ds_p, ds_s, inverse * FACTOR, o - o_ref

    def stage_c(g, u, kp_t, ds_p, ds_s, scale):
        c, j = units[u]
        ks_t = sk[pl.ds(c * STEP, STEP), block_cols(g)].T
        dq = ((nn(kp_t, ds_p) + nn(ks_t, ds_s)) * scale).astype(bf16)
        for i in range(2):
            h = 4 * j + 2 * i
            nat = dq[:, i * HD : (i + 1) * HD].T
            for k in range(2):
                gbuf[pl.ds(c * STEP, STEP), (h + k) * HD : (h + k + 1) * HD] = nat[
                    k * STEP : (k + 1) * STEP
                ]

    def tail(g, dd):
        col = pl.multiple_of(g * GCOL, GCOL)
        gq = gbuf[...]
        ubuf[:, pl.ds(col, GCOL)] = nn(down_signed, gq).astype(bf16)
        return dd + nt(up[:, pl.ds(col, GCOL)], gq)

    def send_up(g):
        for i in range(dests):
            p = g * dests + i

            @pl.when(p != me)
            def _(p=p):
                up_copy(p).start()

    def group_body(g, carry, first):
        accs = list(carry[:4])
        following = jnp.minimum(g + 1, KVH - 1)
        dd = carry[4] if first else tail(g - 1, carry[4])
        kp_t = kv[:, :, :, block_cols(g + 1)].reshape(prefix, HD).T
        for u in range(4):
            if u == 1:
                rvx[1] = expand(rvf[...], g, 1)
            if u == 3:
                rvx[0] = expand(rvf[...], following, 0)
            if u < 3:
                stage_a(g, u + 1, (u + 1) % 2)
            else:
                if first:
                    forward_copy(1, 1 - core).wait_recv()
                stage_a(following, 0, 0)
            ds_p, ds_s, scale, diff = stage_b(g, u, u % 2)
            accs[u] = accs[u] + diff
            stage_c(g, u, kp_t, ds_p, ds_s, scale)
        return (*accs, dd)

    def group_step(g, carry):
        @pl.when(g == 3)
        def _():
            arrive(3)

        @pl.when(g == 4)
        def _():
            forward_copy(3, 1 - core).wait_recv()

        @pl.when(g >= 2)
        def _():
            send_up(g - 2)

        return group_body(g, carry, False)

    arrive(0)
    forward_copy(0, 1 - core).wait_recv()
    projected = kv[:, :, :, 0:HD].reshape(prefix, HD)
    rvt[...] = projected.T
    projected = projected.astype(f32)
    rvf[...] = projected + pltpu.roll(projected, HD - HPG, 1)
    rvx[0] = expand(rvf[...], 0, 0)

    gbuf[...] = jnp.zeros_like(gbuf)
    stage_a(0, 0, 0)
    zero_acc = jnp.zeros((1, HALF), f32)
    arrive(1)
    carry = group_body(0, (zero_acc,) * 4 + (jnp.zeros((RANK, HD), f32),), True)
    arrive(2)
    forward_copy(2, 1 - core).wait_recv()
    carry = lax.fori_loop(1, KVH, group_step, carry)
    send_up(KVH - 2)
    dd = tail(KVH - 1, carry[4])
    send_up(KVH - 1)

    tl = lax.rem(iota((1, HALF), 1), STEP)
    m0 = jnp.sum(jnp.where(tl < len0, carry[0] + carry[2], 0.0), axis=1, keepdims=True)
    m1 = jnp.sum(jnp.where(tl < len1, carry[1] + carry[3], 0.0), axis=1, keepdims=True)
    zv = BETA * (m0 - m1)
    small = jnp.exp(-jnp.abs(zv))
    loss = jnp.maximum(-zv, 0.0) + jnp.log1p(small)
    weight = (BETA * LOSS_SCALE) * jnp.where(zv >= 0.0, small, 1.0) / (1.0 + small)

    dd = (ADAPTER_SCALE * dd * sign).astype(bf16)
    for i in range(KVH):
        cols = pl.ds(i * GCOL, GCOL)
        dbuf[:, cols] = (nn(dd, tokens[:, cols]) * weight).astype(bf16)

    def start_down(k, carry):
        p = lax.rem(me + k, n_plane)
        cols = pl.ds(pl.multiple_of(p * width, 128), width)
        remote(dbuf.at[:, cols], rdn.at[me], dsend.at[0], drecv.at[0], plane_dev(p)).start()
        return carry

    lax.fori_loop(1, n_plane, start_down, 0)

    notes[me] = jnp.where(iota((2, HD), 0) == 0, loss, weight)

    def start_note(k, carry):
        to = plane_dev(lax.rem(me + k, n_plane))
        remote(notes.at[me], notes.at[me], nsend.at[0], nrecv.at[0], to).start()
        return carry

    lax.fori_loop(1, n_plane, start_note, 0)

    my_cols = pl.ds(pl.multiple_of(me * width, 128), width)

    def z_start(buf, send, recv):
        for k in range(1, n_z):
            remote(buf.at[zi], buf.at[zi], send, recv, z_dev(lax.rem(zi + k, n_z))).start()

    def z_end(buf, send, recv):
        others = buf.at[pl.ds(0, n_z - 1)]
        remote(others, others, send, recv, sibling).wait_recv()
        out = buf[0].astype(f32)
        for z in range(1, n_z):
            out = out + buf[z].astype(f32)
        return out

    def all_start(row, send, recv):
        part = grads.at[pl.ds(row, RANK), my_cols]

        def one(k, carry):
            to = plane_dev(core * n_half + lax.rem(place + k, n_half))
            remote(part, part, send, recv, to).start()
            return carry

        lax.fori_loop(1, n_half, one, 0)

    def half_of(row, which):
        return grads.at[
            pl.ds(row, RANK), pl.ds(pl.multiple_of(which * n_half * width, 128), n_half * width)
        ]

    def all_forward(row, recv, send, to_sibling):
        others = grads.at[pl.ds(row, RANK), pl.ds(0, (n_half - 1) * width)]
        remote(others, others, send, recv, sibling).wait_recv()
        remote(half_of(row, core), half_of(row, core), send, to_sibling, sibling).start()

    def all_end(row, send, to_sibling):
        remote(half_of(row, core), half_of(row, 1 - core), send, to_sibling, sibling).wait_recv()

    def weighted(p):
        return jnp.concatenate([notes[p][1:2]] * (width // HD), axis=1) * ru[p].astype(f32)

    others = rdn.at[pl.ds(0, n_plane - 1)]
    remote(others, others, dsend.at[0], drecv.at[0], sibling).wait_recv()
    rdn[me] = dbuf[:, my_cols]
    acc = rdn[0].astype(f32)
    for p in range(1, n_plane):
        acc = acc + rdn[p].astype(f32)
    zd[zi] = acc.astype(bf16)
    z_start(zd, zdsend.at[0], zdrecv.at[0])

    others = notes.at[pl.ds(0, n_plane - 1)]
    remote(others, others, nsend.at[0], nrecv.at[0], sibling).wait_recv()
    others = ru.at[pl.ds(0, n_plane - 1)]
    remote(others, others, usend.at[0], urecv.at[0], sibling).wait_recv()
    ru[me] = ubuf[:, my_cols]
    acc = weighted(0)
    for p in range(1, n_plane):
        acc = acc + weighted(p)
    zu[zi] = (ADAPTER_SCALE * acc).astype(bf16)
    z_start(zu, zusend.at[0], zurecv.at[0])

    loss_sum = notes[0][0:1]
    for p in range(1, n_plane):
        loss_sum = loss_sum + notes[p][0:1]
    znotes[zi] = loss_sum
    z_start(znotes, znsend.at[0], znrecv.at[0])

    grads[pl.ds(RANK, RANK), my_cols] = z_end(zd, zdsend.at[0], zdrecv.at[0]).astype(bf16)
    all_start(RANK, adsend.at[0], adrecv.at[0])
    grads[pl.ds(0, RANK), my_cols] = z_end(zu, zusend.at[0], zurecv.at[0]).astype(bf16)
    all_start(0, ausend.at[0], aurecv.at[0])
    loss_out[...] = z_end(znotes, znsend.at[0], znrecv.at[0])

    all_forward(RANK, adrecv.at[0], sdsend.at[0], sdrecv.at[0])

    def sent(ref, sem):
        remote(ref, ref, sem, sem, sibling).wait_send()

    for n in range(n_parts):
        sent(kv.at[core, pl.ds(0, n_chip - 1), :, part_cols(n)], gsend.at[n])
        sent(kv.at[core, :, :, part_cols(n)], fsend.at[n])
    sent(ru.at[pl.ds(0, n_plane - 1)], usend.at[0])
    sent(rdn.at[pl.ds(0, n_plane - 1)], dsend.at[0])
    sent(notes.at[pl.ds(0, n_plane - 1)], nsend.at[0])
    sent(zu.at[pl.ds(0, n_z - 1)], zusend.at[0])
    sent(zd.at[pl.ds(0, n_z - 1)], zdsend.at[0])
    sent(znotes.at[pl.ds(0, n_z - 1)], znsend.at[0])

    all_forward(0, aurecv.at[0], susend.at[0], surecv.at[0])
    for row, sem in ((0, ausend), (RANK, adsend)):
        sent(grads.at[pl.ds(row, RANK), pl.ds(0, (n_half - 1) * width)], sem.at[0])
    all_end(0, susend.at[0], surecv.at[0])
    all_end(RANK, sdsend.at[0], sdrecv.at[0])
    sent(half_of(0, core), susend.at[0])
    sent(half_of(RANK, core), sdsend.at[0])


def local(n_cont, n_z, tokens, fq, sk, sv, kshard, vshard, dmap, up, readout, lens, plen, mask):
    n_plane = 2 * n_cont
    n_chip = n_cont // 2
    width = FEATURES // n_plane
    rows = tokens.shape[0]
    prefix = BLOCK * n_cont
    cols = HD + KVH * HD
    anyspec = pl.BlockSpec(memory_space=pl.ANY)
    vspec = pl.BlockSpec(memory_space=pltpu.VMEM)
    dma = pltpu.SemaphoreType.DMA
    grads, loss = pl.pallas_call(
        functools.partial(kernel, (n_cont, n_z)),
        out_shape=(
            jax.ShapeDtypeStruct((2 * RANK, FEATURES), bf16),
            jax.ShapeDtypeStruct((1, 128), f32),
        ),
        in_specs=[anyspec] * 12,
        out_specs=(vspec, vspec),
        scratch_shapes=[
            pltpu.VMEM((rows, FEATURES), bf16),
            pltpu.VMEM((rows, FEATURES), bf16),
            pltpu.VMEM((rows, KVH * HD), bf16),
            pltpu.VMEM((rows, KVH * HD), bf16),
            pltpu.VMEM((RANK, FEATURES), bf16),
            pltpu.VMEM((RANK, FEATURES), bf16),
            pltpu.VMEM((BLOCK, KVH * HD), bf16),
            pltpu.VMEM((HQ, HD), bf16),
            pltpu.SMEM((1, 2), jnp.int32),
            pltpu.SMEM((1,), jnp.int32),
            pltpu.SMEM((2, n_cont), jnp.int32),
            pltpu.VMEM((2, n_chip, BLOCK, cols), bf16),
            pltpu.VMEM((BLOCK, cols), bf16),
            pltpu.VMEM((RANK, FEATURES), bf16),
            pltpu.VMEM((RANK, FEATURES), bf16),
            pltpu.VMEM((n_plane, RANK, width), bf16),
            pltpu.VMEM((n_plane, RANK, width), bf16),
            pltpu.VMEM((n_z, RANK, width), bf16),
            pltpu.VMEM((n_z, RANK, width), bf16),
            pltpu.VMEM((2, KVH, HD, 2 * LANES), bf16),
            pltpu.VMEM((prefix, HD), bf16),
            pltpu.VMEM((2, HD, HALF), bf16),
            pltpu.VMEM((prefix, HD), f32),
            pltpu.VMEM((HD, prefix), bf16),
            pltpu.VMEM((rows, HD), f32),
            pltpu.VMEM((2, HD, STEP), bf16),
            pltpu.VMEM((2, prefix, HALF), f32),
            pltpu.VMEM((2, 2, prefix + STEP, HALF), f32),
            pltpu.VMEM((2, 2, 1, HALF), f32),
            pltpu.VMEM((rows, GCOL), bf16),
            pltpu.VMEM((n_plane, 2, 128), f32),
            pltpu.VMEM((n_z, 1, 128), f32),
            dma((12,)),
            *[dma((4,))] * 4,
            *[dma((1,))] * 20,
        ],
        compiler_params=pltpu.CompilerParams(
            collective_id=0, has_side_effects=True, vmem_limit_bytes=60 * 1024 * 1024
        ),
    )(tokens, fq, sk, sv, kshard, vshard, dmap, up, readout.reshape(HQ, HD), lens, plen, mask)
    return loss[0, 0], grads[RANK:].astype(f32), grads[0:RANK].astype(f32)


def solution(mesh):
    return jax.shard_map(
        functools.partial(local, mesh.shape["cont"], mesh.shape["dp"] // 2),
        mesh=mesh,
        in_specs=(
            P(("dp", "cont"), None),
            P(("dp", "cont"), None),
            P(("dp", "cont"), None),
            P(("dp", "cont"), None),
            P(("dp", "cont"), None),
            P(("dp", "cont"), None),
            P(),
            P(),
            P(),
            P(("dp", "cont"), None),
            P("dp"),
            P(("dp", "cont"), None),
        ),
        out_specs=(P(), P(), P()),
        check_vma=False,
    )
```

```python
import functools

import jax
import jax.numpy as jnp
from jax import lax
from jax.experimental import pallas as pl
from jax.experimental.pallas import tpu as pltpu
from jax.sharding import PartitionSpec as P

HQ = 64
KVH = 8
HD = 128
HPG = HQ // KVH
BLOCK = 32
STEP = 64
RANK = 16
FEATURES = 8192
GCOL = HPG * HD
LANES = HPG * STEP
HALF = LANES // 2
MASK = 16

NEG = -1e30
BETA = 0.1
ADAPTER_SCALE = 2.0
LOSS_SCALE = 1024.0
FACTOR = HD**-0.5
LOG2E = 1.4426950408889634

MESH = pl.DeviceIdType.MESH
f32 = jnp.float32
bf16 = jnp.bfloat16


def nn(a, b):
    return lax.dot_general(a, b, (((1,), (0,)), ((), ())), preferred_element_type=f32)


def nt(a, b):
    return lax.dot_general(a, b, (((1,), (1,)), ((), ())), preferred_element_type=f32)


def iota(shape, dim):
    return lax.broadcasted_iota(jnp.int32, shape, dim)


def kernel(
    dims,
    tokens_hbm, fq_hbm, sk_hbm, sv_hbm, ks_hbm, vs_hbm, dmap_hbm, up_hbm, rd_hbm,
    lens_hbm, plen_hbm, mask_hbm,
    grads, loss_out,
    tokens, fq, sk, sv, dmap, up, vshard, rd, lens, plen, mask,
    kv, shard, ubuf, dbuf, ru, rdn, zu, zd, qt, seen, picks, rvf, rvt, rvs, rvst, rvx, sbuf, mbuf, gbuf, dsib, dsum, ushare, lpair, notes, znotes,
    local_sem, gsend, grecv, fsend, frecv, usend, urecv, dsend, drecv, nsend, nrecv,
    zusend, zurecv, zdsend, zdrecv, znsend, znrecv, ausend, aurecv, adsend, adrecv,
    susend, surecv, sdsend, sdrecv, xsend, xrecv, gvsend, gvrecv, tlsend, tlrecv,
):
    n_cont, n_z = dims
    n_plane = 2 * n_cont
    n_chip = n_cont // 2
    prefix = BLOCK * n_cont
    width = FEATURES // n_plane
    dests = n_plane // KVH
    n_half = n_plane // 2
    dp = lax.axis_index("dp")
    cont = lax.axis_index("cont")
    core = lax.rem(cont, 2)
    chip = cont // 2
    zi = dp // 2
    xlo = lax.rem(dp, 2)
    place = xlo * n_chip + chip
    me = core * n_half + place

    def plane_dev(p):
        r = lax.rem(p, n_half)
        return {"dp": zi * 2 + r // n_chip, "cont": lax.rem(r, n_chip) * 2 + p // n_half}

    sibling = {"cont": chip * 2 + (1 - core)}

    def remote(src, dst, send, recv, to):
        return pltpu.make_async_remote_copy(
            src_ref=src, dst_ref=dst, send_sem=send, recv_sem=recv, device_id=to, device_id_type=MESH
        )

    def z_dev(z):
        return {"dp": z * 2 + xlo, "cont": cont}

    barrier = pltpu.get_barrier_semaphore()

    def peer(k):
        return plane_dev(core * n_half + lax.rem(place + k, n_half))

    def greet(to):
        pl.semaphore_signal(barrier, inc=1, device_id=to, device_id_type=MESH)

    def greet_peer(k, carry):
        greet(peer(k))
        return carry

    def greet_z(k, carry):
        greet(z_dev(lax.rem(zi + k, n_z)))
        return carry

    lax.fori_loop(1, n_half, greet_peer, 0)
    lax.fori_loop(1, n_z, greet_z, 0)
    greet(sibling)

    loads = []
    for i, (src, dst) in enumerate(
        (
            (vs_hbm, vshard),
            (rd_hbm, rd),
            (ks_hbm, shard.at[:, HD:]),
            (dmap_hbm, dmap),
            (tokens_hbm, tokens),
            (sv_hbm, sv),
            (lens_hbm, lens),
            (plen_hbm, plen),
            (mask_hbm, mask),
            (fq_hbm, fq),
            (up_hbm, up),
            (sk_hbm, sk),
        )
    ):
        cp = pltpu.make_async_copy(src, dst, local_sem.at[i])
        cp.start()
        loads.append(cp)
    ld_vs, ld_rd, ld_ks, ld_dmap, ld_tokens, ld_sv, ld_lens, ld_plen, ld_mask, ld_fq, ld_up, ld_sk = loads

    ld_vs.wait()
    ld_rd.wait()
    rdf = rd[...].astype(f32)
    rd2 = jnp.concatenate(
        [rdf[(i // 2) * HPG : (i // 2 + 1) * HPG] for i in range(2 * KVH)], axis=0
    ).astype(bf16)
    row_g = iota((HD, HD), 0) // (2 * HPG)

    def rv_of(values):
        total = None
        for g in range(KVH):
            w = jnp.where(row_g == g, rd2, jnp.zeros_like(rd2))
            part = nt(values[:, g * HD : (g + 1) * HD], w)
            total = part if total is None else total + part
        return total

    def parts_of(x):
        high = x.astype(bf16).astype(f32)
        return jnp.where(lax.rem(iota(x.shape, 1) // HPG, 2) == 0, high, x - high).astype(bf16)

    shard[:, 0:HD] = parts_of(rv_of(vshard[...]))
    ld_ks.wait()
    kv[core, chip] = shard[...]

    pl.semaphore_wait(barrier, n_half - 1 + n_z - 1 + 1)

    part_at = (0, 2, 3, 6, 9)
    n_parts = len(part_at) - 1

    def part_cols(n):
        return pl.ds(part_at[n] * HD, (part_at[n + 1] - part_at[n]) * HD)

    def block_cols(n):
        return pl.ds(pl.multiple_of(n * HD, HD), HD)

    def issue(n):
        def one(k, carry):
            remote(
                shard.at[:, part_cols(n)],
                kv.at[core, chip, :, part_cols(n)],
                gsend.at[n],
                grecv.at[n],
                {"cont": lax.rem(chip + k, n_chip) * 2 + core},
            ).start()
            return carry

        lax.fori_loop(1, n_chip, one, 0)

    def forward_copy(n, which):
        part = kv.at[core, :, :, part_cols(n)]
        return remote(part, kv.at[which, :, :, part_cols(n)], fsend.at[n], frecv.at[n], sibling)

    def arrive(n):
        part = kv.at[core, pl.ds(0, n_chip - 1), :, part_cols(n)]
        remote(part, part, gsend.at[n], grecv.at[n], sibling).wait_recv()
        forward_copy(n, core).start()

    issue(0)
    issue(1)

    ld_dmap.wait()
    ld_tokens.wait()
    down_t = nt(dmap[...], tokens[...]).astype(bf16)
    down = down_t.astype(f32).T.astype(bf16)
    ld_lens.wait()
    len0 = lens[0, 0]
    len1 = lens[0, 1]
    lane = iota((RANK, HD), 1)
    t_of = lax.rem(lane, STEP)
    sign = jnp.where(
        lane < STEP,
        jnp.where(t_of < len0, -1.0, 0.0),
        jnp.where(t_of < len1, 1.0, 0.0),
    ).astype(f32)
    down_signed = (down_t.astype(f32) * sign).astype(bf16)

    ld_plen.wait()
    ld_mask.wait()
    limit = plen[0]
    seen[pl.ds(prefix, STEP), :] = jnp.zeros((STEP, MASK), bf16)
    for b in range(n_cont):
        block = 2 * (b % n_chip) + b // n_chip
        inside = block * BLOCK < limit
        fill = [jnp.where((mask[c, block] > 0) & inside, 0.0, NEG) for c in range(2)]
        col = iota((BLOCK, MASK), 1)
        seen[pl.ds(b * BLOCK, BLOCK), :] = jnp.where(
            col == 0, fill[0], jnp.where(col == 1, fill[1], 0.0)
        ).astype(bf16)
    causal = jnp.where(iota((STEP, HD), 0) > lax.rem(iota((STEP, HD), 1), STEP), NEG, 0.0).astype(f32)
    causal = jnp.concatenate([causal] * (HALF // HD), axis=1)

    ld_sv.wait()
    rvs[...] = rv_of(sv[...])
    step_parts = parts_of(rvs[...]).astype(f32)
    for c in range(2):
        rvst[c] = step_parts[c * STEP : (c + 1) * STEP].T.astype(bf16)
    issue(2)
    ld_fq.wait()
    ld_up.wait()
    ld_sk.wait()

    def prepare(g, carry):
        col = pl.multiple_of(g * GCOL, GCOL)
        frozen = fq[:, pl.ds(col, GCOL)].astype(f32) * (FACTOR * LOG2E)
        change = nn(down, up[:, pl.ds(col, GCOL)]) * (ADAPTER_SCALE * FACTOR * LOG2E)
        for s, q in enumerate(((frozen + change).astype(bf16), frozen.astype(bf16))):
            for c in range(2):
                rows = slice(c * STEP, (c + 1) * STEP)
                for h in range(0, HPG, 2):
                    pair = [q[rows, (h + i) * HD : (h + i + 1) * HD] for i in range(2)]
                    at = c * LANES + h * STEP
                    qt[s, g, :, at : at + HD] = jnp.concatenate(pair, axis=0).T
        return carry

    lax.fori_loop(0, KVH, prepare, 0)
    issue(3)
    for c in range(2):
        picks[c] = (iota((MASK, HALF), 0) == c).astype(f32).astype(bf16)

    units = [(c, j) for j in range(2) for c in range(2)]

    def stage_a(g, u, slot):
        c, j = units[u]
        kp = kv[:, :, :, block_cols(g + 1)].reshape(prefix, HD)
        ks = sk[pl.ds(c * STEP, STEP), block_cols(g)]
        at = c * LANES + j * HALF
        keys = jnp.concatenate([jnp.concatenate([kp, ks], axis=0), seen[...]], axis=1)
        for s in range(2):
            q = qt[s, g, :, at : at + HALF]
            scores = nn(keys, jnp.concatenate([q, picks[c]], axis=0))
            s_p = scores[0:prefix]
            s_s = scores[prefix:] + causal
            sbuf[slot, s, pl.ds(0, prefix), :] = s_p
            sbuf[slot, s, pl.ds(prefix, STEP), :] = s_s
            mbuf[slot, s] = jnp.maximum(
                jnp.max(s_p, axis=0, keepdims=True), jnp.max(s_s, axis=0, keepdims=True)
            )

    def expand(rows, g, j):
        parts = []
        for i in range(2):
            index = g * (2 * HPG) + 4 * j + 2 * i + iota(rows.shape, 1) // STEP
            parts.append(jnp.take_along_axis(rows, index, axis=1))
        return jnp.concatenate(parts, axis=1)

    def weights(slot, s):
        peak = mbuf[slot, s]
        e_p = jnp.exp2(sbuf[slot, s, pl.ds(0, prefix), :] - peak)
        e_s = jnp.exp2(sbuf[slot, s, pl.ds(prefix, STEP), :] - peak)
        return e_p, e_s

    def stage_b(g, u, slot):
        c, j = units[u]
        rv_p = rvx[j]
        rv_s = expand(rvs[pl.ds(c * STEP, STEP), :], g, j)
        e_p, e_s = weights(slot, 0)
        total = jnp.sum(e_p, axis=0, keepdims=True) + jnp.sum(e_s, axis=0, keepdims=True)
        o = jnp.sum(e_p * rv_p, axis=0, keepdims=True) + jnp.sum(e_s * rv_s, axis=0, keepdims=True)
        inverse = 1.0 / total
        o = o * inverse
        ds_p = (e_p * (rv_p - o)).astype(bf16)
        ds_s = (e_s * (rv_s - o)).astype(bf16)
        e_p, e_s = weights(slot, 1)
        own = pl.ds(pl.multiple_of(g * 16, 16), 16)
        sums = nn(jnp.concatenate([rvt[own, :], jnp.ones((16, prefix), bf16)], axis=0), e_p.astype(bf16))
        sums = sums + nn(
            jnp.concatenate([rvst[c, own, :], jnp.ones((16, STEP), bf16)], axis=0), e_s.astype(bf16)
        )
        shape = (16, HALF)
        mine = lax.rem(iota(shape, 0), HPG) == 4 * j + iota(shape, 1) // STEP
        o_ref = jnp.sum(jnp.where(mine, sums[0:16], 0.0), axis=0, keepdims=True) / sums[16:17]
        return ds_p, ds_s, inverse * FACTOR, o - o_ref

    def stage_c(g, u, kp_t, ds_p, ds_s, scale):
        c, j = units[u]
        ks_t = sk[pl.ds(c * STEP, STEP), block_cols(g)].T
        dq = ((nn(kp_t, ds_p) + nn(ks_t, ds_s)) * scale).astype(bf16)
        for i in range(2):
            h = 4 * j + 2 * i
            nat = dq[:, i * HD : (i + 1) * HD].T
            for k in range(2):
                gbuf[pl.ds(c * STEP, STEP), (h + k) * HD : (h + k + 1) * HD] = nat[
                    k * STEP : (k + 1) * STEP
                ]

    def tail(g, dd):
        col = pl.multiple_of(g * GCOL, GCOL)
        gq = gbuf[...]
        ubuf[:, pl.ds(col, GCOL)] = nn(down_signed, gq).astype(bf16)
        return dd + nt(up[:, pl.ds(col, GCOL)], gq)

    def send_up(g):
        for i in range(dests):
            p = g * dests + i
            r = lax.rem(p, n_half)

            @pl.when(r != place)
            def _(p=p, r=r):
                cols = pl.ds(pl.multiple_of(p * width, 128), width)
                to = plane_dev(core * n_half + r)
                remote(ubuf.at[:, cols], ru.at[p // n_half, place], usend.at[0], urecv.at[0], to).start()

    def group_body(g, carry, peeled=None):
        accs = list(carry[:4])
        following = jnp.minimum(g + 1, KVH - 1)
        dd = carry[4] if peeled == 0 else tail(g - 1, carry[4])
        kp_t = kv[:, :, :, block_cols(g + 1)].reshape(prefix, HD).T
        for u in range(4):
            if u == 1:
                rvx[1] = expand(rvf[...], g, 1)
            if u == 3:
                rvx[0] = expand(rvf[...], following, 0)
            if u < 3:
                stage_a(g, u + 1, (u + 1) % 2)
            else:
                if peeled is not None:
                    forward_copy(peeled + 1, 1 - core).wait_recv()
                if peeled == 0:
                    arrive(2)
                stage_a(following, 0, 0)
            ds_p, ds_s, scale, diff = stage_b(g, u, u % 2)
            accs[u] = accs[u] + diff
            stage_c(g, u, kp_t, ds_p, ds_s, scale)
        return (*accs, dd)

    def group_step(g, carry):
        @pl.when(g == 3)
        def _():
            arrive(3)

        @pl.when(g == 4)
        def _():
            forward_copy(3, 1 - core).wait_recv()

        send_up(g - 2)
        return group_body(g, carry)

    arrive(0)
    forward_copy(0, 1 - core).wait_recv()
    projected = kv[:, :, :, 0:HD].reshape(prefix, HD)
    rvt[...] = projected.T
    projected = projected.astype(f32)
    rvf[...] = projected + pltpu.roll(projected, HD - HPG, 1)
    rvx[0] = expand(rvf[...], 0, 0)

    gbuf[...] = jnp.zeros_like(gbuf)
    stage_a(0, 0, 0)
    zero_acc = jnp.zeros((1, HALF), f32)
    arrive(1)
    carry = group_body(0, (zero_acc,) * 4 + (jnp.zeros((RANK, HD), f32),), 0)
    carry = group_body(1, carry, 1)
    carry = lax.fori_loop(2, KVH, group_step, carry)
    send_up(KVH - 2)
    dd = tail(KVH - 1, carry[4])
    send_up(KVH - 1)

    tl = lax.rem(iota((1, HALF), 1), STEP)
    m0 = jnp.sum(jnp.where(tl < len0, carry[0] + carry[2], 0.0), axis=1, keepdims=True)
    m1 = jnp.sum(jnp.where(tl < len1, carry[1] + carry[3], 0.0), axis=1, keepdims=True)
    zv = BETA * (m0 - m1)
    small = jnp.exp(-jnp.abs(zv))
    loss = jnp.maximum(-zv, 0.0) + jnp.log1p(small)
    weight = (BETA * LOSS_SCALE) * jnp.where(zv >= 0.0, small, 1.0) / (1.0 + small)

    dd = (ADAPTER_SCALE * dd * sign).astype(bf16)
    for i in range(KVH):
        cols = pl.ds(i * GCOL, GCOL)
        dbuf[:, cols] = (nn(dd, tokens[:, cols]) * weight).astype(bf16)

    def side(which):
        return pl.ds(pl.multiple_of(which * n_half * width, 128), n_half * width)

    def cols_of(p):
        return pl.ds(pl.multiple_of(p * width, 128), width)

    swap = remote(dbuf.at[:, side(1 - core)], dsib, xsend.at[0], xrecv.at[0], sibling)
    swap.start()

    notes[place] = jnp.where(iota((2, HD), 0) == 0, loss, weight)

    def start_note(k, carry):
        remote(notes.at[place], notes.at[place], nsend.at[0], nrecv.at[0], peer(k)).start()
        return carry

    lax.fori_loop(1, n_half, start_note, 0)
    for h in range(2):
        ru[h, place] = ubuf[:, cols_of(h * n_half + place)]

    swap.wait_recv()
    dsum[...] = (dbuf[:, side(core)].astype(f32) + dsib[...].astype(f32)).astype(bf16)

    def start_down(k, carry):
        cols = cols_of(lax.rem(place + k, n_half))
        remote(dsum.at[:, cols], rdn.at[place], dsend.at[0], drecv.at[0], peer(k)).start()
        return carry

    lax.fori_loop(1, n_half, start_down, 0)

    my_cols = pl.ds(pl.multiple_of(me * width, 128), width)

    def z_start(buf, send, recv):
        for k in range(1, n_z):
            remote(buf.at[zi], buf.at[zi], send, recv, z_dev(lax.rem(zi + k, n_z))).start()

    def z_end(buf, send, recv):
        others = buf.at[pl.ds(0, n_z - 1)]
        remote(others, others, send, recv, sibling).wait_recv()
        out = buf[0].astype(f32)
        for z in range(1, n_z):
            out = out + buf[z].astype(f32)
        return out

    def all_start(row, send, recv):
        part = grads.at[pl.ds(row, RANK), my_cols]

        def one(k, carry):
            remote(part, part, send, recv, peer(k)).start()
            return carry

        lax.fori_loop(1, n_half, one, 0)

    def half_of(row, which):
        return grads.at[pl.ds(row, RANK), side(which)]

    def all_forward(row, recv, send, to_sibling):
        others = grads.at[pl.ds(row, RANK), pl.ds(0, (n_half - 1) * width)]
        remote(others, others, send, recv, sibling).wait_recv()
        remote(half_of(row, core), half_of(row, core), send, to_sibling, sibling).start()

    def all_end(row, send, to_sibling):
        remote(half_of(row, core), half_of(row, 1 - core), send, to_sibling, sibling).wait_recv()

    others = notes.at[pl.ds(0, n_half - 1)]
    remote(others, others, nsend.at[0], nrecv.at[0], sibling).wait_recv()
    others = ru.at[:, pl.ds(0, n_half - 1)]
    remote(others, others, usend.at[0], urecv.at[0], sibling).wait_recv()

    def share(h):
        acc = jnp.zeros((RANK, width), f32)
        for r in range(n_half):
            w = jnp.concatenate([notes[r][1:2]] * (width // HD), axis=1)
            acc = acc + w * ru[h, r].astype(f32)
        return acc * ADAPTER_SCALE

    ushare[0] = share(1 - core).astype(bf16)
    loss_sum = notes[0][0:1]
    for r in range(1, n_half):
        loss_sum = loss_sum + notes[r][0:1]
    lpair[core] = loss_sum
    give = remote(ushare.at[0], ushare.at[1], gvsend.at[0], gvrecv.at[0], sibling)
    give.start()
    tell = remote(lpair.at[core], lpair.at[core], tlsend.at[0], tlrecv.at[0], sibling)
    tell.start()
    mine = share(core)

    others = rdn.at[pl.ds(0, n_half - 1)]
    remote(others, others, dsend.at[0], drecv.at[0], sibling).wait_recv()
    rdn[place] = dsum[:, cols_of(place)]
    acc = rdn[0].astype(f32)
    for r in range(1, n_half):
        acc = acc + rdn[r].astype(f32)
    zd[zi] = acc.astype(bf16)
    z_start(zd, zdsend.at[0], zdrecv.at[0])

    give.wait_recv()
    zu[zi] = (mine + ushare[1].astype(f32)).astype(bf16)
    z_start(zu, zusend.at[0], zurecv.at[0])
    tell.wait_recv()
    znotes[zi] = lpair[0] + lpair[1]
    z_start(znotes, znsend.at[0], znrecv.at[0])

    grads[pl.ds(RANK, RANK), my_cols] = z_end(zd, zdsend.at[0], zdrecv.at[0]).astype(bf16)
    all_start(RANK, adsend.at[0], adrecv.at[0])
    grads[pl.ds(0, RANK), my_cols] = z_end(zu, zusend.at[0], zurecv.at[0]).astype(bf16)
    all_start(0, ausend.at[0], aurecv.at[0])
    loss_out[...] = z_end(znotes, znsend.at[0], znrecv.at[0])

    all_forward(RANK, adrecv.at[0], sdsend.at[0], sdrecv.at[0])

    def sent(ref, sem):
        remote(ref, ref, sem, sem, sibling).wait_send()

    for n in range(n_parts):
        sent(kv.at[core, pl.ds(0, n_chip - 1), :, part_cols(n)], gsend.at[n])
        sent(kv.at[core, :, :, part_cols(n)], fsend.at[n])
    sent(ru.at[:, pl.ds(0, n_half - 1)], usend.at[0])
    sent(rdn.at[pl.ds(0, n_half - 1)], dsend.at[0])
    sent(notes.at[pl.ds(0, n_half - 1)], nsend.at[0])
    swap.wait_send()
    give.wait_send()
    tell.wait_send()
    sent(zu.at[pl.ds(0, n_z - 1)], zusend.at[0])
    sent(zd.at[pl.ds(0, n_z - 1)], zdsend.at[0])
    sent(znotes.at[pl.ds(0, n_z - 1)], znsend.at[0])

    all_forward(0, aurecv.at[0], susend.at[0], surecv.at[0])
    for row, sem in ((0, ausend), (RANK, adsend)):
        sent(grads.at[pl.ds(row, RANK), pl.ds(0, (n_half - 1) * width)], sem.at[0])
    all_end(0, susend.at[0], surecv.at[0])
    all_end(RANK, sdsend.at[0], sdrecv.at[0])
    sent(half_of(0, core), susend.at[0])
    sent(half_of(RANK, core), sdsend.at[0])


def local(n_cont, n_z, tokens, fq, sk, sv, kshard, vshard, dmap, up, readout, lens, plen, mask):
    n_plane = 2 * n_cont
    n_half = n_cont
    n_chip = n_cont // 2
    width = FEATURES // n_plane
    rows = tokens.shape[0]
    prefix = BLOCK * n_cont
    cols = HD + KVH * HD
    anyspec = pl.BlockSpec(memory_space=pl.ANY)
    vspec = pl.BlockSpec(memory_space=pltpu.VMEM)
    dma = pltpu.SemaphoreType.DMA
    grads, loss = pl.pallas_call(
        functools.partial(kernel, (n_cont, n_z)),
        out_shape=(
            jax.ShapeDtypeStruct((2 * RANK, FEATURES), bf16),
            jax.ShapeDtypeStruct((1, 128), f32),
        ),
        in_specs=[anyspec] * 12,
        out_specs=(vspec, vspec),
        scratch_shapes=[
            pltpu.VMEM((rows, FEATURES), bf16),
            pltpu.VMEM((rows, FEATURES), bf16),
            pltpu.VMEM((rows, KVH * HD), bf16),
            pltpu.VMEM((rows, KVH * HD), bf16),
            pltpu.VMEM((RANK, FEATURES), bf16),
            pltpu.VMEM((RANK, FEATURES), bf16),
            pltpu.VMEM((BLOCK, KVH * HD), bf16),
            pltpu.VMEM((HQ, HD), bf16),
            pltpu.SMEM((1, 2), jnp.int32),
            pltpu.SMEM((1,), jnp.int32),
            pltpu.SMEM((2, n_cont), jnp.int32),
            pltpu.VMEM((2, n_chip, BLOCK, cols), bf16),
            pltpu.VMEM((BLOCK, cols), bf16),
            pltpu.VMEM((RANK, FEATURES), bf16),
            pltpu.VMEM((RANK, FEATURES), bf16),
            pltpu.VMEM((2, n_half, RANK, width), bf16),
            pltpu.VMEM((n_half, RANK, width), bf16),
            pltpu.VMEM((n_z, RANK, width), bf16),
            pltpu.VMEM((n_z, RANK, width), bf16),
            pltpu.VMEM((2, KVH, HD, 2 * LANES), bf16),
            pltpu.VMEM((prefix + STEP, MASK), bf16),
            pltpu.VMEM((2, MASK, HALF), bf16),
            pltpu.VMEM((prefix, HD), f32),
            pltpu.VMEM((HD, prefix), bf16),
            pltpu.VMEM((rows, HD), f32),
            pltpu.VMEM((2, HD, STEP), bf16),
            pltpu.VMEM((2, prefix, HALF), f32),
            pltpu.VMEM((2, 2, prefix + STEP, HALF), f32),
            pltpu.VMEM((2, 2, 1, HALF), f32),
            pltpu.VMEM((rows, GCOL), bf16),
            pltpu.VMEM((RANK, n_half * width), bf16),
            pltpu.VMEM((RANK, n_half * width), bf16),
            pltpu.VMEM((2, RANK, width), bf16),
            pltpu.VMEM((2, 1, 128), f32),
            pltpu.VMEM((n_half, 2, 128), f32),
            pltpu.VMEM((n_z, 1, 128), f32),
            dma((12,)),
            *[dma((4,))] * 4,
            *[dma((1,))] * 26,
        ],
        compiler_params=pltpu.CompilerParams(
            collective_id=0, has_side_effects=True, vmem_limit_bytes=60 * 1024 * 1024
        ),
    )(tokens, fq, sk, sv, kshard, vshard, dmap, up, readout.reshape(HQ, HD), lens, plen, mask)
    return loss[0, 0], grads[RANK:].astype(f32), grads[0:RANK].astype(f32)


def solution(mesh):
    return jax.shard_map(
        functools.partial(local, mesh.shape["cont"], mesh.shape["dp"] // 2),
        mesh=mesh,
        in_specs=(
            P(("dp", "cont"), None),
            P(("dp", "cont"), None),
            P(("dp", "cont"), None),
            P(("dp", "cont"), None),
            P(("dp", "cont"), None),
            P(("dp", "cont"), None),
            P(),
            P(),
            P(),
            P(("dp", "cont"), None),
            P("dp"),
            P(("dp", "cont"), None),
        ),
        out_specs=(P(), P(), P()),
        check_vma=False,
    )
```

```python
import functools

import jax
import jax.numpy as jnp
from jax import lax
from jax.experimental import pallas as pl
from jax.experimental.pallas import tpu as pltpu
from jax.sharding import PartitionSpec as P

HQ = 64
KVH = 8
HD = 128
HPG = HQ // KVH
BLOCK = 32
STEP = 64
RANK = 16
FEATURES = 8192
GCOL = HPG * HD
LANES = HPG * STEP
HALF = LANES // 2
MASK = 16

NEG = -1e30
BETA = 0.1
ADAPTER_SCALE = 2.0
LOSS_SCALE = 1024.0
FACTOR = HD**-0.5
LOG2E = 1.4426950408889634

MESH = pl.DeviceIdType.MESH
f32 = jnp.float32
bf16 = jnp.bfloat16


def nn(a, b):
    return lax.dot_general(a, b, (((1,), (0,)), ((), ())), preferred_element_type=f32)


def nt(a, b):
    return lax.dot_general(a, b, (((1,), (1,)), ((), ())), preferred_element_type=f32)


def iota(shape, dim):
    return lax.broadcasted_iota(jnp.int32, shape, dim)


def kernel(
    dims,
    tokens_hbm, fq_hbm, sk_hbm, sv_hbm, ks_hbm, vs_hbm, dmap_hbm, up_hbm, rd_hbm,
    lens_hbm, plen_hbm, mask_hbm,
    grads, loss_out,
    tokens, fq, sk, sv, dmap, up, vshard, rd, lens, plen, mask,
    kv, shard, ubuf, dbuf, ru, rdn, zu, zd, qt, seen, picks, rvf, rvt, rvs, rvst, rvx, sbuf, mbuf, gbuf, dsib, dsum, ushare, lpair, notes, znotes,
    local_sem, gsend, grecv, fsend, frecv, usend, urecv, dsend, drecv, nsend, nrecv,
    zusend, zurecv, zdsend, zdrecv, znsend, znrecv, ausend, aurecv, adsend, adrecv,
    susend, surecv, sdsend, sdrecv, xsend, xrecv, gvsend, gvrecv, tlsend, tlrecv,
):
    n_cont, n_z = dims
    n_plane = 2 * n_cont
    n_chip = n_cont // 2
    prefix = BLOCK * n_cont
    width = FEATURES // n_plane
    dests = n_plane // KVH
    n_half = n_plane // 2
    dp = lax.axis_index("dp")
    cont = lax.axis_index("cont")
    core = lax.rem(cont, 2)
    chip = cont // 2
    zi = dp // 2
    xlo = lax.rem(dp, 2)
    place = xlo * n_chip + chip
    me = core * n_half + place

    def plane_dev(p):
        r = lax.rem(p, n_half)
        return {"dp": zi * 2 + r // n_chip, "cont": lax.rem(r, n_chip) * 2 + p // n_half}

    sibling = {"cont": chip * 2 + (1 - core)}

    def remote(src, dst, send, recv, to):
        return pltpu.make_async_remote_copy(
            src_ref=src, dst_ref=dst, send_sem=send, recv_sem=recv, device_id=to, device_id_type=MESH
        )

    def z_dev(z):
        return {"dp": z * 2 + xlo, "cont": cont}

    barrier = pltpu.get_barrier_semaphore()

    n_y = n_chip // 2
    x = 2 * lax.rem(chip, 2) + xlo
    y = chip // 2

    def hops(o):
        return min(o[0], n_y - o[0]) + min(o[1], 4 - o[1])

    plane_offsets = sorted(
        [(oy, ox) for oy in range(n_y) for ox in range(4) if (oy, ox) != (0, 0)], key=hops, reverse=True
    )
    group_offsets = [o for o in plane_offsets if o[1] % 2 == 0]
    z_offsets = sorted(range(1, n_z), key=lambda k: min(k, n_z - k), reverse=True)

    def place_at(o):
        px = lax.rem(x + o[1], 4)
        return lax.rem(px, 2) * n_chip + lax.rem(y + o[0], n_y) * 2 + px // 2

    def device_at(r):
        return plane_dev(core * n_half + r)

    def greet(to):
        pl.semaphore_signal(barrier, inc=1, device_id=to, device_id_type=MESH)

    for k in z_offsets:
        greet(z_dev(lax.rem(zi + k, n_z)))
    for o in plane_offsets:
        greet(device_at(place_at(o)))
    greet(sibling)

    loads = []
    for i, (src, dst) in enumerate(
        (
            (vs_hbm, vshard),
            (rd_hbm, rd),
            (ks_hbm, shard.at[:, HD:]),
            (dmap_hbm, dmap),
            (tokens_hbm, tokens),
            (sv_hbm, sv),
            (lens_hbm, lens),
            (plen_hbm, plen),
            (mask_hbm, mask),
            (fq_hbm, fq),
            (up_hbm, up),
            (sk_hbm, sk),
        )
    ):
        cp = pltpu.make_async_copy(src, dst, local_sem.at[i])
        cp.start()
        loads.append(cp)
    ld_vs, ld_rd, ld_ks, ld_dmap, ld_tokens, ld_sv, ld_lens, ld_plen, ld_mask, ld_fq, ld_up, ld_sk = loads

    ld_vs.wait()
    ld_rd.wait()
    rdf = rd[...].astype(f32)
    rd2 = jnp.concatenate(
        [rdf[(i // 2) * HPG : (i // 2 + 1) * HPG] for i in range(2 * KVH)], axis=0
    ).astype(bf16)
    row_g = iota((HD, HD), 0) // (2 * HPG)

    def rv_of(values):
        total = None
        for g in range(KVH):
            w = jnp.where(row_g == g, rd2, jnp.zeros_like(rd2))
            part = nt(values[:, g * HD : (g + 1) * HD], w)
            total = part if total is None else total + part
        return total

    def parts_of(x):
        high = x.astype(bf16).astype(f32)
        return jnp.where(lax.rem(iota(x.shape, 1) // HPG, 2) == 0, high, x - high).astype(bf16)

    shard[:, 0:HD] = parts_of(rv_of(vshard[...]))
    ld_ks.wait()
    kv[core, chip] = shard[...]

    pl.semaphore_wait(barrier, n_half - 1 + n_z - 1 + 1)

    part_at = (0, 2, 3, 6, 9)
    n_parts = len(part_at) - 1

    def part_cols(n):
        return pl.ds(part_at[n] * HD, (part_at[n + 1] - part_at[n]) * HD)

    def block_cols(n):
        return pl.ds(pl.multiple_of(n * HD, HD), HD)

    def issue(n):
        for o in group_offsets:
            remote(
                shard.at[:, part_cols(n)],
                kv.at[core, chip, :, part_cols(n)],
                gsend.at[n],
                grecv.at[n],
                device_at(place_at(o)),
            ).start()

    def forward_copy(n, which):
        part = kv.at[core, :, :, part_cols(n)]
        return remote(part, kv.at[which, :, :, part_cols(n)], fsend.at[n], frecv.at[n], sibling)

    def arrive(n):
        part = kv.at[core, pl.ds(0, n_chip - 1), :, part_cols(n)]
        remote(part, part, gsend.at[n], grecv.at[n], sibling).wait_recv()
        forward_copy(n, core).start()

    issue(0)
    issue(1)

    ld_dmap.wait()
    ld_tokens.wait()
    down_t = nt(dmap[...], tokens[...]).astype(bf16)
    down = down_t.astype(f32).T.astype(bf16)
    ld_lens.wait()
    len0 = lens[0, 0]
    len1 = lens[0, 1]
    lane = iota((RANK, HD), 1)
    t_of = lax.rem(lane, STEP)
    sign = jnp.where(
        lane < STEP,
        jnp.where(t_of < len0, -1.0, 0.0),
        jnp.where(t_of < len1, 1.0, 0.0),
    ).astype(f32)
    down_signed = (down_t.astype(f32) * sign).astype(bf16)

    ld_plen.wait()
    ld_mask.wait()
    limit = plen[0]
    seen[pl.ds(prefix, STEP), :] = jnp.zeros((STEP, MASK), bf16)
    for b in range(n_cont):
        block = 2 * (b % n_chip) + b // n_chip
        inside = block * BLOCK < limit
        fill = [jnp.where((mask[c, block] > 0) & inside, 0.0, NEG) for c in range(2)]
        col = iota((BLOCK, MASK), 1)
        seen[pl.ds(b * BLOCK, BLOCK), :] = jnp.where(
            col == 0, fill[0], jnp.where(col == 1, fill[1], 0.0)
        ).astype(bf16)
    causal = jnp.where(iota((STEP, HD), 0) > lax.rem(iota((STEP, HD), 1), STEP), NEG, 0.0).astype(f32)
    causal = jnp.concatenate([causal] * (HALF // HD), axis=1)

    ld_sv.wait()
    rvs[...] = rv_of(sv[...])
    step_parts = parts_of(rvs[...]).astype(f32)
    for c in range(2):
        rvst[c] = step_parts[c * STEP : (c + 1) * STEP].T.astype(bf16)
    issue(2)
    ld_fq.wait()
    ld_up.wait()
    ld_sk.wait()

    def prepare(g, carry):
        col = pl.multiple_of(g * GCOL, GCOL)
        frozen = fq[:, pl.ds(col, GCOL)].astype(f32) * (FACTOR * LOG2E)
        change = nn(down, up[:, pl.ds(col, GCOL)]) * (ADAPTER_SCALE * FACTOR * LOG2E)
        for s, q in enumerate(((frozen + change).astype(bf16), frozen.astype(bf16))):
            for c in range(2):
                rows = slice(c * STEP, (c + 1) * STEP)
                for h in range(0, HPG, 2):
                    pair = [q[rows, (h + i) * HD : (h + i + 1) * HD] for i in range(2)]
                    at = c * LANES + h * STEP
                    qt[s, g, :, at : at + HD] = jnp.concatenate(pair, axis=0).T
        return carry

    lax.fori_loop(0, KVH, prepare, 0)
    issue(3)
    for c in range(2):
        picks[c] = (iota((MASK, HALF), 0) == c).astype(f32).astype(bf16)

    units = [(c, j) for j in range(2) for c in range(2)]

    def stage_a(g, u, slot):
        c, j = units[u]
        kp = kv[:, :, :, block_cols(g + 1)].reshape(prefix, HD)
        ks = sk[pl.ds(c * STEP, STEP), block_cols(g)]
        at = c * LANES + j * HALF
        keys = jnp.concatenate([jnp.concatenate([kp, ks], axis=0), seen[...]], axis=1)
        for s in range(2):
            q = qt[s, g, :, at : at + HALF]
            scores = nn(keys, jnp.concatenate([q, picks[c]], axis=0))
            s_p = scores[0:prefix]
            s_s = scores[prefix:] + causal
            sbuf[slot, s, pl.ds(0, prefix), :] = s_p
            sbuf[slot, s, pl.ds(prefix, STEP), :] = s_s
            mbuf[slot, s] = jnp.maximum(
                jnp.max(s_p, axis=0, keepdims=True), jnp.max(s_s, axis=0, keepdims=True)
            )

    def expand(rows, g, j):
        parts = []
        for i in range(2):
            index = g * (2 * HPG) + 4 * j + 2 * i + iota(rows.shape, 1) // STEP
            parts.append(jnp.take_along_axis(rows, index, axis=1))
        return jnp.concatenate(parts, axis=1)

    def weights(slot, s):
        peak = mbuf[slot, s]
        e_p = jnp.exp2(sbuf[slot, s, pl.ds(0, prefix), :] - peak)
        e_s = jnp.exp2(sbuf[slot, s, pl.ds(prefix, STEP), :] - peak)
        return e_p, e_s

    def stage_b(g, u, slot):
        c, j = units[u]
        rv_p = rvx[j]
        rv_s = expand(rvs[pl.ds(c * STEP, STEP), :], g, j)
        e_p, e_s = weights(slot, 0)
        total = jnp.sum(e_p, axis=0, keepdims=True) + jnp.sum(e_s, axis=0, keepdims=True)
        o = jnp.sum(e_p * rv_p, axis=0, keepdims=True) + jnp.sum(e_s * rv_s, axis=0, keepdims=True)
        inverse = 1.0 / total
        o = o * inverse
        ds_p = (e_p * (rv_p - o)).astype(bf16)
        ds_s = (e_s * (rv_s - o)).astype(bf16)
        e_p, e_s = weights(slot, 1)
        own = pl.ds(pl.multiple_of(g * 16, 16), 16)
        sums = nn(jnp.concatenate([rvt[own, :], jnp.ones((16, prefix), bf16)], axis=0), e_p.astype(bf16))
        sums = sums + nn(
            jnp.concatenate([rvst[c, own, :], jnp.ones((16, STEP), bf16)], axis=0), e_s.astype(bf16)
        )
        shape = (16, HALF)
        mine = lax.rem(iota(shape, 0), HPG) == 4 * j + iota(shape, 1) // STEP
        o_ref = jnp.sum(jnp.where(mine, sums[0:16], 0.0), axis=0, keepdims=True) / sums[16:17]
        return ds_p, ds_s, inverse * FACTOR, o - o_ref

    def stage_c(g, u, kp_t, ds_p, ds_s, scale):
        c, j = units[u]
        ks_t = sk[pl.ds(c * STEP, STEP), block_cols(g)].T
        dq = ((nn(kp_t, ds_p) + nn(ks_t, ds_s)) * scale).astype(bf16)
        for i in range(2):
            h = 4 * j + 2 * i
            nat = dq[:, i * HD : (i + 1) * HD].T
            for k in range(2):
                gbuf[pl.ds(c * STEP, STEP), (h + k) * HD : (h + k + 1) * HD] = nat[
                    k * STEP : (k + 1) * STEP
                ]

    def tail(g, dd):
        col = pl.multiple_of(g * GCOL, GCOL)
        gq = gbuf[...]
        ubuf[:, pl.ds(col, GCOL)] = nn(down_signed, gq).astype(bf16)
        return dd + nt(up[:, pl.ds(col, GCOL)], gq)

    def send_up(g):
        for i in range(dests):
            p = g * dests + i
            r = lax.rem(p, n_half)

            @pl.when(r != place)
            def _(p=p, r=r):
                cols = pl.ds(pl.multiple_of(p * width, 128), width)
                to = plane_dev(core * n_half + r)
                remote(ubuf.at[:, cols], ru.at[p // n_half, place], usend.at[0], urecv.at[0], to).start()

    def group_body(g, carry, peeled=None):
        accs = list(carry[:4])
        following = jnp.minimum(g + 1, KVH - 1)
        dd = carry[4] if peeled == 0 else tail(g - 1, carry[4])
        kp_t = kv[:, :, :, block_cols(g + 1)].reshape(prefix, HD).T
        for u in range(4):
            if u == 1:
                rvx[1] = expand(rvf[...], g, 1)
            if u == 3:
                rvx[0] = expand(rvf[...], following, 0)
            if u < 3:
                stage_a(g, u + 1, (u + 1) % 2)
            else:
                if peeled is not None:
                    forward_copy(peeled + 1, 1 - core).wait_recv()
                if peeled == 0:
                    arrive(2)
                stage_a(following, 0, 0)
            ds_p, ds_s, scale, diff = stage_b(g, u, u % 2)
            accs[u] = accs[u] + diff
            stage_c(g, u, kp_t, ds_p, ds_s, scale)
        return (*accs, dd)

    def group_step(g, carry):
        @pl.when(g == 3)
        def _():
            arrive(3)

        @pl.when(g == 4)
        def _():
            forward_copy(3, 1 - core).wait_recv()

        send_up(g - 2)
        return group_body(g, carry)

    arrive(0)
    forward_copy(0, 1 - core).wait_recv()
    projected = kv[:, :, :, 0:HD].reshape(prefix, HD)
    rvt[...] = projected.T
    projected = projected.astype(f32)
    rvf[...] = projected + pltpu.roll(projected, HD - HPG, 1)
    rvx[0] = expand(rvf[...], 0, 0)

    gbuf[...] = jnp.zeros_like(gbuf)
    stage_a(0, 0, 0)
    zero_acc = jnp.zeros((1, HALF), f32)
    arrive(1)
    carry = group_body(0, (zero_acc,) * 4 + (jnp.zeros((RANK, HD), f32),), 0)
    carry = group_body(1, carry, 1)
    carry = lax.fori_loop(2, KVH, group_step, carry)
    send_up(KVH - 2)
    dd = tail(KVH - 1, carry[4])
    send_up(KVH - 1)

    tl = lax.rem(iota((1, HALF), 1), STEP)
    m0 = jnp.sum(jnp.where(tl < len0, carry[0] + carry[2], 0.0), axis=1, keepdims=True)
    m1 = jnp.sum(jnp.where(tl < len1, carry[1] + carry[3], 0.0), axis=1, keepdims=True)
    zv = BETA * (m0 - m1)
    small = jnp.exp(-jnp.abs(zv))
    loss = jnp.maximum(-zv, 0.0) + jnp.log1p(small)
    weight = (BETA * LOSS_SCALE) * jnp.where(zv >= 0.0, small, 1.0) / (1.0 + small)

    dd = (ADAPTER_SCALE * dd * sign).astype(bf16)
    for i in range(KVH):
        cols = pl.ds(i * GCOL, GCOL)
        dbuf[:, cols] = (nn(dd, tokens[:, cols]) * weight).astype(bf16)

    def side(which):
        return pl.ds(pl.multiple_of(which * n_half * width, 128), n_half * width)

    def cols_of(p):
        return pl.ds(pl.multiple_of(p * width, 128), width)

    swap = remote(dbuf.at[:, side(1 - core)], dsib, xsend.at[0], xrecv.at[0], sibling)
    swap.start()

    notes[place] = jnp.where(iota((2, HD), 0) == 0, loss, weight)

    for o in plane_offsets:
        to = device_at(place_at(o))
        remote(notes.at[place], notes.at[place], nsend.at[0], nrecv.at[0], to).start()
    for h in range(2):
        ru[h, place] = ubuf[:, cols_of(h * n_half + place)]

    swap.wait_recv()
    dsum[...] = (dbuf[:, side(core)].astype(f32) + dsib[...].astype(f32)).astype(bf16)

    for o in plane_offsets:
        r = place_at(o)
        remote(dsum.at[:, cols_of(r)], rdn.at[place], dsend.at[0], drecv.at[0], device_at(r)).start()

    my_cols = pl.ds(pl.multiple_of(me * width, 128), width)

    def z_start(buf, send, recv):
        for k in z_offsets:
            remote(buf.at[zi], buf.at[zi], send, recv, z_dev(lax.rem(zi + k, n_z))).start()

    def z_end(buf, send, recv):
        others = buf.at[pl.ds(0, n_z - 1)]
        remote(others, others, send, recv, sibling).wait_recv()
        out = buf[0].astype(f32)
        for z in range(1, n_z):
            out = out + buf[z].astype(f32)
        return out

    def all_start(row, send, recv):
        part = grads.at[pl.ds(row, RANK), my_cols]

        for o in plane_offsets:
            remote(part, part, send, recv, device_at(place_at(o))).start()

    def half_of(row, which):
        return grads.at[pl.ds(row, RANK), side(which)]

    def all_forward(row, recv, send, to_sibling):
        others = grads.at[pl.ds(row, RANK), pl.ds(0, (n_half - 1) * width)]
        remote(others, others, send, recv, sibling).wait_recv()
        remote(half_of(row, core), half_of(row, core), send, to_sibling, sibling).start()

    def all_end(row, send, to_sibling):
        remote(half_of(row, core), half_of(row, 1 - core), send, to_sibling, sibling).wait_recv()

    others = notes.at[pl.ds(0, n_half - 1)]
    remote(others, others, nsend.at[0], nrecv.at[0], sibling).wait_recv()
    others = ru.at[:, pl.ds(0, n_half - 1)]
    remote(others, others, usend.at[0], urecv.at[0], sibling).wait_recv()

    def share(h):
        acc = jnp.zeros((RANK, width), f32)
        for r in range(n_half):
            w = jnp.concatenate([notes[r][1:2]] * (width // HD), axis=1)
            acc = acc + w * ru[h, r].astype(f32)
        return acc * ADAPTER_SCALE

    ushare[0] = share(1 - core).astype(bf16)
    loss_sum = notes[0][0:1]
    for r in range(1, n_half):
        loss_sum = loss_sum + notes[r][0:1]
    lpair[core] = loss_sum
    give = remote(ushare.at[0], ushare.at[1], gvsend.at[0], gvrecv.at[0], sibling)
    give.start()
    tell = remote(lpair.at[core], lpair.at[core], tlsend.at[0], tlrecv.at[0], sibling)
    tell.start()
    mine = share(core)

    others = rdn.at[pl.ds(0, n_half - 1)]
    remote(others, others, dsend.at[0], drecv.at[0], sibling).wait_recv()
    rdn[place] = dsum[:, cols_of(place)]
    acc = rdn[0].astype(f32)
    for r in range(1, n_half):
        acc = acc + rdn[r].astype(f32)
    zd[zi] = acc.astype(bf16)
    z_start(zd, zdsend.at[0], zdrecv.at[0])

    give.wait_recv()
    zu[zi] = (mine + ushare[1].astype(f32)).astype(bf16)
    z_start(zu, zusend.at[0], zurecv.at[0])
    tell.wait_recv()
    znotes[zi] = lpair[0] + lpair[1]
    z_start(znotes, znsend.at[0], znrecv.at[0])

    grads[pl.ds(RANK, RANK), my_cols] = z_end(zd, zdsend.at[0], zdrecv.at[0]).astype(bf16)
    all_start(RANK, adsend.at[0], adrecv.at[0])
    grads[pl.ds(0, RANK), my_cols] = z_end(zu, zusend.at[0], zurecv.at[0]).astype(bf16)
    all_start(0, ausend.at[0], aurecv.at[0])
    loss_out[...] = z_end(znotes, znsend.at[0], znrecv.at[0])

    all_forward(RANK, adrecv.at[0], sdsend.at[0], sdrecv.at[0])

    def sent(ref, sem):
        remote(ref, ref, sem, sem, sibling).wait_send()

    for n in range(n_parts):
        sent(kv.at[core, pl.ds(0, n_chip - 1), :, part_cols(n)], gsend.at[n])
        sent(kv.at[core, :, :, part_cols(n)], fsend.at[n])
    sent(ru.at[:, pl.ds(0, n_half - 1)], usend.at[0])
    sent(rdn.at[pl.ds(0, n_half - 1)], dsend.at[0])
    sent(notes.at[pl.ds(0, n_half - 1)], nsend.at[0])
    swap.wait_send()
    give.wait_send()
    tell.wait_send()
    sent(zu.at[pl.ds(0, n_z - 1)], zusend.at[0])
    sent(zd.at[pl.ds(0, n_z - 1)], zdsend.at[0])
    sent(znotes.at[pl.ds(0, n_z - 1)], znsend.at[0])

    all_forward(0, aurecv.at[0], susend.at[0], surecv.at[0])
    for row, sem in ((0, ausend), (RANK, adsend)):
        sent(grads.at[pl.ds(row, RANK), pl.ds(0, (n_half - 1) * width)], sem.at[0])
    all_end(0, susend.at[0], surecv.at[0])
    all_end(RANK, sdsend.at[0], sdrecv.at[0])
    sent(half_of(0, core), susend.at[0])
    sent(half_of(RANK, core), sdsend.at[0])


def local(n_cont, n_z, tokens, fq, sk, sv, kshard, vshard, dmap, up, readout, lens, plen, mask):
    n_plane = 2 * n_cont
    n_half = n_cont
    n_chip = n_cont // 2
    width = FEATURES // n_plane
    rows = tokens.shape[0]
    prefix = BLOCK * n_cont
    cols = HD + KVH * HD
    anyspec = pl.BlockSpec(memory_space=pl.ANY)
    vspec = pl.BlockSpec(memory_space=pltpu.VMEM)
    dma = pltpu.SemaphoreType.DMA
    grads, loss = pl.pallas_call(
        functools.partial(kernel, (n_cont, n_z)),
        out_shape=(
            jax.ShapeDtypeStruct((2 * RANK, FEATURES), bf16),
            jax.ShapeDtypeStruct((1, 128), f32),
        ),
        in_specs=[anyspec] * 12,
        out_specs=(vspec, vspec),
        scratch_shapes=[
            pltpu.VMEM((rows, FEATURES), bf16),
            pltpu.VMEM((rows, FEATURES), bf16),
            pltpu.VMEM((rows, KVH * HD), bf16),
            pltpu.VMEM((rows, KVH * HD), bf16),
            pltpu.VMEM((RANK, FEATURES), bf16),
            pltpu.VMEM((RANK, FEATURES), bf16),
            pltpu.VMEM((BLOCK, KVH * HD), bf16),
            pltpu.VMEM((HQ, HD), bf16),
            pltpu.SMEM((1, 2), jnp.int32),
            pltpu.SMEM((1,), jnp.int32),
            pltpu.SMEM((2, n_cont), jnp.int32),
            pltpu.VMEM((2, n_chip, BLOCK, cols), bf16),
            pltpu.VMEM((BLOCK, cols), bf16),
            pltpu.VMEM((RANK, FEATURES), bf16),
            pltpu.VMEM((RANK, FEATURES), bf16),
            pltpu.VMEM((2, n_half, RANK, width), bf16),
            pltpu.VMEM((n_half, RANK, width), bf16),
            pltpu.VMEM((n_z, RANK, width), bf16),
            pltpu.VMEM((n_z, RANK, width), bf16),
            pltpu.VMEM((2, KVH, HD, 2 * LANES), bf16),
            pltpu.VMEM((prefix + STEP, MASK), bf16),
            pltpu.VMEM((2, MASK, HALF), bf16),
            pltpu.VMEM((prefix, HD), f32),
            pltpu.VMEM((HD, prefix), bf16),
            pltpu.VMEM((rows, HD), f32),
            pltpu.VMEM((2, HD, STEP), bf16),
            pltpu.VMEM((2, prefix, HALF), f32),
            pltpu.VMEM((2, 2, prefix + STEP, HALF), f32),
            pltpu.VMEM((2, 2, 1, HALF), f32),
            pltpu.VMEM((rows, GCOL), bf16),
            pltpu.VMEM((RANK, n_half * width), bf16),
            pltpu.VMEM((RANK, n_half * width), bf16),
            pltpu.VMEM((2, RANK, width), bf16),
            pltpu.VMEM((2, 1, 128), f32),
            pltpu.VMEM((n_half, 2, 128), f32),
            pltpu.VMEM((n_z, 1, 128), f32),
            dma((12,)),
            *[dma((4,))] * 4,
            *[dma((1,))] * 26,
        ],
        compiler_params=pltpu.CompilerParams(
            collective_id=0, has_side_effects=True, vmem_limit_bytes=60 * 1024 * 1024
        ),
    )(tokens, fq, sk, sv, kshard, vshard, dmap, up, readout.reshape(HQ, HD), lens, plen, mask)
    return loss[0, 0], grads[RANK:].astype(f32), grads[0:RANK].astype(f32)


def solution(mesh):
    return jax.shard_map(
        functools.partial(local, mesh.shape["cont"], mesh.shape["dp"] // 2),
        mesh=mesh,
        in_specs=(
            P(("dp", "cont"), None),
            P(("dp", "cont"), None),
            P(("dp", "cont"), None),
            P(("dp", "cont"), None),
            P(("dp", "cont"), None),
            P(("dp", "cont"), None),
            P(),
            P(),
            P(),
            P(("dp", "cont"), None),
            P("dp"),
            P(("dp", "cont"), None),
        ),
        out_specs=(P(), P(), P()),
        check_vma=False,
    )
```

```python
import functools

import jax
import jax.numpy as jnp
from jax import lax
from jax.experimental import pallas as pl
from jax.experimental.pallas import tpu as pltpu
from jax.sharding import PartitionSpec as P

HQ = 64
KVH = 8
HD = 128
HPG = HQ // KVH
BLOCK = 32
STEP = 64
RANK = 16
FEATURES = 8192
GCOL = HPG * HD
LANES = HPG * STEP
HALF = LANES // 2
MASK = 16

NEG = -1e30
BETA = 0.1
ADAPTER_SCALE = 2.0
LOSS_SCALE = 1024.0
FACTOR = HD**-0.5
LOG2E = 1.4426950408889634

MESH = pl.DeviceIdType.MESH
f32 = jnp.float32
bf16 = jnp.bfloat16


def nn(a, b):
    return lax.dot_general(a, b, (((1,), (0,)), ((), ())), preferred_element_type=f32)


def nt(a, b):
    return lax.dot_general(a, b, (((1,), (1,)), ((), ())), preferred_element_type=f32)


def iota(shape, dim):
    return lax.broadcasted_iota(jnp.int32, shape, dim)


def kernel(
    dims,
    tokens_hbm, fq_hbm, sk_hbm, sv_hbm, ks_hbm, vs_hbm, dmap_hbm, up_hbm, rd_hbm,
    lens_hbm, plen_hbm, mask_hbm,
    grads, loss_out,
    tokens, fq, sk, sv, dmap, up, vshard, rd, lens, plen, mask,
    kv, shard, ubuf, dbuf, ru, rdn, zu, zd, qt, seen, picks, rvf, rvt, rvs, rvst, rvx, sbuf, mbuf, gbuf, dsib, dsum, ushare, lpair, notes, znotes,
    local_sem, gsend, grecv, fsend, frecv, usend, urecv, dsend, drecv, nsend, nrecv,
    zusend, zurecv, zdsend, zdrecv, znsend, znrecv, ausend, aurecv, adsend, adrecv,
    susend, surecv, sdsend, sdrecv, xsend, xrecv, gvsend, gvrecv, tlsend, tlrecv,
):
    n_cont, n_z = dims
    n_plane = 2 * n_cont
    n_chip = n_cont // 2
    prefix = BLOCK * n_cont
    width = FEATURES // n_plane
    dests = n_plane // KVH
    n_half = n_plane // 2
    dp = lax.axis_index("dp")
    cont = lax.axis_index("cont")
    core = lax.rem(cont, 2)
    chip = cont // 2
    zi = dp // 2
    xlo = lax.rem(dp, 2)
    place = xlo * n_chip + chip
    me = core * n_half + place

    def plane_dev(p):
        r = lax.rem(p, n_half)
        return {"dp": zi * 2 + r // n_chip, "cont": lax.rem(r, n_chip) * 2 + p // n_half}

    sibling = {"cont": chip * 2 + (1 - core)}

    def remote(src, dst, send, recv, to):
        return pltpu.make_async_remote_copy(
            src_ref=src, dst_ref=dst, send_sem=send, recv_sem=recv, device_id=to, device_id_type=MESH
        )

    def z_dev(z):
        return {"dp": z * 2 + xlo, "cont": cont}

    barrier = pltpu.get_barrier_semaphore()

    n_y = n_chip // 2
    x = 2 * lax.rem(chip, 2) + xlo
    y = chip // 2

    def hops(o):
        return min(o[0], n_y - o[0]) + min(o[1], 4 - o[1])

    plane_offsets = sorted(
        [(oy, ox) for oy in range(n_y) for ox in range(4) if (oy, ox) != (0, 0)], key=hops, reverse=True
    )
    group_offsets = [o for o in plane_offsets if o[1] % 2 == 0]
    z_offsets = sorted(range(1, n_z), key=lambda k: min(k, n_z - k), reverse=True)

    def place_at(o):
        px = lax.rem(x + o[1], 4)
        return lax.rem(px, 2) * n_chip + lax.rem(y + o[0], n_y) * 2 + px // 2

    def device_at(r):
        return plane_dev(core * n_half + r)

    def greet(to):
        pl.semaphore_signal(barrier, inc=1, device_id=to, device_id_type=MESH)

    for k in z_offsets:
        greet(z_dev(lax.rem(zi + k, n_z)))
    for o in plane_offsets:
        greet(device_at(place_at(o)))
    greet(sibling)

    loads = []
    for i, (src, dst) in enumerate(
        (
            (vs_hbm, vshard),
            (rd_hbm, rd),
            (ks_hbm, shard.at[:, HD:]),
            (dmap_hbm, dmap),
            (tokens_hbm, tokens),
            (sv_hbm, sv),
            (lens_hbm, lens),
            (plen_hbm, plen),
            (mask_hbm, mask),
            (fq_hbm, fq),
            (up_hbm, up),
            (sk_hbm, sk),
        )
    ):
        cp = pltpu.make_async_copy(src, dst, local_sem.at[i])
        cp.start()
        loads.append(cp)
    ld_vs, ld_rd, ld_ks, ld_dmap, ld_tokens, ld_sv, ld_lens, ld_plen, ld_mask, ld_fq, ld_up, ld_sk = loads

    ld_vs.wait()
    ld_rd.wait()
    rdf = rd[...].astype(f32)
    rd2 = jnp.concatenate(
        [rdf[(i // 2) * HPG : (i // 2 + 1) * HPG] for i in range(2 * KVH)], axis=0
    ).astype(bf16)
    row_g = iota((HD, HD), 0) // (2 * HPG)

    def rv_of(values):
        total = None
        for g in range(KVH):
            w = jnp.where(row_g == g, rd2, jnp.zeros_like(rd2))
            part = nt(values[:, g * HD : (g + 1) * HD], w)
            total = part if total is None else total + part
        return total

    def parts_of(x):
        high = x.astype(bf16).astype(f32)
        return jnp.where(lax.rem(iota(x.shape, 1) // HPG, 2) == 0, high, x - high).astype(bf16)

    shard[:, 0:HD] = parts_of(rv_of(vshard[...]))
    ld_ks.wait()
    kv[core, chip] = shard[...]

    pl.semaphore_wait(barrier, n_half - 1 + n_z - 1 + 1)

    part_at = (0, 2, 3, 6, 9)
    n_parts = len(part_at) - 1

    def part_cols(n):
        return pl.ds(part_at[n] * HD, (part_at[n + 1] - part_at[n]) * HD)

    def block_cols(n):
        return pl.ds(pl.multiple_of(n * HD, HD), HD)

    def issue(n):
        for o in group_offsets:
            remote(
                shard.at[:, part_cols(n)],
                kv.at[core, chip, :, part_cols(n)],
                gsend.at[n],
                grecv.at[n],
                device_at(place_at(o)),
            ).start()

    def forward_copy(n, which):
        part = kv.at[core, :, :, part_cols(n)]
        return remote(part, kv.at[which, :, :, part_cols(n)], fsend.at[n], frecv.at[n], sibling)

    def arrive(n):
        part = kv.at[core, pl.ds(0, n_chip - 1), :, part_cols(n)]
        remote(part, part, gsend.at[n], grecv.at[n], sibling).wait_recv()
        forward_copy(n, core).start()

    issue(0)
    issue(1)

    ld_dmap.wait()
    ld_tokens.wait()
    down_t = nt(dmap[...], tokens[...]).astype(bf16)
    down = down_t.astype(f32).T.astype(bf16)
    ld_lens.wait()
    len0 = lens[0, 0]
    len1 = lens[0, 1]
    lane = iota((RANK, HD), 1)
    t_of = lax.rem(lane, STEP)
    sign = jnp.where(
        lane < STEP,
        jnp.where(t_of < len0, -1.0, 0.0),
        jnp.where(t_of < len1, 1.0, 0.0),
    ).astype(f32)
    down_signed = (down_t.astype(f32) * sign).astype(bf16)

    ld_plen.wait()
    ld_mask.wait()
    limit = plen[0]
    seen[pl.ds(prefix, STEP), :] = jnp.zeros((STEP, MASK), bf16)
    for b in range(n_cont):
        block = 2 * (b % n_chip) + b // n_chip
        inside = block * BLOCK < limit
        fill = [jnp.where((mask[c, block] > 0) & inside, 0.0, NEG) for c in range(2)]
        col = iota((BLOCK, MASK), 1)
        seen[pl.ds(b * BLOCK, BLOCK), :] = jnp.where(
            col == 0, fill[0], jnp.where(col == 1, fill[1], 0.0)
        ).astype(bf16)
    causal = jnp.where(iota((STEP, HD), 0) > lax.rem(iota((STEP, HD), 1), STEP), NEG, 0.0).astype(f32)
    causal = jnp.concatenate([causal] * (HALF // HD), axis=1)

    ld_sv.wait()
    rvs[...] = rv_of(sv[...])
    step_parts = parts_of(rvs[...]).astype(f32)
    for c in range(2):
        rvst[c] = step_parts[c * STEP : (c + 1) * STEP].T.astype(bf16)
    issue(2)
    ld_fq.wait()
    ld_up.wait()
    ld_sk.wait()

    def prepare(g, carry):
        col = pl.multiple_of(g * GCOL, GCOL)
        frozen = fq[:, pl.ds(col, GCOL)].astype(f32) * (FACTOR * LOG2E)
        change = nn(down, up[:, pl.ds(col, GCOL)]) * (ADAPTER_SCALE * FACTOR * LOG2E)
        for s, q in enumerate(((frozen + change).astype(bf16), frozen.astype(bf16))):
            for c in range(2):
                rows = slice(c * STEP, (c + 1) * STEP)
                for h in range(0, HPG, 2):
                    pair = [q[rows, (h + i) * HD : (h + i + 1) * HD] for i in range(2)]
                    at = c * LANES + h * STEP
                    qt[s, g, :, at : at + HD] = jnp.concatenate(pair, axis=0).T
        return carry

    lax.fori_loop(0, KVH, prepare, 0)
    issue(3)
    for c in range(2):
        picks[c] = (iota((MASK, HALF), 0) == c).astype(f32).astype(bf16)

    units = [(c, j) for j in range(2) for c in range(2)]

    def stage_a(g, u, slot):
        c, j = units[u]
        kp = kv[:, :, :, block_cols(g + 1)].reshape(prefix, HD)
        ks = sk[pl.ds(c * STEP, STEP), block_cols(g)]
        at = c * LANES + j * HALF
        keys = jnp.concatenate([jnp.concatenate([kp, ks], axis=0), seen[...]], axis=1)
        for s in range(2):
            q = qt[s, g, :, at : at + HALF]
            scores = nn(keys, jnp.concatenate([q, picks[c]], axis=0))
            s_p = scores[0:prefix]
            s_s = scores[prefix:] + causal
            sbuf[slot, s, pl.ds(0, prefix), :] = s_p
            sbuf[slot, s, pl.ds(prefix, STEP), :] = s_s
            mbuf[slot, s] = jnp.maximum(
                jnp.max(s_p, axis=0, keepdims=True), jnp.max(s_s, axis=0, keepdims=True)
            )

    def expand(rows, g, j):
        parts = []
        for i in range(2):
            index = g * (2 * HPG) + 4 * j + 2 * i + iota(rows.shape, 1) // STEP
            parts.append(jnp.take_along_axis(rows, index, axis=1))
        return jnp.concatenate(parts, axis=1)

    def weights(slot, s):
        peak = mbuf[slot, s]
        e_p = jnp.exp2(sbuf[slot, s, pl.ds(0, prefix), :] - peak)
        e_s = jnp.exp2(sbuf[slot, s, pl.ds(prefix, STEP), :] - peak)
        return e_p, e_s

    def stage_b(g, u, slot):
        c, j = units[u]
        rv_p = rvx[j]
        rv_s = expand(rvs[pl.ds(c * STEP, STEP), :], g, j)
        e_p, e_s = weights(slot, 0)
        total = jnp.sum(e_p, axis=0, keepdims=True) + jnp.sum(e_s, axis=0, keepdims=True)
        o = jnp.sum(e_p * rv_p, axis=0, keepdims=True) + jnp.sum(e_s * rv_s, axis=0, keepdims=True)
        inverse = 1.0 / total
        o = o * inverse
        ds_p = (e_p * (rv_p - o)).astype(bf16)
        ds_s = (e_s * (rv_s - o)).astype(bf16)
        e_p, e_s = weights(slot, 1)
        own = pl.ds(pl.multiple_of(g * 16, 16), 16)
        sums = nn(jnp.concatenate([rvt[own, :], jnp.ones((16, prefix), bf16)], axis=0), e_p.astype(bf16))
        sums = sums + nn(
            jnp.concatenate([rvst[c, own, :], jnp.ones((16, STEP), bf16)], axis=0), e_s.astype(bf16)
        )
        shape = (16, HALF)
        mine = lax.rem(iota(shape, 0), HPG) == 4 * j + iota(shape, 1) // STEP
        o_ref = jnp.sum(jnp.where(mine, sums[0:16], 0.0), axis=0, keepdims=True) / sums[16:17]
        return ds_p, ds_s, inverse * FACTOR, o - o_ref

    def stage_c(g, u, kp_t, ds_p, ds_s, scale):
        c, j = units[u]
        ks_t = sk[pl.ds(c * STEP, STEP), block_cols(g)].T
        dq = ((nn(kp_t, ds_p) + nn(ks_t, ds_s)) * scale).astype(bf16)
        for i in range(2):
            h = 4 * j + 2 * i
            nat = dq[:, i * HD : (i + 1) * HD].T
            for k in range(2):
                gbuf[pl.ds(c * STEP, STEP), (h + k) * HD : (h + k + 1) * HD] = nat[
                    k * STEP : (k + 1) * STEP
                ]

    def tail(g, dd):
        col = pl.multiple_of(g * GCOL, GCOL)
        gq = gbuf[...]
        ubuf[:, pl.ds(col, GCOL)] = nn(down_signed, gq).astype(bf16)
        return dd + nt(up[:, pl.ds(col, GCOL)], gq)

    def send_up(g):
        for i in range(dests):
            p = g * dests + i
            r = lax.rem(p, n_half)

            @pl.when(r != place)
            def _(p=p, r=r):
                cols = pl.ds(pl.multiple_of(p * width, 128), width)
                to = plane_dev(core * n_half + r)
                remote(ubuf.at[:, cols], ru.at[p // n_half, place], usend.at[0], urecv.at[0], to).start()

    def group_body(g, carry, peeled=None):
        accs = list(carry[:4])
        following = jnp.minimum(g + 1, KVH - 1)
        dd = carry[4] if peeled == 0 else tail(g - 1, carry[4])
        kp_t = kv[:, :, :, block_cols(g + 1)].reshape(prefix, HD).T
        for u in range(4):
            if u == 1:
                rvx[1] = expand(rvf[...], g, 1)
            if u == 3:
                rvx[0] = expand(rvf[...], following, 0)
            if u < 3:
                stage_a(g, u + 1, (u + 1) % 2)
            else:
                if peeled is not None:
                    forward_copy(peeled + 1, 1 - core).wait_recv()
                if peeled == 0:
                    arrive(2)
                stage_a(following, 0, 0)
            ds_p, ds_s, scale, diff = stage_b(g, u, u % 2)
            accs[u] = accs[u] + diff
            stage_c(g, u, kp_t, ds_p, ds_s, scale)
        return (*accs, dd)

    def group_step(g, carry):
        @pl.when(g == 3)
        def _():
            arrive(3)

        @pl.when(g == 4)
        def _():
            forward_copy(3, 1 - core).wait_recv()

        send_up(g - 2)
        return group_body(g, carry)

    arrive(0)
    forward_copy(0, 1 - core).wait_recv()
    projected = kv[:, :, :, 0:HD].reshape(prefix, HD)
    rvt[...] = projected.T
    projected = projected.astype(f32)
    rvf[...] = projected + pltpu.roll(projected, HD - HPG, 1)
    rvx[0] = expand(rvf[...], 0, 0)

    gbuf[...] = jnp.zeros_like(gbuf)
    stage_a(0, 0, 0)
    zero_acc = jnp.zeros((1, HALF), f32)
    arrive(1)
    carry = group_body(0, (zero_acc,) * 4 + (jnp.zeros((RANK, HD), f32),), 0)
    carry = group_body(1, carry, 1)
    carry = lax.fori_loop(2, KVH, group_step, carry)
    send_up(KVH - 2)
    dd = tail(KVH - 1, carry[4])
    send_up(KVH - 1)

    tl = lax.rem(iota((1, HALF), 1), STEP)
    m0 = jnp.sum(jnp.where(tl < len0, carry[0] + carry[2], 0.0), axis=1, keepdims=True)
    m1 = jnp.sum(jnp.where(tl < len1, carry[1] + carry[3], 0.0), axis=1, keepdims=True)
    zv = BETA * (m0 - m1)
    small = jnp.exp(-jnp.abs(zv))
    loss = jnp.maximum(-zv, 0.0) + jnp.log1p(small)
    weight = (BETA * LOSS_SCALE) * jnp.where(zv >= 0.0, small, 1.0) / (1.0 + small)

    dd = (ADAPTER_SCALE * dd * sign).astype(bf16)
    for i in range(KVH):
        cols = pl.ds(i * GCOL, GCOL)
        dbuf[:, cols] = (nn(dd, tokens[:, cols]) * weight).astype(bf16)

    def side(which):
        return pl.ds(pl.multiple_of(which * n_half * width, 128), n_half * width)

    def cols_of(p):
        return pl.ds(pl.multiple_of(p * width, 128), width)

    swap = remote(dbuf.at[:, side(1 - core)], dsib, xsend.at[0], xrecv.at[0], sibling)
    swap.start()

    notes[place] = jnp.where(iota((2, HD), 0) == 0, loss, weight)

    for o in plane_offsets:
        to = device_at(place_at(o))
        remote(notes.at[place], notes.at[place], nsend.at[0], nrecv.at[0], to).start()
    for h in range(2):
        ru[h, place] = ubuf[:, cols_of(h * n_half + place)]

    swap.wait_recv()
    dsum[...] = (dbuf[:, side(core)].astype(f32) + dsib[...].astype(f32)).astype(bf16)

    for o in plane_offsets:
        r = place_at(o)
        remote(dsum.at[:, cols_of(r)], rdn.at[place], dsend.at[0], drecv.at[0], device_at(r)).start()

    my_cols = pl.ds(pl.multiple_of(me * width, 128), width)

    def z_start(buf, send, recv):
        for k in z_offsets:
            remote(buf.at[zi], buf.at[zi], send, recv, z_dev(lax.rem(zi + k, n_z))).start()

    def z_end(buf, send, recv):
        others = buf.at[pl.ds(0, n_z - 1)]
        remote(others, others, send, recv, sibling).wait_recv()
        out = buf[0].astype(f32)
        for z in range(1, n_z):
            out = out + buf[z].astype(f32)
        return out

    def all_start(row, send, recv):
        part = grads.at[pl.ds(row, RANK), my_cols]

        for o in plane_offsets:
            remote(part, part, send, recv, device_at(place_at(o))).start()

    def half_of(row, which):
        return grads.at[pl.ds(row, RANK), side(which)]

    def all_forward(row, recv, send, to_sibling):
        others = grads.at[pl.ds(row, RANK), pl.ds(0, (n_half - 1) * width)]
        remote(others, others, send, recv, sibling).wait_recv()
        remote(half_of(row, core), half_of(row, core), send, to_sibling, sibling).start()

    def all_end(row, send, to_sibling):
        remote(half_of(row, core), half_of(row, 1 - core), send, to_sibling, sibling).wait_recv()

    others = notes.at[pl.ds(0, n_half - 1)]
    remote(others, others, nsend.at[0], nrecv.at[0], sibling).wait_recv()
    others = ru.at[:, pl.ds(0, n_half - 1)]
    remote(others, others, usend.at[0], urecv.at[0], sibling).wait_recv()

    def share(h):
        acc = jnp.zeros((RANK, width), f32)
        for r in range(n_half):
            w = jnp.concatenate([notes[r][1:2]] * (width // HD), axis=1)
            acc = acc + w * ru[h, r].astype(f32)
        return acc * ADAPTER_SCALE

    ushare[0] = share(1 - core).astype(bf16)
    loss_sum = notes[0][0:1]
    for r in range(1, n_half):
        loss_sum = loss_sum + notes[r][0:1]
    lpair[core] = loss_sum
    give = remote(ushare.at[0], ushare.at[1], gvsend.at[0], gvrecv.at[0], sibling)
    give.start()
    tell = remote(lpair.at[core], lpair.at[core], tlsend.at[0], tlrecv.at[0], sibling)
    tell.start()
    mine = share(core)

    others = rdn.at[pl.ds(0, n_half - 1)]
    remote(others, others, dsend.at[0], drecv.at[0], sibling).wait_recv()
    rdn[place] = dsum[:, cols_of(place)]
    acc = rdn[0].astype(f32)
    for r in range(1, n_half):
        acc = acc + rdn[r].astype(f32)
    zd[zi] = acc.astype(bf16)
    z_start(zd, zdsend.at[0], zdrecv.at[0])

    give.wait_recv()
    zu[zi] = (mine + ushare[1].astype(f32)).astype(bf16)
    z_start(zu, zusend.at[0], zurecv.at[0])
    tell.wait_recv()
    znotes[zi] = lpair[0] + lpair[1]
    z_start(znotes, znsend.at[0], znrecv.at[0])

    grads[pl.ds(RANK, RANK), my_cols] = z_end(zd, zdsend.at[0], zdrecv.at[0]).astype(bf16)
    all_start(RANK, adsend.at[0], adrecv.at[0])
    grads[pl.ds(0, RANK), my_cols] = z_end(zu, zusend.at[0], zurecv.at[0]).astype(bf16)
    all_start(0, ausend.at[0], aurecv.at[0])
    loss_out[...] = z_end(znotes, znsend.at[0], znrecv.at[0])

    all_forward(RANK, adrecv.at[0], sdsend.at[0], sdrecv.at[0])

    def sent(ref, sem):
        remote(ref, ref, sem, sem, sibling).wait_send()

    for n in range(n_parts):
        sent(kv.at[core, pl.ds(0, n_chip - 1), :, part_cols(n)], gsend.at[n])
        sent(kv.at[core, :, :, part_cols(n)], fsend.at[n])
    sent(ru.at[:, pl.ds(0, n_half - 1)], usend.at[0])
    sent(rdn.at[pl.ds(0, n_half - 1)], dsend.at[0])
    sent(notes.at[pl.ds(0, n_half - 1)], nsend.at[0])
    swap.wait_send()
    give.wait_send()
    tell.wait_send()
    sent(zu.at[pl.ds(0, n_z - 1)], zusend.at[0])
    sent(zd.at[pl.ds(0, n_z - 1)], zdsend.at[0])
    sent(znotes.at[pl.ds(0, n_z - 1)], znsend.at[0])

    all_forward(0, aurecv.at[0], susend.at[0], surecv.at[0])
    for row, sem in ((0, ausend), (RANK, adsend)):
        sent(grads.at[pl.ds(row, RANK), pl.ds(0, (n_half - 1) * width)], sem.at[0])
    all_end(0, susend.at[0], surecv.at[0])
    all_end(RANK, sdsend.at[0], sdrecv.at[0])
    sent(half_of(0, core), susend.at[0])
    sent(half_of(RANK, core), sdsend.at[0])


def local(n_cont, n_z, tokens, fq, sk, sv, kshard, vshard, dmap, up, readout, lens, plen, mask):
    n_plane = 2 * n_cont
    n_half = n_cont
    n_chip = n_cont // 2
    width = FEATURES // n_plane
    rows = tokens.shape[0]
    prefix = BLOCK * n_cont
    cols = HD + KVH * HD
    anyspec = pl.BlockSpec(memory_space=pl.ANY)
    vspec = pl.BlockSpec(memory_space=pltpu.VMEM)
    dma = pltpu.SemaphoreType.DMA
    grads, loss = pl.pallas_call(
        functools.partial(kernel, (n_cont, n_z)),
        out_shape=(
            pltpu.VMEM((2 * RANK, FEATURES), bf16),
            jax.ShapeDtypeStruct((1, 128), f32),
        ),
        in_specs=[anyspec] * 12,
        out_specs=(vspec, vspec),
        scratch_shapes=[
            pltpu.VMEM((rows, FEATURES), bf16),
            pltpu.VMEM((rows, FEATURES), bf16),
            pltpu.VMEM((rows, KVH * HD), bf16),
            pltpu.VMEM((rows, KVH * HD), bf16),
            pltpu.VMEM((RANK, FEATURES), bf16),
            pltpu.VMEM((RANK, FEATURES), bf16),
            pltpu.VMEM((BLOCK, KVH * HD), bf16),
            pltpu.VMEM((HQ, HD), bf16),
            pltpu.SMEM((1, 2), jnp.int32),
            pltpu.SMEM((1,), jnp.int32),
            pltpu.SMEM((2, n_cont), jnp.int32),
            pltpu.VMEM((2, n_chip, BLOCK, cols), bf16),
            pltpu.VMEM((BLOCK, cols), bf16),
            pltpu.VMEM((RANK, FEATURES), bf16),
            pltpu.VMEM((RANK, FEATURES), bf16),
            pltpu.VMEM((2, n_half, RANK, width), bf16),
            pltpu.VMEM((n_half, RANK, width), bf16),
            pltpu.VMEM((n_z, RANK, width), bf16),
            pltpu.VMEM((n_z, RANK, width), bf16),
            pltpu.VMEM((2, KVH, HD, 2 * LANES), bf16),
            pltpu.VMEM((prefix + STEP, MASK), bf16),
            pltpu.VMEM((2, MASK, HALF), bf16),
            pltpu.VMEM((prefix, HD), f32),
            pltpu.VMEM((HD, prefix), bf16),
            pltpu.VMEM((rows, HD), f32),
            pltpu.VMEM((2, HD, STEP), bf16),
            pltpu.VMEM((2, prefix, HALF), f32),
            pltpu.VMEM((2, 2, prefix + STEP, HALF), f32),
            pltpu.VMEM((2, 2, 1, HALF), f32),
            pltpu.VMEM((rows, GCOL), bf16),
            pltpu.VMEM((RANK, n_half * width), bf16),
            pltpu.VMEM((RANK, n_half * width), bf16),
            pltpu.VMEM((2, RANK, width), bf16),
            pltpu.VMEM((2, 1, 128), f32),
            pltpu.VMEM((n_half, 2, 128), f32),
            pltpu.VMEM((n_z, 1, 128), f32),
            dma((12,)),
            *[dma((4,))] * 4,
            *[dma((1,))] * 26,
        ],
        compiler_params=pltpu.CompilerParams(
            collective_id=0, has_side_effects=True, vmem_limit_bytes=60 * 1024 * 1024
        ),
    )(tokens, fq, sk, sv, kshard, vshard, dmap, up, readout.reshape(HQ, HD), lens, plen, mask)
    return loss[0, 0], grads[RANK:].astype(f32), grads[0:RANK].astype(f32)


def solution(mesh):
    return jax.shard_map(
        functools.partial(local, mesh.shape["cont"], mesh.shape["dp"] // 2),
        mesh=mesh,
        in_specs=(
            P(("dp", "cont"), None),
            P(("dp", "cont"), None),
            P(("dp", "cont"), None),
            P(("dp", "cont"), None),
            P(("dp", "cont"), None),
            P(("dp", "cont"), None),
            P(),
            P(),
            P(),
            P(("dp", "cont"), None),
            P("dp"),
            P(("dp", "cont"), None),
        ),
        out_specs=(P(), P(), P()),
        check_vma=False,
    )
```

```python
import functools

import jax
import jax.numpy as jnp
from jax import lax
from jax.experimental import pallas as pl
from jax.experimental.pallas import tpu as pltpu
from jax.sharding import PartitionSpec as P

HQ = 64
KVH = 8
HD = 128
HPG = HQ // KVH
BLOCK = 32
STEP = 64
RANK = 16
FEATURES = 8192
GCOL = HPG * HD
LANES = HPG * STEP
HALF = LANES // 2
MASK = 16

NEG = -1e30
BETA = 0.1
ADAPTER_SCALE = 2.0
LOSS_SCALE = 1024.0
FACTOR = HD**-0.5
LOG2E = 1.4426950408889634

MESH = pl.DeviceIdType.MESH
f32 = jnp.float32
bf16 = jnp.bfloat16


def nn(a, b):
    return lax.dot_general(a, b, (((1,), (0,)), ((), ())), preferred_element_type=f32)


def nt(a, b):
    return lax.dot_general(a, b, (((1,), (1,)), ((), ())), preferred_element_type=f32)


def iota(shape, dim):
    return lax.broadcasted_iota(jnp.int32, shape, dim)


def kernel(
    dims,
    tokens_hbm, fq_hbm, sk_hbm, sv_hbm, ks_hbm, vs_hbm, dmap_hbm, up_hbm, rd_hbm,
    lens_hbm, plen_hbm, mask_hbm,
    grads, loss_out,
    tokens, fq, sk, sv, dmap, up, vshard, rd, lens, plen, mask,
    kv, shard, ubuf, dbuf, ru, rdn, zu, zd, qt, seen, picks, rvf, rvt, rvs, rvst, rvx, sbuf, mbuf, gbuf, dsib, dsum, ushare, lpair, notes, znotes,
    local_sem, gsend, grecv, fsend, frecv, usend, urecv, dsend, drecv, nsend, nrecv,
    zusend, zurecv, zdsend, zdrecv, znsend, znrecv, ausend, aurecv, adsend, adrecv,
    susend, surecv, sdsend, sdrecv, xsend, xrecv, gvsend, gvrecv, tlsend, tlrecv,
):
    n_cont, n_z = dims
    n_plane = 2 * n_cont
    n_chip = n_cont // 2
    prefix = BLOCK * n_cont
    width = FEATURES // n_plane
    dests = n_plane // KVH
    n_half = n_plane // 2
    dp = lax.axis_index("dp")
    cont = lax.axis_index("cont")
    core = lax.rem(cont, 2)
    chip = cont // 2
    zi = dp // 2
    xlo = lax.rem(dp, 2)
    place = xlo * n_chip + chip
    me = core * n_half + place

    def plane_dev(p):
        r = lax.rem(p, n_half)
        return {"dp": zi * 2 + r // n_chip, "cont": lax.rem(r, n_chip) * 2 + p // n_half}

    sibling = {"cont": chip * 2 + (1 - core)}

    def remote(src, dst, send, recv, to):
        return pltpu.make_async_remote_copy(
            src_ref=src, dst_ref=dst, send_sem=send, recv_sem=recv, device_id=to, device_id_type=MESH
        )

    def z_dev(z):
        return {"dp": z * 2 + xlo, "cont": cont}

    barrier = pltpu.get_barrier_semaphore()

    n_y = n_chip // 2
    x = 2 * lax.rem(chip, 2) + xlo
    y = chip // 2

    def hops(o):
        return min(o[0], n_y - o[0]) + min(o[1], 4 - o[1])

    plane_offsets = sorted(
        [(oy, ox) for oy in range(n_y) for ox in range(4) if (oy, ox) != (0, 0)], key=hops, reverse=True
    )
    group_offsets = [o for o in plane_offsets if o[1] % 2 == 0]
    z_offsets = sorted(range(1, n_z), key=lambda k: min(k, n_z - k), reverse=True)

    def place_at(o):
        px = lax.rem(x + o[1], 4)
        return lax.rem(px, 2) * n_chip + lax.rem(y + o[0], n_y) * 2 + px // 2

    def device_at(r):
        return plane_dev(core * n_half + r)

    def greet(to):
        pl.semaphore_signal(barrier, inc=1, device_id=to, device_id_type=MESH)

    for k in z_offsets:
        greet(z_dev(lax.rem(zi + k, n_z)))
    for o in plane_offsets:
        greet(device_at(place_at(o)))
    greet(sibling)

    loads = []
    for i, (src, dst) in enumerate(
        (
            (vs_hbm, vshard),
            (rd_hbm, rd),
            (ks_hbm, shard.at[:, HD:]),
            (dmap_hbm, dmap),
            (tokens_hbm, tokens),
            (sv_hbm, sv),
            (lens_hbm, lens),
            (plen_hbm, plen),
            (mask_hbm, mask),
            (fq_hbm, fq),
            (up_hbm, up),
            (sk_hbm, sk),
        )
    ):
        cp = pltpu.make_async_copy(src, dst, local_sem.at[i])
        cp.start()
        loads.append(cp)
    ld_vs, ld_rd, ld_ks, ld_dmap, ld_tokens, ld_sv, ld_lens, ld_plen, ld_mask, ld_fq, ld_up, ld_sk = loads

    ld_vs.wait()
    ld_rd.wait()
    rdf = rd[...].astype(f32)
    rd2 = jnp.concatenate(
        [rdf[(i // 2) * HPG : (i // 2 + 1) * HPG] for i in range(2 * KVH)], axis=0
    ).astype(bf16)
    row_g = iota((HD, HD), 0) // (2 * HPG)

    def rv_of(values):
        total = None
        for g in range(KVH):
            w = jnp.where(row_g == g, rd2, jnp.zeros_like(rd2))
            part = nt(values[:, g * HD : (g + 1) * HD], w)
            total = part if total is None else total + part
        return total

    def parts_of(x):
        high = x.astype(bf16).astype(f32)
        return jnp.where(lax.rem(iota(x.shape, 1) // HPG, 2) == 0, high, x - high).astype(bf16)

    shard[:, 0:HD] = parts_of(rv_of(vshard[...]))
    ld_ks.wait()
    kv[core, chip] = shard[...]

    pl.semaphore_wait(barrier, n_half - 1 + n_z - 1 + 1)

    part_at = (0, 2, 3, 6, 9)
    n_parts = len(part_at) - 1

    def part_cols(n):
        return pl.ds(part_at[n] * HD, (part_at[n + 1] - part_at[n]) * HD)

    def block_cols(n):
        return pl.ds(pl.multiple_of(n * HD, HD), HD)

    def issue(n):
        for o in group_offsets:
            remote(
                shard.at[:, part_cols(n)],
                kv.at[core, chip, :, part_cols(n)],
                gsend.at[n],
                grecv.at[n],
                device_at(place_at(o)),
            ).start()

    def forward_copy(n, which):
        part = kv.at[core, :, :, part_cols(n)]
        return remote(part, kv.at[which, :, :, part_cols(n)], fsend.at[n], frecv.at[n], sibling)

    def arrive(n):
        part = kv.at[core, pl.ds(0, n_chip - 1), :, part_cols(n)]
        remote(part, part, gsend.at[n], grecv.at[n], sibling).wait_recv()
        forward_copy(n, core).start()

    issue(0)
    issue(1)

    ld_dmap.wait()
    ld_tokens.wait()
    down_t = nt(dmap[...], tokens[...]).astype(bf16)
    down = down_t.astype(f32).T.astype(bf16)
    ld_lens.wait()
    len0 = lens[0, 0]
    len1 = lens[0, 1]
    lane = iota((RANK, HD), 1)
    t_of = lax.rem(lane, STEP)
    sign = jnp.where(
        lane < STEP,
        jnp.where(t_of < len0, -1.0, 0.0),
        jnp.where(t_of < len1, 1.0, 0.0),
    ).astype(f32)
    down_signed = (down_t.astype(f32) * sign).astype(bf16)

    ld_plen.wait()
    ld_mask.wait()
    limit = plen[0]
    seen[pl.ds(prefix, STEP), :] = jnp.zeros((STEP, MASK), bf16)
    for b in range(n_cont):
        block = 2 * (b % n_chip) + b // n_chip
        inside = block * BLOCK < limit
        fill = [jnp.where((mask[c, block] > 0) & inside, 0.0, NEG) for c in range(2)]
        col = iota((BLOCK, MASK), 1)
        seen[pl.ds(b * BLOCK, BLOCK), :] = jnp.where(
            col == 0, fill[0], jnp.where(col == 1, fill[1], 0.0)
        ).astype(bf16)
    causal = jnp.where(iota((STEP, HD), 0) > lax.rem(iota((STEP, HD), 1), STEP), NEG, 0.0).astype(f32)
    causal = jnp.concatenate([causal] * (HALF // HD), axis=1)

    ld_sv.wait()
    rvs[...] = rv_of(sv[...])
    step_parts = parts_of(rvs[...]).astype(f32)
    for c in range(2):
        rvst[c] = step_parts[c * STEP : (c + 1) * STEP].T.astype(bf16)
    issue(2)
    ld_fq.wait()
    ld_up.wait()
    ld_sk.wait()

    def prepare(g, carry):
        col = pl.multiple_of(g * GCOL, GCOL)
        frozen = fq[:, pl.ds(col, GCOL)].astype(f32) * (FACTOR * LOG2E)
        change = nn(down, up[:, pl.ds(col, GCOL)]) * (ADAPTER_SCALE * FACTOR * LOG2E)
        for s, q in enumerate(((frozen + change).astype(bf16), frozen.astype(bf16))):
            for c in range(2):
                rows = slice(c * STEP, (c + 1) * STEP)
                for h in range(0, HPG, 2):
                    pair = [q[rows, (h + i) * HD : (h + i + 1) * HD] for i in range(2)]
                    at = c * LANES + h * STEP
                    qt[s, g, :, at : at + HD] = jnp.concatenate(pair, axis=0).T
        return carry

    lax.fori_loop(0, KVH, prepare, 0)
    issue(3)
    for c in range(2):
        picks[c] = (iota((MASK, HALF), 0) == c).astype(f32).astype(bf16)

    units = [(c, j) for j in range(2) for c in range(2)]

    def stage_a(g, u, slot):
        c, j = units[u]
        kp = kv[:, :, :, block_cols(g + 1)].reshape(prefix, HD)
        ks = sk[pl.ds(c * STEP, STEP), block_cols(g)]
        at = c * LANES + j * HALF
        keys = jnp.concatenate([jnp.concatenate([kp, ks], axis=0), seen[...]], axis=1)
        for s in range(2):
            q = qt[s, g, :, at : at + HALF]
            scores = nn(keys, jnp.concatenate([q, picks[c]], axis=0))
            s_p = scores[0:prefix]
            s_s = scores[prefix:] + causal
            sbuf[slot, s, pl.ds(0, prefix), :] = s_p
            sbuf[slot, s, pl.ds(prefix, STEP), :] = s_s
            mbuf[slot, s] = jnp.maximum(
                jnp.max(s_p, axis=0, keepdims=True), jnp.max(s_s, axis=0, keepdims=True)
            )

    def expand(rows, g, j):
        parts = []
        for i in range(2):
            index = g * (2 * HPG) + 4 * j + 2 * i + iota(rows.shape, 1) // STEP
            parts.append(jnp.take_along_axis(rows, index, axis=1))
        return jnp.concatenate(parts, axis=1)

    def weights(slot, s):
        peak = mbuf[slot, s]
        e_p = jnp.exp2(sbuf[slot, s, pl.ds(0, prefix), :] - peak)
        e_s = jnp.exp2(sbuf[slot, s, pl.ds(prefix, STEP), :] - peak)
        return e_p, e_s

    def stage_b(g, u, slot):
        c, j = units[u]
        rv_p = rvx[j]
        rv_s = expand(rvs[pl.ds(c * STEP, STEP), :], g, j)
        e_p, e_s = weights(slot, 0)
        total = jnp.sum(e_p, axis=0, keepdims=True) + jnp.sum(e_s, axis=0, keepdims=True)
        o = jnp.sum(e_p * rv_p, axis=0, keepdims=True) + jnp.sum(e_s * rv_s, axis=0, keepdims=True)
        inverse = 1.0 / total
        o = o * inverse
        ds_p = (e_p * (rv_p - o)).astype(bf16)
        ds_s = (e_s * (rv_s - o)).astype(bf16)
        e_p, e_s = weights(slot, 1)
        own = pl.ds(pl.multiple_of(g * 16, 16), 16)
        sums = nn(jnp.concatenate([rvt[own, :], jnp.ones((16, prefix), bf16)], axis=0), e_p.astype(bf16))
        sums = sums + nn(
            jnp.concatenate([rvst[c, own, :], jnp.ones((16, STEP), bf16)], axis=0), e_s.astype(bf16)
        )
        shape = (16, HALF)
        mine = lax.rem(iota(shape, 0), HPG) == 4 * j + iota(shape, 1) // STEP
        o_ref = jnp.sum(jnp.where(mine, sums[0:16], 0.0), axis=0, keepdims=True) / sums[16:17]
        return ds_p, ds_s, inverse * FACTOR, o - o_ref

    def stage_c(g, u, kp_t, ds_p, ds_s, scale):
        c, j = units[u]
        ks_t = sk[pl.ds(c * STEP, STEP), block_cols(g)].T
        dq = ((nn(kp_t, ds_p) + nn(ks_t, ds_s)) * scale).astype(bf16)
        for i in range(2):
            h = 4 * j + 2 * i
            nat = dq[:, i * HD : (i + 1) * HD].T
            for k in range(2):
                gbuf[pl.ds(c * STEP, STEP), (h + k) * HD : (h + k + 1) * HD] = nat[
                    k * STEP : (k + 1) * STEP
                ]

    def tail(g, dd):
        col = pl.multiple_of(g * GCOL, GCOL)
        gq = gbuf[...]
        ubuf[:, pl.ds(col, GCOL)] = nn(down_signed, gq).astype(bf16)
        return dd + nt(up[:, pl.ds(col, GCOL)], gq)

    def send_up(g):
        for i in range(dests):
            p = g * dests + i
            r = lax.rem(p, n_half)

            @pl.when(r != place)
            def _(p=p, r=r):
                cols = pl.ds(pl.multiple_of(p * width, 128), width)
                to = plane_dev(core * n_half + r)
                remote(ubuf.at[:, cols], ru.at[p // n_half, place], usend.at[0], urecv.at[0], to).start()

    def group_body(g, carry, peeled=None):
        accs = list(carry[:4])
        following = jnp.minimum(g + 1, KVH - 1)
        dd = carry[4] if peeled == 0 else tail(g - 1, carry[4])
        kp_t = kv[:, :, :, block_cols(g + 1)].reshape(prefix, HD).T
        for u in range(4):
            if u == 1:
                rvx[1] = expand(rvf[...], g, 1)
            if u == 3:
                rvx[0] = expand(rvf[...], following, 0)
            if u < 3:
                stage_a(g, u + 1, (u + 1) % 2)
            else:
                if peeled is not None:
                    forward_copy(peeled + 1, 1 - core).wait_recv()
                if peeled == 0:
                    arrive(2)
                stage_a(following, 0, 0)
            ds_p, ds_s, scale, diff = stage_b(g, u, u % 2)
            accs[u] = accs[u] + diff
            stage_c(g, u, kp_t, ds_p, ds_s, scale)
        return (*accs, dd)

    def group_step(g, carry):
        @pl.when(g == 3)
        def _():
            arrive(3)

        @pl.when(g == 4)
        def _():
            forward_copy(3, 1 - core).wait_recv()

        send_up(g - 2)
        return group_body(g, carry)

    arrive(0)
    forward_copy(0, 1 - core).wait_recv()
    projected = kv[:, :, :, 0:HD].reshape(prefix, HD)
    rvt[...] = projected.T
    projected = projected.astype(f32)
    rvf[...] = projected + pltpu.roll(projected, HD - HPG, 1)
    rvx[0] = expand(rvf[...], 0, 0)

    gbuf[...] = jnp.zeros_like(gbuf)
    stage_a(0, 0, 0)
    zero_acc = jnp.zeros((1, HALF), f32)
    arrive(1)
    carry = group_body(0, (zero_acc,) * 4 + (jnp.zeros((RANK, HD), f32),), 0)
    carry = group_body(1, carry, 1)
    carry = lax.fori_loop(2, KVH, group_step, carry)
    send_up(KVH - 2)
    dd = tail(KVH - 1, carry[4])
    send_up(KVH - 1)

    tl = lax.rem(iota((1, HALF), 1), STEP)
    m0 = jnp.sum(jnp.where(tl < len0, carry[0] + carry[2], 0.0), axis=1, keepdims=True)
    m1 = jnp.sum(jnp.where(tl < len1, carry[1] + carry[3], 0.0), axis=1, keepdims=True)
    zv = BETA * (m0 - m1)
    small = jnp.exp(-jnp.abs(zv))
    loss = jnp.maximum(-zv, 0.0) + jnp.log1p(small)
    weight = (BETA * LOSS_SCALE) * jnp.where(zv >= 0.0, small, 1.0) / (1.0 + small)

    dd = (ADAPTER_SCALE * dd * sign).astype(bf16)

    def down_side(which):
        for i in range(KVH // 2):
            cols = pl.ds(pl.multiple_of(which * n_half * width + i * GCOL, 128), GCOL)
            dbuf[:, cols] = (nn(dd, tokens[:, cols]) * weight).astype(bf16)

    down_side(1 - core)

    def side(which):
        return pl.ds(pl.multiple_of(which * n_half * width, 128), n_half * width)

    def cols_of(p):
        return pl.ds(pl.multiple_of(p * width, 128), width)

    swap = remote(dbuf.at[:, side(1 - core)], dsib, xsend.at[0], xrecv.at[0], sibling)
    swap.start()

    notes[place] = jnp.where(iota((2, HD), 0) == 0, loss, weight)

    for o in plane_offsets:
        to = device_at(place_at(o))
        remote(notes.at[place], notes.at[place], nsend.at[0], nrecv.at[0], to).start()
    down_side(core)
    for h in range(2):
        ru[h, place] = ubuf[:, cols_of(h * n_half + place)]

    swap.wait_recv()
    dsum[...] = (dbuf[:, side(core)].astype(f32) + dsib[...].astype(f32)).astype(bf16)

    for o in plane_offsets:
        r = place_at(o)
        remote(dsum.at[:, cols_of(r)], rdn.at[place], dsend.at[0], drecv.at[0], device_at(r)).start()

    my_cols = pl.ds(pl.multiple_of(me * width, 128), width)

    def z_start(buf, send, recv):
        for k in z_offsets:
            remote(buf.at[zi], buf.at[zi], send, recv, z_dev(lax.rem(zi + k, n_z))).start()

    def z_end(buf, send, recv):
        others = buf.at[pl.ds(0, n_z - 1)]
        remote(others, others, send, recv, sibling).wait_recv()
        out = buf[0].astype(f32)
        for z in range(1, n_z):
            out = out + buf[z].astype(f32)
        return out

    def all_start(row, send, recv):
        part = grads.at[pl.ds(row, RANK), my_cols]

        for o in plane_offsets:
            remote(part, part, send, recv, device_at(place_at(o))).start()

    def half_of(row, which):
        return grads.at[pl.ds(row, RANK), side(which)]

    def all_forward(row, recv, send, to_sibling):
        others = grads.at[pl.ds(row, RANK), pl.ds(0, (n_half - 1) * width)]
        remote(others, others, send, recv, sibling).wait_recv()
        remote(half_of(row, core), half_of(row, core), send, to_sibling, sibling).start()

    def all_end(row, send, to_sibling):
        remote(half_of(row, core), half_of(row, 1 - core), send, to_sibling, sibling).wait_recv()

    others = notes.at[pl.ds(0, n_half - 1)]
    remote(others, others, nsend.at[0], nrecv.at[0], sibling).wait_recv()
    others = ru.at[:, pl.ds(0, n_half - 1)]
    remote(others, others, usend.at[0], urecv.at[0], sibling).wait_recv()

    def share(h):
        acc = jnp.zeros((RANK, width), f32)
        for r in range(n_half):
            w = jnp.concatenate([notes[r][1:2]] * (width // HD), axis=1)
            acc = acc + w * ru[h, r].astype(f32)
        return acc * ADAPTER_SCALE

    ushare[0] = share(1 - core).astype(bf16)
    loss_sum = notes[0][0:1]
    for r in range(1, n_half):
        loss_sum = loss_sum + notes[r][0:1]
    lpair[core] = loss_sum
    give = remote(ushare.at[0], ushare.at[1], gvsend.at[0], gvrecv.at[0], sibling)
    give.start()
    tell = remote(lpair.at[core], lpair.at[core], tlsend.at[0], tlrecv.at[0], sibling)
    tell.start()
    mine = share(core)

    others = rdn.at[pl.ds(0, n_half - 1)]
    remote(others, others, dsend.at[0], drecv.at[0], sibling).wait_recv()
    rdn[place] = dsum[:, cols_of(place)]
    acc = rdn[0].astype(f32)
    for r in range(1, n_half):
        acc = acc + rdn[r].astype(f32)
    zd[zi] = acc.astype(bf16)
    z_start(zd, zdsend.at[0], zdrecv.at[0])

    give.wait_recv()
    zu[zi] = (mine + ushare[1].astype(f32)).astype(bf16)
    z_start(zu, zusend.at[0], zurecv.at[0])
    tell.wait_recv()
    znotes[zi] = lpair[0] + lpair[1]
    z_start(znotes, znsend.at[0], znrecv.at[0])

    grads[pl.ds(RANK, RANK), my_cols] = z_end(zd, zdsend.at[0], zdrecv.at[0]).astype(bf16)
    all_start(RANK, adsend.at[0], adrecv.at[0])
    grads[pl.ds(0, RANK), my_cols] = z_end(zu, zusend.at[0], zurecv.at[0]).astype(bf16)
    all_start(0, ausend.at[0], aurecv.at[0])
    loss_out[...] = z_end(znotes, znsend.at[0], znrecv.at[0])

    all_forward(RANK, adrecv.at[0], sdsend.at[0], sdrecv.at[0])

    def sent(ref, sem):
        remote(ref, ref, sem, sem, sibling).wait_send()

    for n in range(n_parts):
        sent(kv.at[core, pl.ds(0, n_chip - 1), :, part_cols(n)], gsend.at[n])
        sent(kv.at[core, :, :, part_cols(n)], fsend.at[n])
    sent(ru.at[:, pl.ds(0, n_half - 1)], usend.at[0])
    sent(rdn.at[pl.ds(0, n_half - 1)], dsend.at[0])
    sent(notes.at[pl.ds(0, n_half - 1)], nsend.at[0])
    swap.wait_send()
    give.wait_send()
    tell.wait_send()
    sent(zu.at[pl.ds(0, n_z - 1)], zusend.at[0])
    sent(zd.at[pl.ds(0, n_z - 1)], zdsend.at[0])
    sent(znotes.at[pl.ds(0, n_z - 1)], znsend.at[0])

    all_forward(0, aurecv.at[0], susend.at[0], surecv.at[0])
    for row, sem in ((0, ausend), (RANK, adsend)):
        sent(grads.at[pl.ds(row, RANK), pl.ds(0, (n_half - 1) * width)], sem.at[0])
    all_end(0, susend.at[0], surecv.at[0])
    all_end(RANK, sdsend.at[0], sdrecv.at[0])
    sent(half_of(0, core), susend.at[0])
    sent(half_of(RANK, core), sdsend.at[0])


def local(n_cont, n_z, tokens, fq, sk, sv, kshard, vshard, dmap, up, readout, lens, plen, mask):
    n_plane = 2 * n_cont
    n_half = n_cont
    n_chip = n_cont // 2
    width = FEATURES // n_plane
    rows = tokens.shape[0]
    prefix = BLOCK * n_cont
    cols = HD + KVH * HD
    anyspec = pl.BlockSpec(memory_space=pl.ANY)
    vspec = pl.BlockSpec(memory_space=pltpu.VMEM)
    dma = pltpu.SemaphoreType.DMA
    grads, loss = pl.pallas_call(
        functools.partial(kernel, (n_cont, n_z)),
        out_shape=(
            pltpu.VMEM((2 * RANK, FEATURES), bf16),
            jax.ShapeDtypeStruct((1, 128), f32),
        ),
        in_specs=[anyspec] * 12,
        out_specs=(vspec, vspec),
        scratch_shapes=[
            pltpu.VMEM((rows, FEATURES), bf16),
            pltpu.VMEM((rows, FEATURES), bf16),
            pltpu.VMEM((rows, KVH * HD), bf16),
            pltpu.VMEM((rows, KVH * HD), bf16),
            pltpu.VMEM((RANK, FEATURES), bf16),
            pltpu.VMEM((RANK, FEATURES), bf16),
            pltpu.VMEM((BLOCK, KVH * HD), bf16),
            pltpu.VMEM((HQ, HD), bf16),
            pltpu.SMEM((1, 2), jnp.int32),
            pltpu.SMEM((1,), jnp.int32),
            pltpu.SMEM((2, n_cont), jnp.int32),
            pltpu.VMEM((2, n_chip, BLOCK, cols), bf16),
            pltpu.VMEM((BLOCK, cols), bf16),
            pltpu.VMEM((RANK, FEATURES), bf16),
            pltpu.VMEM((RANK, FEATURES), bf16),
            pltpu.VMEM((2, n_half, RANK, width), bf16),
            pltpu.VMEM((n_half, RANK, width), bf16),
            pltpu.VMEM((n_z, RANK, width), bf16),
            pltpu.VMEM((n_z, RANK, width), bf16),
            pltpu.VMEM((2, KVH, HD, 2 * LANES), bf16),
            pltpu.VMEM((prefix + STEP, MASK), bf16),
            pltpu.VMEM((2, MASK, HALF), bf16),
            pltpu.VMEM((prefix, HD), f32),
            pltpu.VMEM((HD, prefix), bf16),
            pltpu.VMEM((rows, HD), f32),
            pltpu.VMEM((2, HD, STEP), bf16),
            pltpu.VMEM((2, prefix, HALF), f32),
            pltpu.VMEM((2, 2, prefix + STEP, HALF), f32),
            pltpu.VMEM((2, 2, 1, HALF), f32),
            pltpu.VMEM((rows, GCOL), bf16),
            pltpu.VMEM((RANK, n_half * width), bf16),
            pltpu.VMEM((RANK, n_half * width), bf16),
            pltpu.VMEM((2, RANK, width), bf16),
            pltpu.VMEM((2, 1, 128), f32),
            pltpu.VMEM((n_half, 2, 128), f32),
            pltpu.VMEM((n_z, 1, 128), f32),
            dma((12,)),
            *[dma((4,))] * 4,
            *[dma((1,))] * 26,
        ],
        compiler_params=pltpu.CompilerParams(
            collective_id=0, has_side_effects=True, vmem_limit_bytes=60 * 1024 * 1024
        ),
    )(tokens, fq, sk, sv, kshard, vshard, dmap, up, readout.reshape(HQ, HD), lens, plen, mask)
    return loss[0, 0], grads[RANK:].astype(f32), grads[0:RANK].astype(f32)


def solution(mesh):
    return jax.shard_map(
        functools.partial(local, mesh.shape["cont"], mesh.shape["dp"] // 2),
        mesh=mesh,
        in_specs=(
            P(("dp", "cont"), None),
            P(("dp", "cont"), None),
            P(("dp", "cont"), None),
            P(("dp", "cont"), None),
            P(("dp", "cont"), None),
            P(("dp", "cont"), None),
            P(),
            P(),
            P(),
            P(("dp", "cont"), None),
            P("dp"),
            P(("dp", "cont"), None),
        ),
        out_specs=(P(), P(), P()),
        check_vma=False,
    )
```

```python
import functools

import jax
import jax.numpy as jnp
from jax import lax
from jax.experimental import pallas as pl
from jax.experimental.pallas import tpu as pltpu
from jax.sharding import PartitionSpec as P

HQ = 64
KVH = 8
HD = 128
HPG = HQ // KVH
BLOCK = 32
STEP = 64
RANK = 16
FEATURES = 8192
GCOL = HPG * HD
LANES = HPG * STEP
HALF = LANES // 2
MASK = 16

NEG = -1e30
BETA = 0.1
ADAPTER_SCALE = 2.0
LOSS_SCALE = 1024.0
FACTOR = HD**-0.5
LOG2E = 1.4426950408889634

MESH = pl.DeviceIdType.MESH
f32 = jnp.float32
bf16 = jnp.bfloat16


def nn(a, b):
    return lax.dot_general(a, b, (((1,), (0,)), ((), ())), preferred_element_type=f32)


def nt(a, b):
    return lax.dot_general(a, b, (((1,), (1,)), ((), ())), preferred_element_type=f32)


def iota(shape, dim):
    return lax.broadcasted_iota(jnp.int32, shape, dim)


def kernel(
    dims,
    tokens_hbm, fq_hbm, sk_hbm, sv_hbm, ks_hbm, vs_hbm, dmap_hbm, up_hbm, rd_hbm,
    lens_hbm, plen_hbm, mask_hbm,
    grads, loss_out,
    tokens, fq, sk, sv, dmap, up, vshard, rd, lens, plen, mask,
    kv, shard, ubuf, dbuf, ru, rdn, zu, zd, qt, seen, picks, rvf, rvt, rvs, rvst, rvx, sbuf, mbuf, gbuf, dsib, dsum, ushare, lpair, notes, znotes,
    local_sem, gsend, grecv, fsend, frecv, usend, urecv, dsend, drecv, nsend, nrecv,
    zusend, zurecv, zdsend, zdrecv, znsend, znrecv, ausend, aurecv, adsend, adrecv,
    susend, surecv, sdsend, sdrecv, xsend, xrecv, gvsend, gvrecv, tlsend, tlrecv,
):
    n_cont, n_z = dims
    n_plane = 2 * n_cont
    n_chip = n_cont // 2
    prefix = BLOCK * n_cont
    width = FEATURES // n_plane
    dests = n_plane // KVH
    n_half = n_plane // 2
    dp = lax.axis_index("dp")
    cont = lax.axis_index("cont")
    core = lax.rem(cont, 2)
    chip = cont // 2
    zi = dp // 2
    xlo = lax.rem(dp, 2)
    place = xlo * n_chip + chip
    me = core * n_half + place

    def plane_dev(p):
        r = lax.rem(p, n_half)
        return {"dp": zi * 2 + r // n_chip, "cont": lax.rem(r, n_chip) * 2 + p // n_half}

    sibling = {"cont": chip * 2 + (1 - core)}

    def remote(src, dst, send, recv, to):
        return pltpu.make_async_remote_copy(
            src_ref=src, dst_ref=dst, send_sem=send, recv_sem=recv, device_id=to, device_id_type=MESH
        )

    def z_dev(z):
        return {"dp": z * 2 + xlo, "cont": cont}

    barrier = pltpu.get_barrier_semaphore()

    n_y = n_chip // 2
    x = 2 * lax.rem(chip, 2) + xlo
    y = chip // 2

    def hops(o):
        return min(o[0], n_y - o[0]) + min(o[1], 4 - o[1])

    plane_offsets = sorted(
        [(oy, ox) for oy in range(n_y) for ox in range(4) if (oy, ox) != (0, 0)], key=hops, reverse=True
    )
    group_offsets = [o for o in plane_offsets if o[1] % 2 == 0]
    z_offsets = sorted(range(1, n_z), key=lambda k: min(k, n_z - k), reverse=True)

    def place_at(o):
        px = lax.rem(x + o[1], 4)
        return lax.rem(px, 2) * n_chip + lax.rem(y + o[0], n_y) * 2 + px // 2

    def device_at(r):
        return plane_dev(core * n_half + r)

    def greet(to):
        pl.semaphore_signal(barrier, inc=1, device_id=to, device_id_type=MESH)

    for k in z_offsets:
        greet(z_dev(lax.rem(zi + k, n_z)))
    for o in plane_offsets:
        greet(device_at(place_at(o)))
    greet(sibling)

    loads = []
    for i, (src, dst) in enumerate(
        (
            (vs_hbm, vshard),
            (rd_hbm, rd),
            (ks_hbm, shard.at[:, HD:]),
            (dmap_hbm, dmap),
            (tokens_hbm, tokens),
            (sv_hbm, sv),
            (lens_hbm, lens),
            (plen_hbm, plen),
            (mask_hbm, mask),
            (fq_hbm, fq),
            (up_hbm, up),
            (sk_hbm, sk),
        )
    ):
        cp = pltpu.make_async_copy(src, dst, local_sem.at[i])
        cp.start()
        loads.append(cp)
    ld_vs, ld_rd, ld_ks, ld_dmap, ld_tokens, ld_sv, ld_lens, ld_plen, ld_mask, ld_fq, ld_up, ld_sk = loads

    ld_vs.wait()
    ld_rd.wait()
    rdf = rd[...].astype(f32)
    rd2 = jnp.concatenate(
        [rdf[(i // 2) * HPG : (i // 2 + 1) * HPG] for i in range(2 * KVH)], axis=0
    ).astype(bf16)
    row_g = iota((HD, HD), 0) // (2 * HPG)

    def rv_of(values):
        total = None
        for g in range(KVH):
            w = jnp.where(row_g == g, rd2, jnp.zeros_like(rd2))
            part = nt(values[:, g * HD : (g + 1) * HD], w)
            total = part if total is None else total + part
        return total

    def parts_of(x):
        high = x.astype(bf16).astype(f32)
        return jnp.where(lax.rem(iota(x.shape, 1) // HPG, 2) == 0, high, x - high).astype(bf16)

    shard[:, 0:HD] = parts_of(rv_of(vshard[...]))
    ld_ks.wait()
    kv[core, chip] = shard[...]

    pl.semaphore_wait(barrier, n_half - 1 + n_z - 1 + 1)

    part_at = (0, 2, 3, 6, 9)
    n_parts = len(part_at) - 1

    def part_cols(n):
        return pl.ds(part_at[n] * HD, (part_at[n + 1] - part_at[n]) * HD)

    def block_cols(n):
        return pl.ds(pl.multiple_of(n * HD, HD), HD)

    def issue(n):
        for o in group_offsets:
            remote(
                shard.at[:, part_cols(n)],
                kv.at[core, chip, :, part_cols(n)],
                gsend.at[n],
                grecv.at[n],
                device_at(place_at(o)),
            ).start()

    def forward_copy(n, which):
        part = kv.at[core, :, :, part_cols(n)]
        return remote(part, kv.at[which, :, :, part_cols(n)], fsend.at[n], frecv.at[n], sibling)

    def arrive(n):
        part = kv.at[core, pl.ds(0, n_chip - 1), :, part_cols(n)]
        remote(part, part, gsend.at[n], grecv.at[n], sibling).wait_recv()
        forward_copy(n, core).start()

    issue(0)
    issue(1)

    ld_dmap.wait()
    ld_tokens.wait()
    down_t = nt(dmap[...], tokens[...]).astype(bf16)
    down = down_t.astype(f32).T.astype(bf16)
    ld_lens.wait()
    len0 = lens[0, 0]
    len1 = lens[0, 1]
    lane = iota((RANK, HD), 1)
    t_of = lax.rem(lane, STEP)
    sign = jnp.where(
        lane < STEP,
        jnp.where(t_of < len0, -1.0, 0.0),
        jnp.where(t_of < len1, 1.0, 0.0),
    ).astype(f32)
    down_signed = (down_t.astype(f32) * sign).astype(bf16)

    ld_plen.wait()
    ld_mask.wait()
    limit = plen[0]
    seen[pl.ds(prefix, STEP), :] = jnp.zeros((STEP, MASK), bf16)
    for b in range(n_cont):
        block = 2 * (b % n_chip) + b // n_chip
        inside = block * BLOCK < limit
        fill = [jnp.where((mask[c, block] > 0) & inside, 0.0, NEG) for c in range(2)]
        col = iota((BLOCK, MASK), 1)
        seen[pl.ds(b * BLOCK, BLOCK), :] = jnp.where(
            col == 0, fill[0], jnp.where(col == 1, fill[1], 0.0)
        ).astype(bf16)
    causal = jnp.where(iota((STEP, HD), 0) > lax.rem(iota((STEP, HD), 1), STEP), NEG, 0.0).astype(f32)
    causal = jnp.concatenate([causal] * (HALF // HD), axis=1)

    ld_sv.wait()
    rvs[...] = rv_of(sv[...])
    step_parts = parts_of(rvs[...]).astype(f32)
    for c in range(2):
        rvst[c] = step_parts[c * STEP : (c + 1) * STEP].T.astype(bf16)
    issue(2)
    ld_fq.wait()
    ld_up.wait()
    ld_sk.wait()

    def prepare(g, carry):
        col = pl.multiple_of(g * GCOL, GCOL)
        frozen = fq[:, pl.ds(col, GCOL)].astype(f32) * (FACTOR * LOG2E)
        change = nn(down, up[:, pl.ds(col, GCOL)]) * (ADAPTER_SCALE * FACTOR * LOG2E)
        for s, q in enumerate(((frozen + change).astype(bf16), frozen.astype(bf16))):
            for c in range(2):
                rows = slice(c * STEP, (c + 1) * STEP)
                for h in range(0, HPG, 2):
                    pair = [q[rows, (h + i) * HD : (h + i + 1) * HD] for i in range(2)]
                    at = c * LANES + h * STEP
                    qt[s, g, :, at : at + HD] = jnp.concatenate(pair, axis=0).T
        return carry

    lax.fori_loop(0, KVH, prepare, 0)
    issue(3)
    for c in range(2):
        picks[c] = (iota((MASK, HALF), 0) == c).astype(f32).astype(bf16)

    units = [(c, j) for j in range(2) for c in range(2)]

    def stage_a(g, u, slot):
        c, j = units[u]
        kp = kv[:, :, :, block_cols(g + 1)].reshape(prefix, HD)
        ks = sk[pl.ds(c * STEP, STEP), block_cols(g)]
        at = c * LANES + j * HALF
        keys = jnp.concatenate([jnp.concatenate([kp, ks], axis=0), seen[...]], axis=1)
        for s in range(2):
            q = qt[s, g, :, at : at + HALF]
            scores = nn(keys, jnp.concatenate([q, picks[c]], axis=0))
            s_p = scores[0:prefix]
            s_s = scores[prefix:] + causal
            sbuf[slot, s, pl.ds(0, prefix), :] = s_p
            sbuf[slot, s, pl.ds(prefix, STEP), :] = s_s
            mbuf[slot, s] = jnp.maximum(
                jnp.max(s_p, axis=0, keepdims=True), jnp.max(s_s, axis=0, keepdims=True)
            )

    def expand(rows, g, j):
        parts = []
        for i in range(2):
            index = g * (2 * HPG) + 4 * j + 2 * i + iota(rows.shape, 1) // STEP
            parts.append(jnp.take_along_axis(rows, index, axis=1))
        return jnp.concatenate(parts, axis=1)

    def weights(slot, s):
        peak = mbuf[slot, s]
        e_p = jnp.exp2(sbuf[slot, s, pl.ds(0, prefix), :] - peak)
        e_s = jnp.exp2(sbuf[slot, s, pl.ds(prefix, STEP), :] - peak)
        return e_p, e_s

    def stage_b(g, u, slot):
        c, j = units[u]
        rv_p = rvx[j]
        rv_s = expand(rvs[pl.ds(c * STEP, STEP), :], g, j)
        e_p, e_s = weights(slot, 0)
        total = jnp.sum(e_p, axis=0, keepdims=True) + jnp.sum(e_s, axis=0, keepdims=True)
        o = jnp.sum(e_p * rv_p, axis=0, keepdims=True) + jnp.sum(e_s * rv_s, axis=0, keepdims=True)
        inverse = 1.0 / total
        o = o * inverse
        ds_p = (e_p * (rv_p - o)).astype(bf16)
        ds_s = (e_s * (rv_s - o)).astype(bf16)
        e_p, e_s = weights(slot, 1)
        own = pl.ds(pl.multiple_of(g * 16, 16), 16)
        sums = nn(jnp.concatenate([rvt[own, :], jnp.ones((16, prefix), bf16)], axis=0), e_p.astype(bf16))
        sums = sums + nn(
            jnp.concatenate([rvst[c, own, :], jnp.ones((16, STEP), bf16)], axis=0), e_s.astype(bf16)
        )
        shape = (16, HALF)
        mine = lax.rem(iota(shape, 0), HPG) == 4 * j + iota(shape, 1) // STEP
        o_ref = jnp.sum(jnp.where(mine, sums[0:16], 0.0), axis=0, keepdims=True) / sums[16:17]
        return ds_p, ds_s, inverse * FACTOR, o - o_ref

    def stage_c(g, u, kp_t, ds_p, ds_s, scale):
        c, j = units[u]
        ks_t = sk[pl.ds(c * STEP, STEP), block_cols(g)].T
        dq = ((nn(kp_t, ds_p) + nn(ks_t, ds_s)) * scale).astype(bf16)
        for i in range(2):
            h = 4 * j + 2 * i
            nat = dq[:, i * HD : (i + 1) * HD].T
            for k in range(2):
                gbuf[pl.ds(c * STEP, STEP), (h + k) * HD : (h + k + 1) * HD] = nat[
                    k * STEP : (k + 1) * STEP
                ]

    def tail(g, dd):
        col = pl.multiple_of(g * GCOL, GCOL)
        gq = gbuf[...]
        ubuf[:, pl.ds(col, GCOL)] = nn(down_signed, gq).astype(bf16)
        return dd + nt(up[:, pl.ds(col, GCOL)], gq)

    def send_up(g):
        for i in range(dests):
            p = g * dests + i
            r = lax.rem(p, n_half)

            @pl.when(r != place)
            def _(p=p, r=r):
                cols = pl.ds(pl.multiple_of(p * width, 128), width)
                to = plane_dev(core * n_half + r)
                remote(ubuf.at[:, cols], ru.at[p // n_half, place], usend.at[0], urecv.at[0], to).start()

    def group_body(g, carry, peeled=None):
        accs = list(carry[:4])
        following = jnp.minimum(g + 1, KVH - 1)
        dd = carry[4] if peeled == 0 else tail(g - 1, carry[4])
        kp_t = kv[:, :, :, block_cols(g + 1)].reshape(prefix, HD).T
        for u in range(4):
            if u == 1:
                rvx[1] = expand(rvf[...], g, 1)
            if u == 3:
                rvx[0] = expand(rvf[...], following, 0)
            if u < 3:
                stage_a(g, u + 1, (u + 1) % 2)
            else:
                if peeled is not None:
                    forward_copy(peeled + 1, 1 - core).wait_recv()
                if peeled == 0:
                    arrive(2)
                stage_a(following, 0, 0)
            ds_p, ds_s, scale, diff = stage_b(g, u, u % 2)
            accs[u] = accs[u] + diff
            stage_c(g, u, kp_t, ds_p, ds_s, scale)
        return (*accs, dd)

    def group_step(g, carry):
        @pl.when(g == 3)
        def _():
            arrive(3)

        @pl.when(g == 4)
        def _():
            forward_copy(3, 1 - core).wait_recv()

        send_up(g - 2)
        return group_body(g, carry)

    arrive(0)
    forward_copy(0, 1 - core).wait_recv()
    projected = kv[:, :, :, 0:HD].reshape(prefix, HD)
    rvt[...] = projected.T
    projected = projected.astype(f32)
    rvf[...] = projected + pltpu.roll(projected, HD - HPG, 1)
    rvx[0] = expand(rvf[...], 0, 0)

    gbuf[...] = jnp.zeros_like(gbuf)
    stage_a(0, 0, 0)
    zero_acc = jnp.zeros((1, HALF), f32)
    arrive(1)
    carry = group_body(0, (zero_acc,) * 4 + (jnp.zeros((RANK, HD), f32),), 0)
    carry = group_body(1, carry, 1)
    carry = lax.fori_loop(2, KVH, group_step, carry)
    send_up(KVH - 2)
    dd = tail(KVH - 1, carry[4])
    send_up(KVH - 1)

    tl = lax.rem(iota((1, HALF), 1), STEP)
    m0 = jnp.sum(jnp.where(tl < len0, carry[0] + carry[2], 0.0), axis=1, keepdims=True)
    m1 = jnp.sum(jnp.where(tl < len1, carry[1] + carry[3], 0.0), axis=1, keepdims=True)
    zv = BETA * (m0 - m1)
    small = jnp.exp(-jnp.abs(zv))
    loss = jnp.maximum(-zv, 0.0) + jnp.log1p(small)
    weight = (BETA * LOSS_SCALE) * jnp.where(zv >= 0.0, small, 1.0) / (1.0 + small)

    dd = (ADAPTER_SCALE * dd * sign).astype(bf16)

    def down_side(which):
        for i in range(KVH // 2):
            cols = pl.ds(pl.multiple_of(which * n_half * width + i * GCOL, 128), GCOL)
            dbuf[:, cols] = (nn(dd, tokens[:, cols]) * weight).astype(bf16)

    down_side(1 - core)

    def side(which):
        return pl.ds(pl.multiple_of(which * n_half * width, 128), n_half * width)

    def cols_of(p):
        return pl.ds(pl.multiple_of(p * width, 128), width)

    swap = remote(dbuf.at[:, side(1 - core)], dsib, xsend.at[0], xrecv.at[0], sibling)
    swap.start()

    notes[place] = jnp.where(iota((2, HD), 0) == 0, loss, weight)

    for o in plane_offsets:
        to = device_at(place_at(o))
        remote(notes.at[place], notes.at[place], nsend.at[0], nrecv.at[0], to).start()
    down_side(core)
    for h in range(2):
        ru[h, place] = ubuf[:, cols_of(h * n_half + place)]

    swap.wait_recv()
    dsum[...] = (dbuf[:, side(core)].astype(f32) + dsib[...].astype(f32)).astype(bf16)

    for o in plane_offsets:
        r = place_at(o)
        remote(dsum.at[:, cols_of(r)], rdn.at[place], dsend.at[0], drecv.at[0], device_at(r)).start()

    my_cols = pl.ds(pl.multiple_of(me * width, 128), width)

    def z_start(buf, send, recv):
        for k in z_offsets:
            remote(buf.at[zi], buf.at[zi], send, recv, z_dev(lax.rem(zi + k, n_z))).start()

    def z_end(buf, send, recv):
        others = buf.at[pl.ds(0, n_z - 1)]
        remote(others, others, send, recv, sibling).wait_recv()
        out = buf[0].astype(f32)
        for z in range(1, n_z):
            out = out + buf[z].astype(f32)
        return out

    def all_start(row, send, recv):
        part = grads.at[pl.ds(row, RANK), my_cols]

        for o in plane_offsets:
            remote(part, part, send.at[o[1] % 2], recv.at[o[1] % 2], device_at(place_at(o))).start()

    def quarter(row, which, low):
        first = pl.multiple_of((which * n_half + low * n_chip) * width, 128)
        return grads.at[pl.ds(row, RANK), pl.ds(first, n_chip * width)]

    def pieces(row, even):
        return grads.at[pl.ds(row, RANK), pl.ds(0, (n_chip - 1 if even else n_chip) * width)]

    def all_forward(row, recv, send, to_sibling):
        for way in (0, 1):
            low = lax.rem(xlo + way, 2)
            others = pieces(row, way == 0)
            remote(others, others, recv.at[way], recv.at[way], sibling).wait_recv()
            part = quarter(row, core, low)
            remote(part, part, send.at[way], to_sibling.at[way], sibling).start()

    def all_end(row, send, to_sibling):
        for way in (0, 1):
            part = quarter(row, 1 - core, lax.rem(xlo + way, 2))
            remote(part, part, send.at[way], to_sibling.at[way], sibling).wait_recv()

    others = notes.at[pl.ds(0, n_half - 1)]
    remote(others, others, nsend.at[0], nrecv.at[0], sibling).wait_recv()
    others = ru.at[:, pl.ds(0, n_half - 1)]
    remote(others, others, usend.at[0], urecv.at[0], sibling).wait_recv()

    def share(h):
        acc = jnp.zeros((RANK, width), f32)
        for r in range(n_half):
            w = jnp.concatenate([notes[r][1:2]] * (width // HD), axis=1)
            acc = acc + w * ru[h, r].astype(f32)
        return acc * ADAPTER_SCALE

    ushare[0] = share(1 - core).astype(bf16)
    loss_sum = notes[0][0:1]
    for r in range(1, n_half):
        loss_sum = loss_sum + notes[r][0:1]
    lpair[core] = loss_sum
    give = remote(ushare.at[0], ushare.at[1], gvsend.at[0], gvrecv.at[0], sibling)
    give.start()
    tell = remote(lpair.at[core], lpair.at[core], tlsend.at[0], tlrecv.at[0], sibling)
    tell.start()
    mine = share(core)

    others = rdn.at[pl.ds(0, n_half - 1)]
    remote(others, others, dsend.at[0], drecv.at[0], sibling).wait_recv()
    rdn[place] = dsum[:, cols_of(place)]
    acc = rdn[0].astype(f32)
    for r in range(1, n_half):
        acc = acc + rdn[r].astype(f32)
    zd[zi] = acc.astype(bf16)
    z_start(zd, zdsend.at[0], zdrecv.at[0])

    give.wait_recv()
    zu[zi] = (mine + ushare[1].astype(f32)).astype(bf16)
    z_start(zu, zusend.at[0], zurecv.at[0])
    tell.wait_recv()
    znotes[zi] = lpair[0] + lpair[1]
    z_start(znotes, znsend.at[0], znrecv.at[0])

    grads[pl.ds(RANK, RANK), my_cols] = z_end(zd, zdsend.at[0], zdrecv.at[0]).astype(bf16)
    all_start(RANK, adsend, adrecv)
    grads[pl.ds(0, RANK), my_cols] = z_end(zu, zusend.at[0], zurecv.at[0]).astype(bf16)
    all_start(0, ausend, aurecv)
    loss_out[...] = z_end(znotes, znsend.at[0], znrecv.at[0])

    all_forward(RANK, adrecv, sdsend, sdrecv)

    def sent(ref, sem):
        remote(ref, ref, sem, sem, sibling).wait_send()

    for n in range(n_parts):
        sent(kv.at[core, pl.ds(0, n_chip - 1), :, part_cols(n)], gsend.at[n])
        sent(kv.at[core, :, :, part_cols(n)], fsend.at[n])
    sent(ru.at[:, pl.ds(0, n_half - 1)], usend.at[0])
    sent(rdn.at[pl.ds(0, n_half - 1)], dsend.at[0])
    sent(notes.at[pl.ds(0, n_half - 1)], nsend.at[0])
    swap.wait_send()
    give.wait_send()
    tell.wait_send()
    sent(zu.at[pl.ds(0, n_z - 1)], zusend.at[0])
    sent(zd.at[pl.ds(0, n_z - 1)], zdsend.at[0])
    sent(znotes.at[pl.ds(0, n_z - 1)], znsend.at[0])

    all_forward(0, aurecv, susend, surecv)
    for row, sem in ((0, ausend), (RANK, adsend)):
        for way in (0, 1):
            sent(pieces(row, way == 0), sem.at[way])
    all_end(0, susend, surecv)
    all_end(RANK, sdsend, sdrecv)
    for row, sem in ((0, susend), (RANK, sdsend)):
        for way in (0, 1):
            sent(quarter(row, core, lax.rem(xlo + way, 2)), sem.at[way])


def local(n_cont, n_z, tokens, fq, sk, sv, kshard, vshard, dmap, up, readout, lens, plen, mask):
    n_plane = 2 * n_cont
    n_half = n_cont
    n_chip = n_cont // 2
    width = FEATURES // n_plane
    rows = tokens.shape[0]
    prefix = BLOCK * n_cont
    cols = HD + KVH * HD
    anyspec = pl.BlockSpec(memory_space=pl.ANY)
    vspec = pl.BlockSpec(memory_space=pltpu.VMEM)
    dma = pltpu.SemaphoreType.DMA
    grads, loss = pl.pallas_call(
        functools.partial(kernel, (n_cont, n_z)),
        out_shape=(
            pltpu.VMEM((2 * RANK, FEATURES), bf16),
            jax.ShapeDtypeStruct((1, 128), f32),
        ),
        in_specs=[anyspec] * 12,
        out_specs=(vspec, vspec),
        scratch_shapes=[
            pltpu.VMEM((rows, FEATURES), bf16),
            pltpu.VMEM((rows, FEATURES), bf16),
            pltpu.VMEM((rows, KVH * HD), bf16),
            pltpu.VMEM((rows, KVH * HD), bf16),
            pltpu.VMEM((RANK, FEATURES), bf16),
            pltpu.VMEM((RANK, FEATURES), bf16),
            pltpu.VMEM((BLOCK, KVH * HD), bf16),
            pltpu.VMEM((HQ, HD), bf16),
            pltpu.SMEM((1, 2), jnp.int32),
            pltpu.SMEM((1,), jnp.int32),
            pltpu.SMEM((2, n_cont), jnp.int32),
            pltpu.VMEM((2, n_chip, BLOCK, cols), bf16),
            pltpu.VMEM((BLOCK, cols), bf16),
            pltpu.VMEM((RANK, FEATURES), bf16),
            pltpu.VMEM((RANK, FEATURES), bf16),
            pltpu.VMEM((2, n_half, RANK, width), bf16),
            pltpu.VMEM((n_half, RANK, width), bf16),
            pltpu.VMEM((n_z, RANK, width), bf16),
            pltpu.VMEM((n_z, RANK, width), bf16),
            pltpu.VMEM((2, KVH, HD, 2 * LANES), bf16),
            pltpu.VMEM((prefix + STEP, MASK), bf16),
            pltpu.VMEM((2, MASK, HALF), bf16),
            pltpu.VMEM((prefix, HD), f32),
            pltpu.VMEM((HD, prefix), bf16),
            pltpu.VMEM((rows, HD), f32),
            pltpu.VMEM((2, HD, STEP), bf16),
            pltpu.VMEM((2, prefix, HALF), f32),
            pltpu.VMEM((2, 2, prefix + STEP, HALF), f32),
            pltpu.VMEM((2, 2, 1, HALF), f32),
            pltpu.VMEM((rows, GCOL), bf16),
            pltpu.VMEM((RANK, n_half * width), bf16),
            pltpu.VMEM((RANK, n_half * width), bf16),
            pltpu.VMEM((2, RANK, width), bf16),
            pltpu.VMEM((2, 1, 128), f32),
            pltpu.VMEM((n_half, 2, 128), f32),
            pltpu.VMEM((n_z, 1, 128), f32),
            dma((12,)),
            *[dma((4,))] * 4,
            *[dma((1,))] * 12,
            *[dma((2,))] * 8,
            *[dma((1,))] * 6,
        ],
        compiler_params=pltpu.CompilerParams(
            collective_id=0, has_side_effects=True, vmem_limit_bytes=60 * 1024 * 1024
        ),
    )(tokens, fq, sk, sv, kshard, vshard, dmap, up, readout.reshape(HQ, HD), lens, plen, mask)
    return loss[0, 0], grads[RANK:].astype(f32), grads[0:RANK].astype(f32)


def solution(mesh):
    return jax.shard_map(
        functools.partial(local, mesh.shape["cont"], mesh.shape["dp"] // 2),
        mesh=mesh,
        in_specs=(
            P(("dp", "cont"), None),
            P(("dp", "cont"), None),
            P(("dp", "cont"), None),
            P(("dp", "cont"), None),
            P(("dp", "cont"), None),
            P(("dp", "cont"), None),
            P(),
            P(),
            P(),
            P(("dp", "cont"), None),
            P("dp"),
            P(("dp", "cont"), None),
        ),
        out_specs=(P(), P(), P()),
        check_vma=False,
    )
```
